256 devices in a mesh: seq: 32 (over y, z_lo, core), tp: 8 (over x, z_hi).
Axes of the slice: x: 4, y: 4, z: 8 (z_hi: 2, z_lo: 4; z = z_hi * 4 + z_lo), core: 2. Of those that a mesh axis runs over, the one named last changes fastest.
Arguments:
- hidden_in: bfloat16 [16384, 4096], P(('seq', 'tp')), may hold values from -10 to 10
- norm_gain: float32 [4096], replicated, may hold values from 0.1 to 1.9
- qkv_weight: bfloat16 [4096, 3, 2048], P(None, None, 'tp'), may hold values from -1 to 1
- out_weight: bfloat16 [2048, 4096], P('tp'), may hold values from -0.125 to 0.125
- block_order: int32 [128], replicated, may hold values from 0 to 127, each once
Outputs:
- attended: bfloat16 [16384, 4096], P(('seq', 'tp'))
The draws below stay inside these ranges and needn't reach their ends.
Inputs may be any that keep to these rules, and one draw needn't show every extreme that they name: `block_order`: each sequence block appears exactly once.
All inputs are finite; a program needn't handle non-finite values.
Results may differ from the reference program's by a relative error of at most 0.019.
Values may be sent and summed in bfloat16 or wider, within the bound.
A program may use at most 128 MiB of HBM per device.

```python
import jax
import jax.numpy as jnp
from jax import lax

D = 4096
HEADS = 16
HD = 128
BLK = 128
TOK_DEV = 512
SEQ = 16384
NBLK = 128
N_TP = 8


def draw_hidden_in(key, part):
    key = jax.random.fold_in(key, 1)
    base = jnp.clip(jax.random.normal(key, (SEQ, D), jnp.float32), -6.0, 6.0)
    return base.astype(jnp.bfloat16)


def draw_qkv_weight(key, part):
    key = jax.random.fold_in(key, 2)
    base = jnp.clip(jax.random.normal(key, (D, 3, HEADS * HD), jnp.float32), -5.0, 5.0) * D ** (-0.5)
    return base.astype(jnp.bfloat16)


def block_scale(key, dims, cuts, smallest, high):
    def one(dim, shards_of):
        heights = jax.random.uniform(jax.random.fold_in(jax.random.fold_in(key, 6), dim), (shards_of,), jnp.float32, smallest / len(cuts), high / len(cuts))
        return jnp.repeat(jnp.exp(heights), dims[dim] // shards_of).reshape((-1,) + (1,) * (len(dims) - dim - 1))

    factor_of = one(*cuts[0])
    for cut in cuts[1:]:
        factor_of = factor_of * one(*cut)
    return factor_of


def normal_values(own_key, dims, width, most, split=(), kind=jnp.bfloat16):
    drawn = width * jax.random.normal(own_key, dims, jnp.float32)
    if split:
        drawn = drawn * block_scale(own_key, dims, split, -0.22, 0.18)
    return jnp.clip(drawn, -most, most).astype(kind)


def setup_inputs(seed: int = 0) -> dict:
    keys = jax.random.split(jax.random.key(seed), 6)
    hidden_in = draw_hidden_in(jax.random.fold_in(keys[5], 71), 0)
    norm_gain = jnp.clip(1.0 + 0.18 * jax.random.normal(keys[1], (D,), jnp.float32), 0.1, 1.9)
    qkv_weight = draw_qkv_weight(jax.random.fold_in(keys[5], 71), 0)
    out_weight = normal_values(keys[3], (HEADS * HD, D), (HEADS * HD) ** -0.5, 0.125, ((0, 8),))
    block_order = jax.random.permutation(keys[4], NBLK).astype(jnp.int32)
    return {"hidden_in": hidden_in, "norm_gain": norm_gain, "qkv_weight": qkv_weight, "out_weight": out_weight, "block_order": block_order}


def rotate(tensor, position):
    half = tensor.shape[-1] // 2
    inv_freq = 10000.0 ** (-(jnp.arange(half, dtype=jnp.float32) * 2.0 / tensor.shape[-1]))
    angle = position.astype(jnp.float32)[:, None] * inv_freq[None, :]
    cosine = jnp.cos(angle)[:, None, :]
    sine = jnp.sin(angle)[:, None, :]
    first = tensor[..., :half]
    second = tensor[..., half:]
    return jnp.concatenate([first * cosine - second * sine, second * cosine + first * sine], axis=-1)

def reference(hidden_in, norm_gain, qkv_weight, out_weight, block_order):
    position = (block_order[:, None] * BLK + jnp.arange(BLK, dtype=jnp.int32)[None, :]).reshape(-1)
    floats = hidden_in.astype(jnp.float32)
    scale_row = lax.rsqrt(lax.optimization_barrier(jnp.mean(floats * floats, axis=-1, keepdims=True)) + 1e-05)
    normed = (floats * scale_row * norm_gain[None, :]).astype(jnp.bfloat16)
    weight_flat = qkv_weight.reshape(D, 3 * HEADS * HD)
    projected = jnp.dot(normed, weight_flat, preferred_element_type=jnp.float32).reshape(SEQ, 3, HEADS, HD)
    rot_query = rotate(projected[:, 0], position).astype(jnp.bfloat16)
    rot_key = rotate(projected[:, 1], position).astype(jnp.bfloat16)
    value = projected[:, 2].astype(jnp.bfloat16)
    qblocks = SEQ // TOK_DEV
    factor = 1.0 / HD ** 0.5

    def head_fn(head):
        keys_h = rot_key[:, head]
        values_h = value[:, head]

        def block_fn(index):
            start = index * TOK_DEV
            queries = lax.dynamic_slice_in_dim(rot_query[:, head], start, TOK_DEV, 0)
            qpos = lax.dynamic_slice_in_dim(position, start, TOK_DEV, 0)
            score = jnp.dot(queries, keys_h.T, preferred_element_type=jnp.float32) * factor
            keep = position[None, :] <= qpos[:, None]
            top = lax.optimization_barrier(jnp.max(jnp.where(keep, score, -1e+30), axis=-1, keepdims=True))
            weight = jnp.where(keep, jnp.exp(score - top), 0.0)
            total = lax.optimization_barrier(jnp.sum(weight, axis=-1, keepdims=True))
            summed = jnp.dot(weight.astype(jnp.bfloat16), values_h, preferred_element_type=jnp.float32)
            return (summed / total).astype(jnp.bfloat16)
        return lax.map(block_fn, jnp.arange(qblocks)).reshape(SEQ, HD)
    context = lax.map(head_fn, jnp.arange(HEADS))
    context = jnp.transpose(context, (1, 0, 2)).reshape(SEQ, HEADS * HD)
    group = HEADS * HD // N_TP
    attended = jnp.zeros((SEQ, D), jnp.float32)
    for index in range(N_TP):
        term = jnp.dot(context[:, index * group:(index + 1) * group], out_weight[index * group:(index + 1) * group], preferred_element_type=jnp.float32)
        term = lax.optimization_barrier(term.astype(jnp.bfloat16))
        attended = attended + term.astype(jnp.float32)
    return attended.astype(jnp.bfloat16)
```

```python
import functools
import math

import jax
import jax.numpy as jnp
from jax import lax
from jax.experimental import pallas as pl
from jax.experimental.pallas import tpu as pltpu
from jax.sharding import PartitionSpec as P

HD = 128
BLK = 128
D = 4096
HB = 64
SLOTS = 8
ROWS = HB * SLOTS
SRC = 8
ALL = SRC * ROWS
HALF = HB // 2
TQ = 256
TK = 512
MESH = pl.DeviceIdType.MESH
F32 = jnp.float32
BF16 = jnp.bfloat16

OWN, L0, R0, MIR, O0, L1, R1, O1 = range(8)
CHUNKS = ((0, 0), (0, -1), (0, 1), (1, 0), (0, 2), (1, -1), (1, 1), (1, 2))
OTHERS = [(d, e) for d in range(4) for e in range(2)][1:]


def place():
    s = lax.axis_index("seq")
    t = lax.axis_index("tp")
    return s // 8, (s // 2) % 4, s % 2, t // 2, t % 2


def device(y, zl, c, x, zh):
    return ((y * 4 + zl) * 2 + c, x * 2 + zh)


def other_core(c, e):
    return 1 - c if e else c


def starts_of(block_order, y, zl, c, x, zh):
    out = []
    for mirrored, dx in CHUNKS:
        z = 3 - zl if mirrored else zl
        half = 1 - zh if mirrored else zh
        s = (y * 4 + z) * 2 + c
        row = s * ROWS + (((x + dx) % 4) * 2 + half) * HB
        out.append(row)
    rows = jnp.stack(out, axis=-1).reshape(-1)
    hit = (rows // BLK)[:, None] == jnp.arange(block_order.shape[0], dtype=jnp.int32)[None, :]
    block = jnp.sum(jnp.where(hit, block_order[None, :], 0), axis=1)
    return block * BLK + rows % BLK


def sort_chunks(starts):
    count = starts.shape[-1]
    rank = jnp.sum((starts[:, None] < starts[None, :]).astype(jnp.int32), axis=0)
    hit = rank[None, :] == jnp.arange(count, dtype=jnp.int32)[:, None]
    order = jnp.sum(jnp.where(hit, jnp.arange(count, dtype=jnp.int32)[None, :], 0), axis=1)
    first = jnp.sum(jnp.where(hit, starts[None, :], 0), axis=1)
    return order, first


def greet(peers):
    barrier = pltpu.get_barrier_semaphore()
    for peer in peers:
        pl.semaphore_signal(barrier, inc=1, device_id=peer, device_id_type=MESH)
    return barrier


def remote(src, dst, send, recv, peer):
    return pltpu.make_async_remote_copy(
        src_ref=src, dst_ref=dst, send_sem=send, recv_sem=recv, device_id=peer, device_id_type=MESH
    )


def project_kernel(
    hid, gain, w_hbm, cos, sin, q_out, kv_out,
    rows, wv, qs, kvs, w_sem, x_send, x_recv, z_send, z_recv,
    kv_send, kv_recv, q_send, q_recv, own_sem,
):
    y, zl, c, x, zh = place()
    right = device(y, zl, c, (x + 1) % 4, zh)
    left = device(y, zl, c, (x + 3) % 4, zh)
    mirror = device(y, 3 - zl, c, x, 1 - zh)
    kv_peers = [((y + d) % 4, other_core(c, e)) for d, e in OTHERS]
    q_peers = [((zl + d) % 4, other_core(c, e)) for d, e in OTHERS]
    kv_ids = [device(py, zl, pc, x, zh) for py, pc in kv_peers]
    q_ids = [device(y, pz, pc, x, zh) for pz, pc in q_peers]
    peers = [right, left, mirror] + kv_ids + q_ids[1:]
    barrier = greet(peers)
    w_copy = pltpu.make_async_copy(w_hbm, wv, w_sem)
    w_copy.start()

    floats = hid[...].astype(F32)
    scale = lax.rsqrt(jnp.mean(floats * floats, axis=-1, keepdims=True) + 1e-05)
    rows[0:HB, :] = (floats * scale * gain[...]).astype(BF16)
    pl.semaphore_wait(barrier, len(peers))

    def at(slot, lo=0, hi=HB):
        return rows.at[pl.ds(slot * HB + lo, hi - lo), :]

    def to_right(p, own, slot):
        return remote(at(own), at(slot), x_send.at[p, 0], x_recv.at[p, 0], right)

    def to_left(p, own, slot):
        return remote(at(own), at(slot), x_send.at[p, 1], x_recv.at[p, 1], left)

    def pass_right(p, src, dst):
        return remote(at(src, 0, HALF), at(dst, 0, HALF), x_send.at[p, 2], x_recv.at[p, 2], right)

    def pass_left(p, src, dst):
        return remote(at(src, HALF, HB), at(dst, HALF, HB), x_send.at[p, 3], x_recv.at[p, 3], left)

    to_mirror = remote(at(OWN), at(MIR), z_send, z_recv, mirror)
    r0, l0 = to_right(0, OWN, L0), to_left(0, OWN, R0)
    pr0, pl0 = pass_right(0, L0, O0), pass_left(0, R0, O0)
    r1, l1 = to_right(1, MIR, L1), to_left(1, MIR, R1)
    pr1, pl1 = pass_right(1, L1, O1), pass_left(1, R1, O1)

    to_mirror.start()
    r0.start()
    l0.start()
    mine = y * 2 + c
    mine_q = zl * 2 + c

    def part(ref, lo, hi, *index):
        return ref.at[(*index, pl.ds(lo, hi - lo), slice(None))]

    def work(first, last):
        lo, hi = first * HB, last * HB
        chunk = rows[lo:hi, :]
        cs, sn = cos[lo:hi, :], sin[lo:hi, :]
        q = jnp.dot(chunk, wv[0], preferred_element_type=F32)
        k = jnp.dot(chunk, wv[1], preferred_element_type=F32)
        v = jnp.dot(chunk, wv[2], preferred_element_type=F32)
        for h in range(2):
            lane = slice(h * HD, (h + 1) * HD)
            for out, cols, t in ((qs, slice(0, HD), q[:, lane]), (kvs, slice(0, HD), k[:, lane])):
                turned = t * cs + pltpu.roll(t, HD // 2, 1) * sn
                out[h, lo:hi, cols] = turned.astype(BF16)
            kvs[h, lo:hi, HD : 2 * HD] = v[:, lane].astype(BF16)
        for i, (py, pc) in enumerate(kv_peers):
            remote(
                part(kvs, lo, hi, pc), part(kv_out, lo, hi, mine),
                kv_send.at[i], kv_recv.at[mine], kv_ids[i],
            ).start()
        for i, (pz, pc) in enumerate(q_peers):
            remote(
                part(qs, lo, hi, pc), part(q_out, lo, hi, mine_q),
                q_send.at[i], q_recv.at[mine_q], q_ids[i],
            ).start()

    w_copy.wait()
    work(OWN, OWN + 1)
    r0.wait_recv()
    pr0.start()
    l0.wait_recv()
    pl0.start()
    work(L0, R0 + 1)
    to_mirror.wait_recv()
    r1.start()
    l1.start()
    pr0.wait_recv()
    pl0.wait_recv()
    work(MIR, O0 + 1)
    r1.wait_recv()
    pr1.start()
    l1.wait_recv()
    pl1.start()
    work(L1, R1 + 1)
    pr1.wait_recv()
    pl1.wait_recv()
    work(O1, O1 + 1)
    own_kv = pltpu.make_async_copy(kvs.at[c], kv_out.at[mine], own_sem.at[0])
    own_q = pltpu.make_async_copy(qs.at[c], q_out.at[mine_q], own_sem.at[1])
    own_kv.start()
    own_q.start()
    for copy in (to_mirror, r0, l0, pr0, pl0, r1, l1, pr1, pl1):
        copy.wait_send()
    for i, (py, pc) in enumerate(kv_peers):
        src = py * 2 + pc
        done = remote(kvs.at[pc], kv_out.at[src], kv_send.at[i], kv_recv.at[src], kv_ids[i])
        done.wait_send()
        done.wait_recv()
    for i, (pz, pc) in enumerate(q_peers):
        src = pz * 2 + pc
        done = remote(qs.at[pc], q_out.at[src], q_send.at[i], q_recv.at[src], q_ids[i])
        done.wait_send()
        done.wait_recv()
    own_kv.wait()
    own_q.wait()


def project(hidden_in, norm_gain, weight, cos, sin):
    vmem = pl.BlockSpec(memory_space=pltpu.VMEM)
    hbm = pl.BlockSpec(memory_space=pl.ANY)
    dma = pltpu.SemaphoreType.DMA
    return pl.pallas_call(
        project_kernel,
        out_shape=(
            jax.ShapeDtypeStruct((SRC, ROWS, HD), BF16),
            jax.ShapeDtypeStruct((SRC, ROWS, 2 * HD), BF16),
        ),
        in_specs=[vmem, vmem, hbm, vmem, vmem],
        out_specs=(hbm, hbm),
        scratch_shapes=[
            pltpu.VMEM((ROWS, D), BF16),
            pltpu.VMEM((3, D, 2 * HD), BF16),
            pltpu.VMEM((2, ROWS, HD), BF16),
            pltpu.VMEM((2, ROWS, 2 * HD), BF16),
            dma, dma((2, 4)), dma((2, 4)), dma, dma,
            dma((SRC,)), dma((SRC,)), dma((SRC,)), dma((SRC,)), dma((2,)),
        ],
        compiler_params=pltpu.CompilerParams(
            collective_id=0, has_side_effects=True, vmem_limit_bytes=40 << 20
        ),
        name="project",
    )(hidden_in, norm_gain, weight, cos, sin)


def attend_kernel(meta, q_hbm, kv_hbm, o_out, lse_out, qs, ks, va, scores, top, sems):
    chunks = ALL // HB

    @pl.loop(0, chunks)
    def _(r):
        rows = pl.ds(pl.multiple_of(r * HB, HB), HB)
        oq, ok = meta[0, r], meta[1, r]
        pltpu.make_async_copy(q_hbm.at[oq], qs.at[rows, :], sems.at[0]).start()
        pltpu.make_async_copy(kv_hbm.at[ok, :, 0:HD], ks.at[rows, :], sems.at[1]).start()
        pltpu.make_async_copy(
            kv_hbm.at[ok, :, HD : 2 * HD], va.at[rows, 0:HD], sems.at[2]
        ).start()

    va[:, HD : 2 * HD] = jnp.ones((ALL, HD), BF16)
    pltpu.make_async_copy(qs, qs, sems.at[0]).wait()
    pltpu.make_async_copy(ks, ks, sems.at[1]).wait()
    pltpu.make_async_copy(ks, va.at[:, 0:HD], sems.at[2]).wait()
    scale = math.log2(math.e) / HD**0.5
    per_q, per_k = TQ // HB, TK // HB

    @pl.loop(0, ALL // TQ)
    def _(i):
        q = qs[pl.ds(pl.multiple_of(i * TQ, TQ), TQ), :]
        qmin = meta[2, i * per_q]
        qmax = meta[2, i * per_q + per_q - 1] + HB - 1
        n_all = jnp.int32(0)
        n_full = jnp.int32(0)
        for j in range(ALL // TK):
            n_all += (meta[3, j * per_k] <= qmax).astype(jnp.int32)
            n_full += (meta[3, j * per_k + per_k - 1] + HB - 1 <= qmin).astype(jnp.int32)
        top[...] = jnp.full((TQ, HD), -1e29, F32)

        def score(j, masked):
            at = pl.ds(pl.multiple_of(j * TK, TK), TK)
            s = lax.dot_general(
                q, ks[at, :], (((1,), (1,)), ((), ())), preferred_element_type=F32
            )
            if masked:
                row = lax.broadcasted_iota(jnp.int32, (TQ, 1), 0)
                col = lax.broadcasted_iota(jnp.int32, (1, TK), 1)
                qpos, kpos = row, col
                for u in range(per_q):
                    qpos = jnp.where(row // HB == u, meta[2, i * per_q + u] + row % HB, qpos)
                for u in range(per_k):
                    kpos = jnp.where(col // HB == u, meta[3, j * per_k + u] + col % HB, kpos)
                s = jnp.where(kpos <= qpos, s, -1e30)
            scores[:, at] = s
            best = top[...]
            for u in range(TK // HD):
                best = jnp.maximum(best, s[:, u * HD : (u + 1) * HD])
            top[...] = best

        pl.loop(0, n_full)(lambda j: score(j, False))
        pl.loop(n_full, n_all)(lambda j: score(j, True))
        best = jnp.max(top[...], axis=1, keepdims=True)

        def step(j, acc):
            at = pl.ds(pl.multiple_of(j * TK, TK), TK)
            weight = jnp.exp2((scores[:, at] - best) * scale).astype(BF16)
            return acc + jnp.dot(weight, va[at, :], preferred_element_type=F32)

        acc = lax.fori_loop(0, n_all, step, jnp.zeros((TQ, 2 * HD), F32))
        total = acc[:, HD:]
        some = total > 0
        out = jnp.where(some, acc[:, :HD] / jnp.where(some, total, 1.0), 0.0).astype(BF16)
        lse = jnp.where(some, best * scale + jnp.log2(jnp.where(some, total, 1.0)), -1e30)
        lanes = lse.T
        for u in range(per_q):
            oq = meta[0, i * per_q + u]
            o_out[oq] = out[u * HB : (u + 1) * HB, :]
            lse_out[oq // SLOTS, pl.ds(oq % SLOTS, 1), 0:HB] = lanes[0:1, u * HB : (u + 1) * HB]


def attend(meta, q, kv):
    vmem = pl.BlockSpec(memory_space=pltpu.VMEM)
    hbm = pl.BlockSpec(memory_space=pl.ANY)
    chunks = ALL // HB
    return pl.pallas_call(
        attend_kernel,
        out_shape=(
            jax.ShapeDtypeStruct((chunks, HB, HD), BF16),
            jax.ShapeDtypeStruct((SRC, SLOTS, HD), F32),
        ),
        in_specs=[pl.BlockSpec(memory_space=pltpu.SMEM), hbm, hbm],
        out_specs=(vmem, vmem),
        scratch_shapes=[
            pltpu.VMEM((ALL, HD), BF16),
            pltpu.VMEM((ALL, HD), BF16),
            pltpu.VMEM((ALL, 2 * HD), BF16),
            pltpu.VMEM((TQ, ALL), F32),
            pltpu.VMEM((TQ, HD), F32),
            pltpu.SemaphoreType.DMA((3,)),
        ],
        compiler_params=pltpu.CompilerParams(vmem_limit_bytes=40 << 20),
        name="attend",
    )(meta, q.reshape(chunks, HB, HD), kv.reshape(chunks, HB, 2 * HD))


def combine_kernel(
    o_hbm, lse_in, w_ref, out_ref,
    parts, lses, ctx, terms, halves, fulls, mirrored,
    o_send, o_recv, l_send, l_recv, own_sem, h_send, h_recv, f_send, f_recv, z_send, z_recv,
):
    y, zl, c, x, zh = place()
    right = device(y, zl, c, (x + 1) % 4, zh)
    left = device(y, zl, c, (x + 3) % 4, zh)
    mirror = device(y, 3 - zl, c, x, 1 - zh)
    peers = [((zl + d) % 4, other_core(c, e)) for d, e in OTHERS]
    ids = [device(y, pz, pc, x, zh) for pz, pc in peers]
    mine = zl * 2 + c
    barrier = greet([right, left, mirror] + ids)
    own_o = pltpu.make_async_copy(o_hbm.at[mine], parts.at[mine], own_sem.at[0])
    own_l = pltpu.make_async_copy(lse_in.at[mine], lses.at[mine], own_sem.at[1])
    own_o.start()
    own_l.start()
    pl.semaphore_wait(barrier, len(ids) + 3)
    for i, (pz, pc) in enumerate(peers):
        to = pz * 2 + pc
        remote(lse_in.at[to], lses.at[mine], l_send.at[i], l_recv.at[mine], ids[i]).start()
        remote(o_hbm.at[to], parts.at[mine], o_send.at[i], o_recv.at[mine], ids[i]).start()
    own_o.wait()
    own_l.wait()
    for i, (pz, pc) in enumerate(peers):
        src = pz * 2 + pc
        for done in (
            remote(lse_in.at[src], lses.at[src], l_send.at[i], l_recv.at[src], ids[i]),
            remote(o_hbm.at[src], parts.at[src], o_send.at[i], o_recv.at[src], ids[i]),
        ):
            done.wait_send()
            done.wait_recv()

    stats = lses[...].reshape(SRC * SLOTS, HD)
    stats = jnp.concatenate([stats, stats], axis=0).T
    for slot in range(SLOTS):
        lo, hi = slot * HB, (slot + 1) * HB
        for h in range(2):
            cols = [stats[0:HB, (z * 2 + h) * SLOTS + slot : (z * 2 + h) * SLOTS + slot + 1] for z in range(4)]
            best = jnp.maximum(jnp.maximum(cols[0], cols[1]), jnp.maximum(cols[2], cols[3]))
            shares = [jnp.exp2(col - best) for col in cols]
            total = shares[0] + shares[1] + shares[2] + shares[3]
            mixed = jnp.zeros((HB, HD), F32)
            for z in range(4):
                mixed += (shares[z] / total) * parts[z * 2 + h, lo:hi, :].astype(F32)
            ctx[lo:hi, h * HD : (h + 1) * HD] = mixed.astype(BF16)

    def term(slot):
        lo, hi = slot * HB, (slot + 1) * HB
        terms[lo:hi, :] = jnp.dot(ctx[lo:hi, :], w_ref[...], preferred_element_type=F32).astype(BF16)

    def at(slot, lo=0, hi=HB):
        return terms.at[pl.ds(slot * HB + lo, hi - lo), :]

    def half_right(p, slot):
        return remote(at(slot, 0, HALF), halves.at[p, 0], h_send.at[p, 0], h_recv.at[p, 0], right)

    def half_left(p, slot):
        return remote(at(slot, HALF, HB), halves.at[p, 1], h_send.at[p, 1], h_recv.at[p, 1], left)

    def full_right(p, slot):
        return remote(at(slot), fulls.at[p, 0], f_send.at[p, 0], f_recv.at[p, 0], right)

    def full_left(p, slot):
        return remote(at(slot), fulls.at[p, 1], f_send.at[p, 1], f_recv.at[p, 1], left)

    def add(lo, hi, more):
        terms[lo:hi, :] = (terms[lo:hi, :].astype(F32) + more.astype(F32)).astype(BF16)

    slots = ((L0, R0, O0), (L1, R1, O1))
    started = []
    chains = {}
    for p in (1, 0):
        left_slot, right_slot, far = slots[p]
        term(far)
        hr, hl = half_right(p, far), half_left(p, far)
        hr.start()
        hl.start()
        chains[p] = (hr, hl)
        started += [hr, hl]
    for p in (1, 0):
        left_slot, right_slot, far = slots[p]
        hr, hl = chains[p]
        term(left_slot)
        term(right_slot)
        hr.wait_recv()
        add(right_slot * HB, right_slot * HB + HALF, halves[p, 0])
        fr = full_right(p, right_slot)
        fr.start()
        hl.wait_recv()
        add(left_slot * HB + HALF, left_slot * HB + HB, halves[p, 1])
        fl = full_left(p, left_slot)
        fl.start()
        chains[p] = (fr, fl)
        started += [fr, fl]
    term(MIR)
    term(OWN)
    for copy in chains[1]:
        copy.wait_recv()
    add(MIR * HB, MIR * HB + HB, fulls[1, 0].astype(F32) + fulls[1, 1].astype(F32))
    to_mirror = remote(at(MIR), mirrored, z_send, z_recv, mirror)
    to_mirror.start()
    for copy in chains[0]:
        copy.wait_recv()
    to_mirror.wait_recv()
    total = terms[0:HB, :].astype(F32) + fulls[0, 0].astype(F32)
    total = total + fulls[0, 1].astype(F32) + mirrored[...].astype(F32)
    out_ref[...] = total.astype(BF16)
    for copy in started:
        copy.wait_send()
    to_mirror.wait_send()


def combine(o, lse, out_weight):
    vmem = pl.BlockSpec(memory_space=pltpu.VMEM)
    hbm = pl.BlockSpec(memory_space=pl.ANY)
    dma = pltpu.SemaphoreType.DMA
    return pl.pallas_call(
        combine_kernel,
        out_shape=jax.ShapeDtypeStruct((HB, D), BF16),
        in_specs=[hbm, hbm, vmem],
        out_specs=vmem,
        scratch_shapes=[
            pltpu.VMEM((SRC, ROWS, HD), BF16),
            pltpu.VMEM((SRC, SLOTS, HD), F32),
            pltpu.VMEM((ROWS, 2 * HD), BF16),
            pltpu.VMEM((ROWS, D), BF16),
            pltpu.VMEM((2, 2, HALF, D), BF16),
            pltpu.VMEM((2, 2, HB, D), BF16),
            pltpu.VMEM((HB, D), BF16),
            dma((SRC,)), dma((SRC,)), dma((SRC,)), dma((SRC,)), dma((2,)),
            dma((2, 2)), dma((2, 2)), dma((2, 2)), dma((2, 2)), dma, dma,
        ],
        compiler_params=pltpu.CompilerParams(
            collective_id=1, has_side_effects=True, vmem_limit_bytes=40 << 20
        ),
        name="combine",
    )(o.reshape(SRC, ROWS, HD), lse, out_weight)


def local(hidden_in, norm_gain, qkv_weight, out_weight, block_order):
    y, zl, c, x, zh = place()
    zero = jnp.zeros((4, 2), jnp.int32)
    lane = jnp.arange(4, dtype=jnp.int32)[:, None] + zero
    core = jnp.arange(2, dtype=jnp.int32)[None, :] + zero
    q_starts = starts_of(block_order, zero + y, lane, core, x, zh)
    k_starts = starts_of(block_order, lane, zero + zl, core, x, zh)
    q_order, q_first = sort_chunks(q_starts)
    k_order, k_first = sort_chunks(k_starts)
    meta = jnp.stack([q_order, k_order, q_first, k_first])

    mine = starts_of(block_order, y, zl, c, x, zh)
    position = (mine[:, None] + jnp.arange(HB, dtype=jnp.int32)[None, :]).reshape(-1)
    inv_freq = 10000.0 ** (-(jnp.arange(HD // 2, dtype=F32) * 2.0 / HD))
    angle = position.astype(F32)[:, None] * inv_freq[None, :]
    cosine, sine = jnp.cos(angle), jnp.sin(angle)
    cos = jnp.concatenate([cosine, cosine], axis=1)
    sin = jnp.concatenate([-sine, sine], axis=1)

    weight = jnp.transpose(qkv_weight, (1, 0, 2))
    q, kv = project(hidden_in, norm_gain[None, :], weight, cos, sin)
    o, lse = attend(meta, q, kv)
    return combine(o, lse, out_weight)


def solution(mesh):
    in_specs = (P(("seq", "tp"), None), P(), P(None, None, "tp"), P("tp", None), P())
    out_specs = P(("seq", "tp"), None)
    return jax.shard_map(local, mesh=mesh, in_specs=in_specs, out_specs=out_specs, check_vma=False)
```

```python
import math

import jax
import jax.numpy as jnp
import numpy as np
from jax import lax
from jax.experimental import pallas as pl
from jax.experimental.pallas import tpu as pltpu
from jax.sharding import PartitionSpec as P

HD = 128
BLK = 128
D = 4096
HB = 64
SLOTS = 8
ROWS = HB * SLOTS
SRC = 8
ALL = SRC * ROWS
HALF = HB // 2
TQ = 512
TK = 1024
MESH = pl.DeviceIdType.MESH
F32 = jnp.float32
BF16 = jnp.bfloat16

OWN, L0, R0, MIR, O0, L1, R1, O1 = range(8)
CHUNKS = ((0, 0), (0, -1), (0, 1), (1, 0), (0, 2), (1, -1), (1, 1), (1, 2))
SCALE = math.log2(math.e) / HD**0.5
GROUPS = ((O1, O1 + 1), (L1, R1 + 1), (MIR, MIR + 1), (O0, O0 + 1), (L0, R0 + 1), (OWN, OWN + 1))
OTHERS = [(d, e) for d in range(4) for e in range(2)][1:]


def place():
    s = lax.axis_index("seq")
    t = lax.axis_index("tp")
    return s // 8, (s // 2) % 4, s % 2, t // 2, t % 2


def device(y, zl, c, x, zh):
    return ((y * 4 + zl) * 2 + c, x * 2 + zh)


def other_core(c, e):
    return 1 - c if e else c


def starts_of(block_order, y, zl, c, x, zh):
    index = np.arange(2 * SRC * SLOTS + SLOTS)
    of_q, of_k = index < SRC * SLOTS, (index >= SRC * SLOTS) & (index < 2 * SRC * SLOTS)
    lane, core, slot = index // (2 * SLOTS) % 4, index // SLOTS % 2, index % SLOTS
    mirrored = np.array([m for m, _ in CHUNKS])[slot]
    shift = np.array([dx for _, dx in CHUNKS])[slot] % 4
    py = jnp.where(of_k, lane, y)
    pz = jnp.where(of_q, lane, zl)
    pc = jnp.where(of_q | of_k, core, c)
    pz = jnp.where(mirrored == 1, 3 - pz, pz)
    half = jnp.where(mirrored == 1, 1 - zh, zh)
    block = ((py * 4 + pz) * 2 + pc) * (ROWS // BLK) + ((x + shift) & 3)
    hit = block[:, None] == jnp.arange(block_order.shape[0], dtype=jnp.int32)[None, :]
    return jnp.sum(jnp.where(hit, block_order[None, :], 0), axis=1) * BLK + half * HB


def sort_chunks(starts):
    count = starts.shape[-1]
    index = jnp.arange(count, dtype=jnp.int32)
    rank = jnp.sum((starts[:, :, None] < starts[:, None, :]).astype(jnp.int32), axis=1)
    hit = rank[:, None, :] == index[None, :, None]
    order = jnp.sum(jnp.where(hit, index[None, None, :], 0), axis=2)
    first = jnp.sum(jnp.where(hit, starts[:, None, :], 0), axis=2)
    return order, first


def greet(peers):
    barrier = pltpu.get_barrier_semaphore()
    for peer in peers:
        pl.semaphore_signal(barrier, inc=1, device_id=peer, device_id_type=MESH)
    return barrier


def remote(src, dst, send, recv, peer):
    return pltpu.make_async_remote_copy(
        src_ref=src, dst_ref=dst, send_sem=send, recv_sem=recv, device_id=peer, device_id_type=MESH
    )


def project_kernel(
    hid, gain, w_hbm, cos, sin, q_out, kv_out,
    rows, wv, qs, kvs, w_sem, x_send, x_recv, z_send, z_recv,
    kv_send, kv_recv, q_send, q_recv, own_sem,
):
    y, zl, c, x, zh = place()
    right = device(y, zl, c, (x + 1) % 4, zh)
    left = device(y, zl, c, (x + 3) % 4, zh)
    mirror = device(y, 3 - zl, c, x, 1 - zh)
    kv_peers = [((y + d) % 4, other_core(c, e)) for d, e in OTHERS]
    q_peers = [((zl + d) % 4, other_core(c, e)) for d, e in OTHERS]
    kv_ids = [device(py, zl, pc, x, zh) for py, pc in kv_peers]
    q_ids = [device(y, pz, pc, x, zh) for pz, pc in q_peers]
    peers = [right, left, mirror] + kv_ids + q_ids[1:]
    barrier = greet(peers)
    w_copy = pltpu.make_async_copy(w_hbm, wv, w_sem)
    w_copy.start()

    floats = hid[...].astype(F32)
    scale = lax.rsqrt(jnp.mean(floats * floats, axis=-1, keepdims=True) + 1e-05)
    rows[0:HB, :] = (floats * scale * gain[...]).astype(BF16)
    pl.semaphore_wait(barrier, len(peers))

    def at(slot, lo=0, hi=HB):
        return rows.at[pl.ds(slot * HB + lo, hi - lo), :]

    def step(p, kind, src, dst, lo, hi, peer):
        return remote(at(src, lo, hi), at(dst, lo, hi), x_send.at[p, kind], x_recv.at[p, kind], peer)

    def ring(p, src, from_left, from_right, far):
        return (
            step(p, 0, src, from_left, 0, HALF, right),
            step(p, 1, src, from_right, HALF, HB, left),
            step(p, 2, src, from_left, HALF, HB, right),
            step(p, 3, src, from_right, 0, HALF, left),
            step(p, 4, from_left, far, 0, HALF, right),
            step(p, 5, from_right, far, HALF, HB, left),
        )

    mirror_lo = remote(at(OWN, 0, HALF), at(MIR, 0, HALF), z_send.at[0], z_recv.at[0], mirror)
    mirror_hi = remote(at(OWN, HALF, HB), at(MIR, HALF, HB), z_send.at[1], z_recv.at[1], mirror)
    near = ring(0, OWN, L0, R0, O0)
    far = ring(1, MIR, L1, R1, O1)

    mirror_lo.start()
    mirror_hi.start()
    for copy in near[:4]:
        copy.start()
    mine = y * 2 + c
    mine_q = zl * 2 + c

    def part(ref, lo, hi, *index):
        return ref.at[(*index, pl.ds(lo, hi - lo), slice(None))]

    def work(first, last):
        lo, hi = first * HB, last * HB
        chunk = rows[lo:hi, :]
        cs, sn = cos[lo:hi, :], sin[lo:hi, :]
        q = jnp.dot(chunk, wv[0], preferred_element_type=F32)
        k = jnp.dot(chunk, wv[1], preferred_element_type=F32)
        v = jnp.dot(chunk, wv[2], preferred_element_type=F32)
        for h in range(2):
            lane = slice(h * HD, (h + 1) * HD)
            for out, by, t in ((qs, SCALE, q[:, lane]), (kvs, 1.0, k[:, lane])):
                turned = t * cs + pltpu.roll(t, HD // 2, 1) * sn
                out[h, lo:hi, 0:HD] = (turned * by).astype(BF16)
            kvs[h, lo:hi, HD : 2 * HD] = v[:, lane].astype(BF16)
        for i, (py, pc) in enumerate(kv_peers):
            remote(
                part(kvs, lo, hi, pc), part(kv_out, lo, hi, mine),
                kv_send.at[i], kv_recv.at[mine], kv_ids[i],
            ).start()
        for i, (pz, pc) in enumerate(q_peers):
            remote(
                part(qs, lo, hi, pc), part(q_out, lo, hi, mine_q),
                q_send.at[i], q_recv.at[mine_q], q_ids[i],
            ).start()

    w_copy.wait()
    work(OWN, OWN + 1)
    near[0].wait_recv()
    near[4].start()
    near[1].wait_recv()
    near[5].start()
    near[2].wait_recv()
    near[3].wait_recv()
    work(L0, R0 + 1)
    mirror_lo.wait_recv()
    far[0].start()
    far[3].start()
    near[4].wait_recv()
    near[5].wait_recv()
    work(O0, O0 + 1)
    mirror_hi.wait_recv()
    far[1].start()
    far[2].start()
    work(MIR, MIR + 1)
    far[0].wait_recv()
    far[4].start()
    far[1].wait_recv()
    far[5].start()
    far[2].wait_recv()
    far[3].wait_recv()
    work(L1, R1 + 1)
    far[4].wait_recv()
    far[5].wait_recv()
    work(O1, O1 + 1)
    own_kv = pltpu.make_async_copy(kvs.at[c], kv_out.at[mine], own_sem.at[0])
    own_q = pltpu.make_async_copy(qs.at[c], q_out.at[mine_q], own_sem.at[1])
    own_kv.start()
    own_q.start()
    for copy in (mirror_lo, mirror_hi, *near, *far):
        copy.wait_send()
    for i, (py, pc) in enumerate(kv_peers):
        src = py * 2 + pc
        done = remote(kvs.at[pc], kv_out.at[src], kv_send.at[i], kv_recv.at[src], kv_ids[i])
        done.wait_send()
        done.wait_recv()
    for i, (pz, pc) in enumerate(q_peers):
        src = pz * 2 + pc
        done = remote(qs.at[pc], q_out.at[src], q_send.at[i], q_recv.at[src], q_ids[i])
        done.wait_send()
        done.wait_recv()
    own_kv.wait()
    own_q.wait()


def project(hidden_in, norm_gain, weight, cos, sin):
    vmem = pl.BlockSpec(memory_space=pltpu.VMEM)
    hbm = pl.BlockSpec(memory_space=pl.ANY)
    dma = pltpu.SemaphoreType.DMA
    return pl.pallas_call(
        project_kernel,
        out_shape=(
            jax.ShapeDtypeStruct((SRC, ROWS, HD), BF16),
            jax.ShapeDtypeStruct((SRC, ROWS, 2 * HD), BF16),
        ),
        in_specs=[vmem, vmem, hbm, vmem, vmem],
        out_specs=(hbm, hbm),
        scratch_shapes=[
            pltpu.VMEM((ROWS, D), BF16),
            pltpu.VMEM((3, D, 2 * HD), BF16),
            pltpu.VMEM((2, ROWS, HD), BF16),
            pltpu.VMEM((2, ROWS, 2 * HD), BF16),
            dma, dma((2, 6)), dma((2, 6)), dma((2,)), dma((2,)),
            dma((SRC,)), dma((SRC,)), dma((SRC,)), dma((SRC,)), dma((2,)),
        ],
        compiler_params=pltpu.CompilerParams(
            collective_id=0, has_side_effects=True, vmem_limit_bytes=60 << 20
        ),
        name="project",
    )(hidden_in, norm_gain, weight, cos, sin)


def attend_kernel(meta, q_hbm, kv_hbm, o_out, lse_out, qs, ks, va, scores, top, sems):
    chunks = ALL // HB

    @pl.loop(0, chunks)
    def _(r):
        rows = pl.ds(pl.multiple_of(r * HB, HB), HB)
        oq, ok = meta[0, r], meta[1, r]
        pltpu.make_async_copy(q_hbm.at[oq], qs.at[rows, :], sems.at[0]).start()
        pltpu.make_async_copy(kv_hbm.at[ok, :, 0:HD], ks.at[rows, :], sems.at[1]).start()
        pltpu.make_async_copy(
            kv_hbm.at[ok, :, HD : 2 * HD], va.at[rows, 0:HD], sems.at[2]
        ).start()

    va[:, HD : 2 * HD] = jnp.ones((ALL, HD), BF16)
    pltpu.make_async_copy(qs, qs, sems.at[0]).wait()
    pltpu.make_async_copy(ks, ks, sems.at[1]).wait()
    pltpu.make_async_copy(ks, va.at[:, 0:HD], sems.at[2]).wait()
    per_q, per_k = TQ // HB, TK // HB

    @pl.loop(0, ALL // TQ)
    def _(i):
        q = qs[pl.ds(pl.multiple_of(i * TQ, TQ), TQ), :]
        qmin = meta[2, i * per_q]
        qmax = meta[2, i * per_q + per_q - 1] + HB - 1
        n_all = jnp.int32(0)
        n_full = jnp.int32(0)
        for j in range(ALL // TK):
            n_all += (meta[3, j * per_k] <= qmax).astype(jnp.int32)
            n_full += (meta[3, j * per_k + per_k - 1] + HB - 1 <= qmin).astype(jnp.int32)
        top[...] = jnp.full((TQ, HD), -1e29, F32)

        def score(j, masked):
            at = pl.ds(pl.multiple_of(j * TK, TK), TK)
            s = lax.dot_general(
                q, ks[at, :], (((1,), (1,)), ((), ())), preferred_element_type=F32
            )
            if masked:
                row = lax.broadcasted_iota(jnp.int32, (TQ, 1), 0)
                col = lax.broadcasted_iota(jnp.int32, (1, TK), 1)
                qpos, kpos = row, col
                for u in range(per_q):
                    qpos = jnp.where(row // HB == u, meta[2, i * per_q + u] + row % HB, qpos)
                for u in range(per_k):
                    kpos = jnp.where(col // HB == u, meta[3, j * per_k + u] + col % HB, kpos)
                s = jnp.where(kpos <= qpos, s, -1e30)
            scores[:, at] = s
            best = top[...]
            for u in range(TK // HD):
                best = jnp.maximum(best, s[:, u * HD : (u + 1) * HD])
            top[...] = best

        pl.loop(0, n_full)(lambda j: score(j, False))
        pl.loop(n_full, n_all)(lambda j: score(j, True))
        best = jnp.max(top[...], axis=1, keepdims=True)

        def step(j, acc):
            at = pl.ds(pl.multiple_of(j * TK, TK), TK)
            weight = jnp.exp2(scores[:, at] - best).astype(BF16)
            return acc + jnp.dot(weight, va[at, :], preferred_element_type=F32)

        acc = lax.fori_loop(0, n_all, step, jnp.zeros((TQ, 2 * HD), F32))
        total = acc[:, HD:]
        some = total > 0
        out = jnp.where(some, acc[:, :HD] / jnp.where(some, total, 1.0), 0.0).astype(BF16)
        lse = jnp.where(some, best + jnp.log2(jnp.where(some, total, 1.0)), -1e30)
        lanes = lse.T
        for u in range(per_q):
            oq = meta[0, i * per_q + u]
            o_out[oq] = out[u * HB : (u + 1) * HB, :]
            lse_out[oq // SLOTS, pl.ds(oq % SLOTS, 1), 0:HB] = lanes[0:1, u * HB : (u + 1) * HB]


def attend(meta, q, kv):
    vmem = pl.BlockSpec(memory_space=pltpu.VMEM)
    hbm = pl.BlockSpec(memory_space=pl.ANY)
    chunks = ALL // HB
    return pl.pallas_call(
        attend_kernel,
        out_shape=(
            jax.ShapeDtypeStruct((chunks, HB, HD), BF16),
            jax.ShapeDtypeStruct((SRC, SLOTS, HD), F32),
        ),
        in_specs=[pl.BlockSpec(memory_space=pltpu.SMEM), hbm, hbm],
        out_specs=(vmem, vmem),
        scratch_shapes=[
            pltpu.VMEM((ALL, HD), BF16),
            pltpu.VMEM((ALL, HD), BF16),
            pltpu.VMEM((ALL, 2 * HD), BF16),
            pltpu.VMEM((TQ, ALL), F32),
            pltpu.VMEM((TQ, HD), F32),
            pltpu.SemaphoreType.DMA((3,)),
        ],
        compiler_params=pltpu.CompilerParams(vmem_limit_bytes=60 << 20),
        name="attend",
    )(meta, q.reshape(chunks, HB, HD), kv.reshape(chunks, HB, 2 * HD))


def combine_kernel(
    o_hbm, lse_in, w_hbm, out_ref,
    w_ref, parts, lses, ctx, terms, halves, fulls, mirrored,
    w_sem, o_send, o_recv, l_send, l_recv, own_sem, h_send, h_recv, f_send, f_recv, z_send, z_recv,
):
    y, zl, c, x, zh = place()
    right = device(y, zl, c, (x + 1) % 4, zh)
    left = device(y, zl, c, (x + 3) % 4, zh)
    mirror = device(y, 3 - zl, c, x, 1 - zh)
    peers = [((zl + d) % 4, other_core(c, e)) for d, e in OTHERS]
    ids = [device(y, pz, pc, x, zh) for pz, pc in peers]
    mine = zl * 2 + c
    barrier = greet([right, left, mirror] + ids)
    own_o = pltpu.make_async_copy(o_hbm.at[mine], parts.at[mine], own_sem.at[0])
    own_l = pltpu.make_async_copy(lse_in.at[mine], lses.at[mine], own_sem.at[1])
    own_o.start()
    own_l.start()
    w_copy = pltpu.make_async_copy(w_hbm, w_ref, w_sem)
    w_copy.start()
    pl.semaphore_wait(barrier, len(ids) + 3)
    for i, (pz, pc) in enumerate(peers):
        to = pz * 2 + pc
        remote(lse_in.at[to], lses.at[mine], l_send.at[i], l_recv.at[mine], ids[i]).start()

    def o_rows(ref, index, group):
        first, last = GROUPS[group]
        return ref.at[index, pl.ds(first * HB, (last - first) * HB), :]

    for group in range(len(GROUPS)):
        for i, (pz, pc) in enumerate(peers):
            remote(
                o_rows(o_hbm, pz * 2 + pc, group), o_rows(parts, mine, group),
                o_send.at[i], o_recv.at[group, mine], ids[i],
            ).start()
    own_o.wait()
    own_l.wait()
    w_copy.wait()
    for i, (pz, pc) in enumerate(peers):
        src = pz * 2 + pc
        remote(lse_in.at[src], lses.at[src], l_send.at[i], l_recv.at[src], ids[i]).wait()

    stats = lses[...].reshape(SRC * SLOTS, HD)
    stats = jnp.concatenate([stats, stats], axis=0).T

    def term(group):
        for i, (pz, pc) in enumerate(peers):
            src = pz * 2 + pc
            remote(
                o_rows(o_hbm, src, group), o_rows(parts, src, group),
                o_send.at[i], o_recv.at[group, src], ids[i],
            ).wait_recv()
        first, last = GROUPS[group]
        for slot in range(first, last):
            lo, hi = slot * HB, (slot + 1) * HB
            for h in range(2):
                at = [(z * 2 + h) * SLOTS + slot for z in range(4)]
                cols = [stats[0:HB, i : i + 1] for i in at]
                best = jnp.maximum(jnp.maximum(cols[0], cols[1]), jnp.maximum(cols[2], cols[3]))
                shares = [jnp.exp2(col - best) for col in cols]
                total = shares[0] + shares[1] + shares[2] + shares[3]
                mixed = jnp.zeros((HB, HD), F32)
                for z in range(4):
                    mixed += (shares[z] / total) * parts[z * 2 + h, lo:hi, :].astype(F32)
                ctx[lo:hi, h * HD : (h + 1) * HD] = mixed.astype(BF16)
        lo, hi = first * HB, last * HB
        terms[lo:hi, :] = jnp.dot(ctx[lo:hi, :], w_ref[...], preferred_element_type=F32).astype(BF16)

    def at(slot, lo=0, hi=HB):
        return terms.at[pl.ds(slot * HB + lo, hi - lo), :]

    def far_half(p, slot, side, lo, hi, peer):
        return remote(at(slot, lo, hi), halves.at[p, side], h_send.at[p, side], h_recv.at[p, side], peer)

    def near_half(p, slot, side, upper, peer):
        lo = HALF if upper else 0
        return remote(
            at(slot, lo, lo + HALF), fulls.at[p, side, pl.ds(lo, HALF), :],
            f_send.at[p, side, upper], f_recv.at[p, side, upper], peer,
        )

    def add(lo, more):
        rows = slice(lo, lo + HALF)
        terms[rows, :] = (terms[rows, :].astype(F32) + more.astype(F32)).astype(BF16)

    started = []

    def begin(copy):
        copy.start()
        started.append(copy)
        return copy

    def send_far(p, slot):
        return (
            begin(far_half(p, slot, 0, 0, HALF, right)),
            begin(far_half(p, slot, 1, HALF, HB, left)),
        )

    def send_near(p, from_left, from_right, passed):
        right_hi = begin(near_half(p, from_right, 0, 1, right))
        left_lo = begin(near_half(p, from_left, 1, 0, left))
        passed[0].wait_recv()
        add(from_right * HB, halves[p, 0])
        right_lo = begin(near_half(p, from_right, 0, 0, right))
        passed[1].wait_recv()
        add(from_left * HB + HALF, halves[p, 1])
        left_hi = begin(near_half(p, from_left, 1, 1, left))
        return (right_lo, left_lo), (right_hi, left_hi)

    term(0)
    passed = send_far(1, O1)
    term(1)
    low, high = send_near(1, L1, R1, passed)
    term(2)
    term(3)
    passed = send_far(0, O0)
    mirrors = []
    for upper, copies in enumerate((low, high)):
        for copy in copies:
            copy.wait_recv()
        rows = slice(upper * HALF, (upper + 1) * HALF)
        add(MIR * HB + upper * HALF, fulls[1, 0, rows].astype(F32) + fulls[1, 1, rows].astype(F32))
        mirrors.append(begin(remote(
            at(MIR, upper * HALF, (upper + 1) * HALF), mirrored.at[rows, :],
            z_send.at[upper], z_recv.at[upper], mirror,
        )))
    term(4)
    low, high = send_near(0, L0, R0, passed)
    term(5)
    for upper, copies in enumerate((low, high)):
        rows = slice(upper * HALF, (upper + 1) * HALF)
        for copy in copies:
            copy.wait_recv()
        mirrors[upper].wait_recv()
        total = terms[rows, :].astype(F32) + fulls[0, 0, rows].astype(F32)
        total = total + fulls[0, 1, rows].astype(F32) + mirrored[rows, :].astype(F32)
        out_ref[rows, :] = total.astype(BF16)
    for copy in started:
        copy.wait_send()
    for i, (pz, pc) in enumerate(peers):
        src = pz * 2 + pc
        remote(o_hbm.at[src], parts.at[src], o_send.at[i], o_recv.at[0, src], ids[i]).wait_send()


def combine(o, lse, out_weight):
    vmem = pl.BlockSpec(memory_space=pltpu.VMEM)
    hbm = pl.BlockSpec(memory_space=pl.ANY)
    dma = pltpu.SemaphoreType.DMA
    return pl.pallas_call(
        combine_kernel,
        out_shape=jax.ShapeDtypeStruct((HB, D), BF16),
        in_specs=[hbm, hbm, hbm],
        out_specs=vmem,
        scratch_shapes=[
            pltpu.VMEM((2 * HD, D), BF16),
            pltpu.VMEM((SRC, ROWS, HD), BF16),
            pltpu.VMEM((SRC, SLOTS, HD), F32),
            pltpu.VMEM((ROWS, 2 * HD), BF16),
            pltpu.VMEM((ROWS, D), BF16),
            pltpu.VMEM((2, 2, HALF, D), BF16),
            pltpu.VMEM((2, 2, HB, D), BF16),
            pltpu.VMEM((HB, D), BF16),
            dma, dma((SRC,)), dma((len(GROUPS), SRC)), dma((SRC,)), dma((SRC,)), dma((2,)),
            dma((2, 2)), dma((2, 2)), dma((2, 2, 2)), dma((2, 2, 2)), dma((2,)), dma((2,)),
        ],
        compiler_params=pltpu.CompilerParams(
            collective_id=1, has_side_effects=True, vmem_limit_bytes=60 << 20
        ),
        name="combine",
    )(o.reshape(SRC, ROWS, HD), lse, out_weight)


def local(hidden_in, norm_gain, qkv_weight, out_weight, block_order):
    y, zl, c, x, zh = place()
    starts = starts_of(block_order, y, zl, c, x, zh)
    order, first = sort_chunks(starts[: 2 * SRC * SLOTS].reshape(2, SRC * SLOTS))
    meta = jnp.concatenate([order, first], axis=0)
    mine = starts[2 * SRC * SLOTS :]
    position = (mine[:, None] + jnp.arange(HB, dtype=jnp.int32)[None, :]).reshape(-1)
    inv_freq = 10000.0 ** (-(jnp.arange(HD // 2, dtype=F32) * 2.0 / HD))
    angle = position.astype(F32)[:, None] * inv_freq[None, :]
    cosine, sine = jnp.cos(angle), jnp.sin(angle)
    cos = jnp.concatenate([cosine, cosine], axis=1)
    sin = jnp.concatenate([-sine, sine], axis=1)

    weight = jnp.transpose(qkv_weight, (1, 0, 2))
    q, kv = project(hidden_in, norm_gain[None, :], weight, cos, sin)
    o, lse = attend(meta, q, kv)
    return combine(o, lse, out_weight)


def solution(mesh):
    in_specs = (P(("seq", "tp"), None), P(), P(None, None, "tp"), P("tp", None), P())
    out_specs = P(("seq", "tp"), None)
    return jax.shard_map(local, mesh=mesh, in_specs=in_specs, out_specs=out_specs, check_vma=False)
```

```python
import math

import jax
import jax.numpy as jnp
import numpy as np
from jax import lax
from jax.experimental import pallas as pl
from jax.experimental.pallas import tpu as pltpu
from jax.sharding import PartitionSpec as P

HD = 128
BLK = 128
D = 4096
SEQ = 16384
HB = 64
SLOTS = 8
ROWS = HB * SLOTS
SRC = 8
ALL = SRC * ROWS
HALF = HB // 2
TQ = SRC * HB
TK = 1024
MESH = pl.DeviceIdType.MESH
F32 = jnp.float32
BF16 = jnp.bfloat16

O1, L1, R1, MIR, O0, L0, R0, OWN = range(8)
CHUNKS = ((1, 2), (1, -1), (1, 1), (1, 0), (0, 2), (0, -1), (0, 1), (0, 0))
SCALE = math.log2(math.e) / HD**0.5
OTHERS = [(d, e) for d in range(4) for e in range(2)][1:]


def place():
    s = lax.axis_index("seq")
    t = lax.axis_index("tp")
    return s // 8, (s // 2) % 4, s % 2, t // 2, t % 2


def device(y, zl, c, x, zh):
    return ((y * 4 + zl) * 2 + c, x * 2 + zh)


def other_core(c, e):
    return 1 - c if e else c


def start_of(order, slot, y, zl, c, x, zh):
    mirrored, shift = CHUNKS[slot]
    if mirrored:
        zl, zh = 3 - zl, 1 - zh
    block = ((y * 4 + zl) * 2 + c) * (ROWS // BLK) + (x + shift + 4) % 4
    return order[block] * BLK + zh * HB


def tables():
    frequency = 10000.0 ** (-(np.arange(HD) % (HD // 2)) * 2.0 / HD)
    starts = np.arange(SEQ // HB)[:, None] * float(HB) * frequency[None, :]
    rows = np.arange(HB)[:, None] * frequency[None, :]
    made = [np.cos(starts), np.sin(starts), np.cos(rows), np.sin(rows)]
    return [jnp.asarray(t.astype(np.float32)) for t in made]


def greet(peers):
    barrier = pltpu.get_barrier_semaphore()
    for peer in peers:
        pl.semaphore_signal(barrier, inc=1, device_id=peer, device_id_type=MESH)
    return barrier


def remote(src, dst, send, recv, peer):
    return pltpu.make_async_remote_copy(
        src_ref=src, dst_ref=dst, send_sem=send, recv_sem=recv, device_id=peer, device_id_type=MESH
    )


def project_kernel(
    order, hid, gain, w_hbm, cos_start, sin_start, cos_row, sin_row, q_out, kv_out,
    rows, cos, sin, wv, qs, kvs, w_sem, x_send, x_recv, z_send, z_recv,
    kv_send, kv_recv, q_send, q_recv, own_sem,
):
    y, zl, c, x, zh = place()
    right = device(y, zl, c, (x + 1) % 4, zh)
    left = device(y, zl, c, (x + 3) % 4, zh)
    mirror = device(y, 3 - zl, c, x, 1 - zh)
    kv_peers = [((y + d) % 4, other_core(c, e)) for d, e in OTHERS]
    q_peers = [((zl + d) % 4, other_core(c, e)) for d, e in OTHERS]
    kv_ids = [device(py, zl, pc, x, zh) for py, pc in kv_peers]
    q_ids = [device(y, pz, pc, x, zh) for pz, pc in q_peers]
    peers = [right, left, mirror] + kv_ids + q_ids[1:]
    barrier = greet(peers)
    w_copy = pltpu.make_async_copy(w_hbm, wv, w_sem)
    w_copy.start()

    floats = hid[...].astype(F32)
    scale = lax.rsqrt(jnp.mean(floats * floats, axis=-1, keepdims=True) + 1e-05)
    rows[OWN * HB : (OWN + 1) * HB, :] = (floats * scale * gain[...]).astype(BF16)
    first_half = lax.broadcasted_iota(jnp.int32, (1, HD), 1) < HD // 2
    for slot in range(SLOTS):
        start = start_of(order, slot, y, zl, c, x, zh) // HB
        cs, sn = cos_start[pl.ds(start, 1), :], sin_start[pl.ds(start, 1), :]
        lo, hi = slot * HB, (slot + 1) * HB
        cos[lo:hi, :] = cs * cos_row[...] - sn * sin_row[...]
        sine = sn * cos_row[...] + cs * sin_row[...]
        sin[lo:hi, :] = jnp.where(first_half, -sine, sine)
    pl.semaphore_wait(barrier, len(peers))

    def at(slot, lo=0, hi=HB):
        return rows.at[pl.ds(slot * HB + lo, hi - lo), :]

    def step(p, kind, src, dst, lo, hi, peer):
        return remote(at(src, lo, hi), at(dst, lo, hi), x_send.at[p, kind], x_recv.at[p, kind], peer)

    def ring(p, src, from_left, from_right, far):
        return (
            step(p, 0, src, from_left, 0, HALF, right),
            step(p, 1, src, from_right, HALF, HB, left),
            step(p, 2, src, from_left, HALF, HB, right),
            step(p, 3, src, from_right, 0, HALF, left),
            step(p, 4, from_left, far, 0, HALF, right),
            step(p, 5, from_right, far, HALF, HB, left),
        )

    mirror_lo = remote(at(OWN, 0, HALF), at(MIR, 0, HALF), z_send.at[0], z_recv.at[0], mirror)
    mirror_hi = remote(at(OWN, HALF, HB), at(MIR, HALF, HB), z_send.at[1], z_recv.at[1], mirror)
    near = ring(0, OWN, L0, R0, O0)
    far = ring(1, MIR, L1, R1, O1)

    mirror_lo.start()
    mirror_hi.start()
    for copy in near[:4]:
        copy.start()
    mine = y * 2 + c
    mine_q = zl * 2 + c

    def part(ref, lo, hi, *index):
        return ref.at[(*index, pl.ds(lo, hi - lo), slice(None))]

    def work(first, last):
        lo, hi = first * HB, last * HB
        chunk = rows[lo:hi, :]
        cs, sn = cos[lo:hi, :], sin[lo:hi, :]
        q = jnp.dot(chunk, wv[0], preferred_element_type=F32)
        k = jnp.dot(chunk, wv[1], preferred_element_type=F32)
        v = jnp.dot(chunk, wv[2], preferred_element_type=F32)
        for h in range(2):
            lane = slice(h * HD, (h + 1) * HD)
            for out, by, t in ((qs, SCALE, q[:, lane]), (kvs, 1.0, k[:, lane])):
                turned = t * cs + pltpu.roll(t, HD // 2, 1) * sn
                out[h, lo:hi, 0:HD] = (turned * by).astype(BF16)
            kvs[h, lo:hi, HD : 2 * HD] = v[:, lane].astype(BF16)
        for i, (py, pc) in enumerate(kv_peers):
            remote(
                part(kvs, lo, hi, pc), part(kv_out, lo, hi, mine),
                kv_send.at[i], kv_recv.at[mine], kv_ids[i],
            ).start()
        for i, (pz, pc) in enumerate(q_peers):
            remote(
                part(qs, lo, hi, pc), part(q_out, lo, hi, mine_q),
                q_send.at[i], q_recv.at[mine_q], q_ids[i],
            ).start()

    w_copy.wait()
    work(OWN, OWN + 1)
    near[0].wait_recv()
    near[4].start()
    near[1].wait_recv()
    near[5].start()
    near[2].wait_recv()
    near[3].wait_recv()
    work(L0, R0 + 1)
    mirror_lo.wait_recv()
    far[0].start()
    far[3].start()
    near[4].wait_recv()
    near[5].wait_recv()
    work(O0, O0 + 1)
    mirror_hi.wait_recv()
    far[1].start()
    far[2].start()
    work(MIR, MIR + 1)
    far[0].wait_recv()
    far[4].start()
    far[1].wait_recv()
    far[5].start()
    far[2].wait_recv()
    far[3].wait_recv()
    work(L1, R1 + 1)
    far[4].wait_recv()
    far[5].wait_recv()
    work(O1, O1 + 1)
    own_kv = pltpu.make_async_copy(kvs.at[c], kv_out.at[mine], own_sem.at[0])
    own_q = pltpu.make_async_copy(qs.at[c], q_out.at[mine_q], own_sem.at[1])
    own_kv.start()
    own_q.start()
    for copy in (mirror_lo, mirror_hi, *near, *far):
        copy.wait_send()
    for i, (py, pc) in enumerate(kv_peers):
        src = py * 2 + pc
        done = remote(kvs.at[pc], kv_out.at[src], kv_send.at[i], kv_recv.at[src], kv_ids[i])
        done.wait_send()
        done.wait_recv()
    for i, (pz, pc) in enumerate(q_peers):
        src = pz * 2 + pc
        done = remote(qs.at[pc], q_out.at[src], q_send.at[i], q_recv.at[src], q_ids[i])
        done.wait_send()
        done.wait_recv()
    own_kv.wait()
    own_q.wait()


def project(block_order, hidden_in, norm_gain, weight):
    vmem = pl.BlockSpec(memory_space=pltpu.VMEM)
    hbm = pl.BlockSpec(memory_space=pl.ANY)
    dma = pltpu.SemaphoreType.DMA
    return pl.pallas_call(
        project_kernel,
        out_shape=(
            jax.ShapeDtypeStruct((SRC, ROWS, HD), BF16),
            jax.ShapeDtypeStruct((SRC, ROWS, 2 * HD), BF16),
        ),
        in_specs=[pl.BlockSpec(memory_space=pltpu.SMEM), vmem, vmem, hbm, vmem, vmem, vmem, vmem],
        out_specs=(hbm, hbm),
        scratch_shapes=[
            pltpu.VMEM((ROWS, D), BF16),
            pltpu.VMEM((ROWS, HD), F32),
            pltpu.VMEM((ROWS, HD), F32),
            pltpu.VMEM((3, D, 2 * HD), BF16),
            pltpu.VMEM((2, ROWS, HD), BF16),
            pltpu.VMEM((2, ROWS, 2 * HD), BF16),
            dma, dma((2, 6)), dma((2, 6)), dma((2,)), dma((2,)),
            dma((SRC,)), dma((SRC,)), dma((SRC,)), dma((SRC,)), dma((2,)),
        ],
        compiler_params=pltpu.CompilerParams(
            collective_id=0, has_side_effects=True, vmem_limit_bytes=60 << 20
        ),
        name="project",
    )(block_order, hidden_in, norm_gain, weight, *tables())


def attend_kernel(
    order, q_hbm, kv_hbm, w_hbm, out_ref,
    q_ref, kv_ref, w_ref, scores, top, sums, qpos, kpos, o_mine, l_mine, parts, lses,
    ctx, terms, halves, fulls, mirrored,
    in_sem, o_send, o_recv, l_send, l_recv, h_send, h_recv, f_send, f_recv, z_send, z_recv,
):
    y, zl, c, x, zh = place()
    right = device(y, zl, c, (x + 1) % 4, zh)
    left = device(y, zl, c, (x + 3) % 4, zh)
    mirror = device(y, 3 - zl, c, x, 1 - zh)
    peers = [((zl + d) % 4, other_core(c, e)) for d, e in OTHERS]
    ids = [device(y, pz, pc, x, zh) for pz, pc in peers]
    mine = zl * 2 + c
    barrier = greet([right, left, mirror] + ids)
    loads = [
        pltpu.make_async_copy(src, dst, in_sem.at[i])
        for i, (src, dst) in enumerate(((q_hbm, q_ref), (kv_hbm, kv_ref), (w_hbm, w_ref)))
    ]
    for load in loads:
        load.start()

    lane = lax.broadcasted_iota(jnp.int32, (1, HD), 1)
    row = lax.broadcasted_iota(jnp.int32, (HB, HD), 0)
    for src in range(SRC):
        starts = [start_of(order, slot, src // 2, zl, src % 2, x, zh) for slot in range(SLOTS)]
        for u in range(SLOTS // 2):
            kpos[src * (SLOTS // 2) + u] = jnp.where(
                lane < HB, starts[2 * u] + lane, starts[2 * u + 1] + lane - HB
            )
        for slot in range(SLOTS):
            qpos[slot, src * HB : (src + 1) * HB, :] = row + start_of(
                order, slot, y, src // 2, src % 2, x, zh
            )
    diagonal = lax.broadcasted_iota(jnp.int32, (HD, HD), 0) == lax.broadcasted_iota(
        jnp.int32, (HD, HD), 1
    )
    per = TK // HD
    for load in loads:
        load.wait()
    pl.semaphore_wait(barrier, len(ids) + 3)

    def attend_chunk(t):
        at = pl.ds(pl.multiple_of(t * HB, HB), HB)
        q = q_ref[:, at, :].reshape(TQ, HD)
        top[...] = jnp.full((TQ, HD), -1e29, F32)
        sums[...] = jnp.zeros((TQ, HD), F32)
        for j in range(ALL // TK):
            keys = kv_ref[j * TK : (j + 1) * TK, 0:HD]
            s = lax.dot_general(q, keys, (((1,), (1,)), ((), ())), preferred_element_type=F32)
            best = top[...]
            for u in range(per):
                keep = kpos[j * per + u] <= qpos[t]
                kept = jnp.where(keep, s[:, u * HD : (u + 1) * HD], -1e30)
                scores[j * per + u] = kept
                best = jnp.maximum(best, kept)
            top[...] = best
        best = jnp.broadcast_to(jnp.max(top[...], axis=1, keepdims=True), (TQ, HD))
        acc = jnp.zeros((TQ, HD), F32)
        for j in range(ALL // TK):
            weight = [jnp.exp2(scores[j * per + u] - best) for u in range(per)]
            total = sums[...]
            for part in weight:
                total = total + part
            sums[...] = total
            weight = jnp.concatenate([part.astype(BF16) for part in weight], axis=1)
            values = kv_ref[j * TK : (j + 1) * TK, HD : 2 * HD]
            acc = acc + jnp.dot(weight, values, preferred_element_type=F32)
        total = jnp.broadcast_to(jnp.sum(sums[...], axis=1, keepdims=True), (TQ, HD))
        some = total > 0
        total = jnp.where(some, total, 1.0)
        o_mine[t] = (acc / total).astype(BF16).reshape(SRC, HB, HD)
        lse = jnp.where(some, best + jnp.log2(total), -1e30)
        for u in range(SRC // 2):
            block = lse[u * HD : (u + 1) * HD, :]
            line = jnp.sum(jnp.where(diagonal, block, 0.0), axis=0, keepdims=True)
            l_mine[t, 2 * u, 0:1, :] = line
            l_mine[t, 2 * u + 1, 0:1, :] = pltpu.roll(line, HB, 1)
        parts[t, mine] = o_mine[t, mine]
        lses[t, mine] = l_mine[t, mine]
        for i, (pz, pc) in enumerate(peers):
            to = pz * 2 + pc
            remote(
                l_mine.at[t, to], lses.at[t, mine], l_send.at[i], l_recv.at[t, mine], ids[i]
            ).start()
            remote(
                o_mine.at[t, to], parts.at[t, mine], o_send.at[i], o_recv.at[t, mine], ids[i]
            ).start()

    def term(t):
        for i, (pz, pc) in enumerate(peers):
            src = pz * 2 + pc
            remote(
                l_mine.at[t, src], lses.at[t, src], l_send.at[i], l_recv.at[t, src], ids[i]
            ).wait_recv()
            remote(
                o_mine.at[t, src], parts.at[t, src], o_send.at[i], o_recv.at[t, src], ids[i]
            ).wait_recv()
        stats = jnp.concatenate([lses[t, src, 0:1, :] for src in range(SRC)], axis=0)
        stats = jnp.concatenate([stats] * (HD // SRC), axis=0).T
        for h in range(2):
            cols = [stats[0:HB, z * 2 + h : z * 2 + h + 1] for z in range(4)]
            best = jnp.maximum(jnp.maximum(cols[0], cols[1]), jnp.maximum(cols[2], cols[3]))
            shares = [jnp.exp2(col - best) for col in cols]
            total = shares[0] + shares[1] + shares[2] + shares[3]
            mixed = jnp.zeros((HB, HD), F32)
            for z in range(4):
                mixed += (shares[z] / total) * parts[t, z * 2 + h].astype(F32)
            ctx[:, h * HD : (h + 1) * HD] = mixed.astype(BF16)
        at = pl.ds(pl.multiple_of(t * HB, HB), HB)
        terms[at, :] = jnp.dot(ctx[...], w_ref[...], preferred_element_type=F32).astype(BF16)

    def cols(v):
        return pl.ds(v * (D // 2), D // 2)

    def at(slot, lo, v):
        return terms.at[pl.ds(slot * HB + lo, HALF), cols(v)]

    def far(p, slot, side, v):
        return remote(
            at(slot, side * HALF, v), halves.at[p, side, :, cols(v)],
            h_send.at[p, side, v], h_recv.at[p, side, v], left if side else right,
        )

    def near(p, slot, side, upper, v):
        return remote(
            at(slot, upper * HALF, v), fulls.at[p, side, pl.ds(upper * HALF, HALF), cols(v)],
            f_send.at[p, side, upper, v], f_recv.at[p, side, upper, v], left if side else right,
        )

    def over(upper, v):
        return remote(
            at(MIR, upper * HALF, v), mirrored.at[pl.ds(upper * HALF, HALF), cols(v)],
            z_send.at[upper, v], z_recv.at[upper, v], mirror,
        )

    fars, nears = (O0, O1), ((R0, L0), (R1, L1))

    def add(lo, v, *more):
        rows, columns = slice(lo, lo + HALF), slice(v * (D // 2), (v + 1) * (D // 2))
        total = terms[rows, columns].astype(F32)
        for ref in more:
            total = total + ref[:, columns].astype(F32)
        return total

    def store(lo, v, total):
        terms[lo : lo + HALF, v * (D // 2) : (v + 1) * (D // 2)] = total.astype(BF16)

    def send_far(p):
        for v in range(2):
            for side in range(2):
                far(p, fars[p], side, v).start()

    def send_near(p, side):
        slot = nears[p][side]
        lo = slot * HB + side * HALF
        for v in range(2):
            near(p, slot, side, 1 - side, v).start()
            far(p, fars[p], side, v).wait_recv()
            store(lo, v, add(lo, v, halves.at[p, side]))
            near(p, slot, side, side, v).start()

    def send_over(v):
        for upper in range(2):
            for side in range(2):
                near(1, nears[1][side], side, upper, v).wait_recv()
            lo = MIR * HB + upper * HALF
            rows = pl.ds(upper * HALF, HALF)
            store(lo, v, add(lo, v, fulls.at[1, 0, rows], fulls.at[1, 1, rows]))
            over(upper, v).start()

    @pl.loop(0, SLOTS)
    def _(t):
        attend_chunk(t)
        pl.when(t > 0)(lambda: term(t - 1))

        @pl.when(t == O1 + 1)
        def _():
            send_far(1)

        @pl.when(t == L1 + 1)
        def _():
            send_near(1, 1)

        @pl.when(t == R1 + 1)
        def _():
            send_near(1, 0)

        @pl.when(t == O0 + 1)
        def _():
            send_far(0)
            send_over(0)

        @pl.when(t == L0 + 1)
        def _():
            send_over(1)
            send_near(0, 1)

        @pl.when(t == R0 + 1)
        def _():
            send_near(0, 0)

    term(OWN)
    for v in range(2):
        for upper in range(2):
            for side in range(2):
                near(0, nears[0][side], side, upper, v).wait_recv()
            over(upper, v).wait_recv()
            rows = pl.ds(upper * HALF, HALF)
            total = add(
                OWN * HB + upper * HALF, v, fulls.at[0, 0, rows], fulls.at[0, 1, rows], mirrored.at[rows]
            )
            out_ref[rows, v * (D // 2) : (v + 1) * (D // 2)] = total.astype(BF16)
    for v in range(2):
        for p in range(2):
            for side in range(2):
                far(p, fars[p], side, v).wait_send()
                for upper in range(2):
                    near(p, nears[p][side], side, upper, v).wait_send()
        for upper in range(2):
            over(upper, v).wait_send()
    for i, (pz, pc) in enumerate(peers):
        src = pz * 2 + pc
        remote(l_mine.at[:, src], lses.at[:, src], l_send.at[i], l_recv.at[0, src], ids[i]).wait_send()
        remote(o_mine.at[:, src], parts.at[:, src], o_send.at[i], o_recv.at[0, src], ids[i]).wait_send()


def attend(block_order, q, kv, out_weight):
    vmem = pl.BlockSpec(memory_space=pltpu.VMEM)
    hbm = pl.BlockSpec(memory_space=pl.ANY)
    dma = pltpu.SemaphoreType.DMA
    return pl.pallas_call(
        attend_kernel,
        out_shape=jax.ShapeDtypeStruct((HB, D), BF16),
        in_specs=[pl.BlockSpec(memory_space=pltpu.SMEM), hbm, hbm, hbm],
        out_specs=vmem,
        scratch_shapes=[
            pltpu.VMEM((SRC, ROWS, HD), BF16),
            pltpu.VMEM((ALL, 2 * HD), BF16),
            pltpu.VMEM((2 * HD, D), BF16),
            pltpu.VMEM((ALL // HD, TQ, HD), F32),
            pltpu.VMEM((TQ, HD), F32),
            pltpu.VMEM((TQ, HD), F32),
            pltpu.VMEM((SLOTS, TQ, HD), jnp.int32),
            pltpu.VMEM((ALL // HD, 1, HD), jnp.int32),
            pltpu.VMEM((SLOTS, SRC, HB, HD), BF16),
            pltpu.VMEM((SLOTS, SRC, 8, HD), F32),
            pltpu.VMEM((SLOTS, SRC, HB, HD), BF16),
            pltpu.VMEM((SLOTS, SRC, 8, HD), F32),
            pltpu.VMEM((HB, 2 * HD), BF16),
            pltpu.VMEM((ROWS, D), BF16),
            pltpu.VMEM((2, 2, HALF, D), BF16),
            pltpu.VMEM((2, 2, HB, D), BF16),
            pltpu.VMEM((HB, D), BF16),
            dma((3,)),
            dma((SRC,)), dma((SLOTS, SRC)), dma((SRC,)), dma((SLOTS, SRC)),
            dma((2, 2, 2)), dma((2, 2, 2)), dma((2, 2, 2, 2)), dma((2, 2, 2, 2)),
            dma((2, 2)), dma((2, 2)),
        ],
        compiler_params=pltpu.CompilerParams(
            collective_id=1, has_side_effects=True, vmem_limit_bytes=58 << 20
        ),
        name="attend",
    )(block_order, q, kv.reshape(ALL, 2 * HD), out_weight)


def local(hidden_in, norm_gain, qkv_weight, out_weight, block_order):
    weight = jnp.transpose(qkv_weight, (1, 0, 2))
    q, kv = project(block_order, hidden_in, norm_gain[None, :], weight)
    return attend(block_order, q, kv, out_weight)


def solution(mesh):
    in_specs = (P(("seq", "tp"), None), P(), P(None, None, "tp"), P("tp", None), P())
    out_specs = P(("seq", "tp"), None)
    return jax.shard_map(local, mesh=mesh, in_specs=in_specs, out_specs=out_specs, check_vma=False)
```

```python
import math

import jax
import jax.numpy as jnp
import numpy as np
from jax import lax
from jax.experimental import pallas as pl
from jax.experimental.pallas import tpu as pltpu
from jax.sharding import PartitionSpec as P

HD = 128
BLK = 128
D = 4096
SEQ = 16384
HB = 64
SLOTS = 8
ROWS = HB * SLOTS
SRC = 8
ALL = SRC * ROWS
HALF = HB // 2
TQ = SRC * HB
TK = 4096
MESH = pl.DeviceIdType.MESH
F32 = jnp.float32
BF16 = jnp.bfloat16

O1, L1, R1, MIR, O0, L0, R0, OWN = range(8)
CHUNKS = ((1, 2), (1, -1), (1, 1), (1, 0), (0, 2), (0, -1), (0, 1), (0, 0))
SCALE = math.log2(math.e) / HD**0.5
OTHERS = [(d, e) for d in range(4) for e in range(2)][1:]


def place():
    s = lax.axis_index("seq")
    t = lax.axis_index("tp")
    return s // 8, (s // 2) % 4, s % 2, t // 2, t % 2


def device(y, zl, c, x, zh):
    return ((y * 4 + zl) * 2 + c, x * 2 + zh)


def other_core(c, e):
    return 1 - c if e else c


def start_of(order, slot, y, zl, c, x, zh):
    mirrored, shift = CHUNKS[slot]
    if mirrored:
        zl, zh = 3 - zl, 1 - zh
    block = ((y * 4 + zl) * 2 + c) * (ROWS // BLK) + (x + shift + 4) % 4
    return order[block] * BLK + zh * HB


def tables():
    frequency = 10000.0 ** (-(np.arange(HD) % (HD // 2)) * 2.0 / HD)
    starts = np.arange(SEQ // HB)[:, None] * float(HB) * frequency[None, :]
    rows = np.arange(HB)[:, None] * frequency[None, :]
    made = [np.cos(starts), np.sin(starts), np.cos(rows), np.sin(rows)]
    return [jnp.asarray(t.astype(np.float32)) for t in made]


def greet(peers):
    barrier = pltpu.get_barrier_semaphore()
    for peer in peers:
        pl.semaphore_signal(barrier, inc=1, device_id=peer, device_id_type=MESH)
    return barrier


def remote(src, dst, send, recv, peer):
    return pltpu.make_async_remote_copy(
        src_ref=src, dst_ref=dst, send_sem=send, recv_sem=recv, device_id=peer, device_id_type=MESH
    )


def project_kernel(
    order, hid, gain, w_hbm, cos_start, sin_start, cos_row, sin_row, q_out, kv_out,
    rows, cos, sin, wv, qs, kvs, w_sem, x_send, x_recv, z_send, z_recv,
    kv_send, kv_recv, q_send, q_recv, own_sem,
):
    y, zl, c, x, zh = place()
    right = device(y, zl, c, (x + 1) % 4, zh)
    left = device(y, zl, c, (x + 3) % 4, zh)
    mirror = device(y, 3 - zl, c, x, 1 - zh)
    kv_peers = [((y + d) % 4, other_core(c, e)) for d, e in OTHERS]
    q_peers = [((zl + d) % 4, other_core(c, e)) for d, e in OTHERS]
    kv_ids = [device(py, zl, pc, x, zh) for py, pc in kv_peers]
    q_ids = [device(y, pz, pc, x, zh) for pz, pc in q_peers]
    peers = [right, left, mirror] + kv_ids + q_ids[1:]
    barrier = greet(peers)
    w_copy = pltpu.make_async_copy(w_hbm, wv, w_sem)
    w_copy.start()

    floats = hid[...].astype(F32)
    scale = lax.rsqrt(jnp.mean(floats * floats, axis=-1, keepdims=True) + 1e-05)
    rows[OWN * HB : (OWN + 1) * HB, :] = (floats * scale * gain[...]).astype(BF16)
    first_half = lax.broadcasted_iota(jnp.int32, (1, HD), 1) < HD // 2
    for slot in range(SLOTS):
        start = start_of(order, slot, y, zl, c, x, zh) // HB
        cs, sn = cos_start[pl.ds(start, 1), :], sin_start[pl.ds(start, 1), :]
        lo, hi = slot * HB, (slot + 1) * HB
        cos[lo:hi, :] = cs * cos_row[...] - sn * sin_row[...]
        sine = sn * cos_row[...] + cs * sin_row[...]
        sin[lo:hi, :] = jnp.where(first_half, -sine, sine)
    pl.semaphore_wait(barrier, len(peers))

    def at(slot, lo=0, hi=HB):
        return rows.at[pl.ds(slot * HB + lo, hi - lo), :]

    def step(p, kind, src, dst, lo, hi, peer):
        return remote(at(src, lo, hi), at(dst, lo, hi), x_send.at[p, kind], x_recv.at[p, kind], peer)

    def ring(p, src, from_left, from_right, far):
        return (
            step(p, 0, src, from_left, 0, HALF, right),
            step(p, 1, src, from_right, HALF, HB, left),
            step(p, 2, src, from_left, HALF, HB, right),
            step(p, 3, src, from_right, 0, HALF, left),
            step(p, 4, from_left, far, 0, HALF, right),
            step(p, 5, from_right, far, HALF, HB, left),
        )

    mirror_lo = remote(at(OWN, 0, HALF), at(MIR, 0, HALF), z_send.at[0], z_recv.at[0], mirror)
    mirror_hi = remote(at(OWN, HALF, HB), at(MIR, HALF, HB), z_send.at[1], z_recv.at[1], mirror)
    near = ring(0, OWN, L0, R0, O0)
    far = ring(1, MIR, L1, R1, O1)

    mirror_lo.start()
    mirror_hi.start()
    for copy in near[:4]:
        copy.start()
    mine = y * 2 + c
    mine_q = zl * 2 + c

    def part(ref, lo, hi, *index):
        return ref.at[(*index, pl.ds(lo, hi - lo), slice(None))]

    def work(first, last):
        lo, hi = first * HB, last * HB
        chunk = rows[lo:hi, :]
        cs, sn = cos[lo:hi, :], sin[lo:hi, :]
        q = jnp.dot(chunk, wv[0], preferred_element_type=F32)
        k = jnp.dot(chunk, wv[1], preferred_element_type=F32)
        v = jnp.dot(chunk, wv[2], preferred_element_type=F32)
        for h in range(2):
            lane = slice(h * HD, (h + 1) * HD)
            for out, by, t in ((qs, SCALE, q[:, lane]), (kvs, 1.0, k[:, lane])):
                turned = t * cs + pltpu.roll(t, HD // 2, 1) * sn
                out[h, lo:hi, 0:HD] = (turned * by).astype(BF16)
            kvs[h, lo:hi, HD : 2 * HD] = v[:, lane].astype(BF16)
        for i, (py, pc) in enumerate(kv_peers):
            remote(
                part(kvs, lo, hi, pc), part(kv_out, lo, hi, mine),
                kv_send.at[i], kv_recv.at[mine], kv_ids[i],
            ).start()
        for i, (pz, pc) in enumerate(q_peers):
            remote(
                part(qs, lo, hi, pc), part(q_out, lo, hi, mine_q),
                q_send.at[i], q_recv.at[mine_q], q_ids[i],
            ).start()

    w_copy.wait()
    work(OWN, OWN + 1)
    near[0].wait_recv()
    near[4].start()
    near[1].wait_recv()
    near[5].start()
    near[2].wait_recv()
    near[3].wait_recv()
    work(L0, R0 + 1)
    mirror_lo.wait_recv()
    far[0].start()
    far[3].start()
    near[4].wait_recv()
    near[5].wait_recv()
    work(O0, O0 + 1)
    mirror_hi.wait_recv()
    far[1].start()
    far[2].start()
    work(MIR, MIR + 1)
    far[0].wait_recv()
    far[4].start()
    far[1].wait_recv()
    far[5].start()
    far[2].wait_recv()
    far[3].wait_recv()
    work(L1, R1 + 1)
    far[4].wait_recv()
    far[5].wait_recv()
    work(O1, O1 + 1)
    own_kv = pltpu.make_async_copy(kvs.at[c], kv_out.at[mine], own_sem.at[0])
    own_q = pltpu.make_async_copy(qs.at[c], q_out.at[mine_q], own_sem.at[1])
    own_kv.start()
    own_q.start()
    for copy in (mirror_lo, mirror_hi, *near, *far):
        copy.wait_send()
    for i, (py, pc) in enumerate(kv_peers):
        src = py * 2 + pc
        done = remote(kvs.at[pc], kv_out.at[src], kv_send.at[i], kv_recv.at[src], kv_ids[i])
        done.wait_send()
        done.wait_recv()
    for i, (pz, pc) in enumerate(q_peers):
        src = pz * 2 + pc
        done = remote(qs.at[pc], q_out.at[src], q_send.at[i], q_recv.at[src], q_ids[i])
        done.wait_send()
        done.wait_recv()
    own_kv.wait()
    own_q.wait()


def project(block_order, hidden_in, norm_gain, weight):
    vmem = pl.BlockSpec(memory_space=pltpu.VMEM)
    hbm = pl.BlockSpec(memory_space=pl.ANY)
    dma = pltpu.SemaphoreType.DMA
    return pl.pallas_call(
        project_kernel,
        out_shape=(
            jax.ShapeDtypeStruct((SRC, ROWS, HD), BF16),
            jax.ShapeDtypeStruct((SRC, ROWS, 2 * HD), BF16),
        ),
        in_specs=[pl.BlockSpec(memory_space=pltpu.SMEM), vmem, vmem, hbm, vmem, vmem, vmem, vmem],
        out_specs=(hbm, hbm),
        scratch_shapes=[
            pltpu.VMEM((ROWS, D), BF16),
            pltpu.VMEM((ROWS, HD), F32),
            pltpu.VMEM((ROWS, HD), F32),
            pltpu.VMEM((3, D, 2 * HD), BF16),
            pltpu.VMEM((2, ROWS, HD), BF16),
            pltpu.VMEM((2, ROWS, 2 * HD), BF16),
            dma, dma((2, 6)), dma((2, 6)), dma((2,)), dma((2,)),
            dma((SRC,)), dma((SRC,)), dma((SRC,)), dma((SRC,)), dma((2,)),
        ],
        compiler_params=pltpu.CompilerParams(
            collective_id=0, has_side_effects=True, vmem_limit_bytes=60 << 20
        ),
        name="project",
    )(block_order, hidden_in, norm_gain, weight, *tables())


def attend_kernel(
    order, q_hbm, kv_hbm, w_hbm, out_ref,
    q_ref, kv_ref, w_ref, values, scores_a, scores_b, top_a, top_b, summed, qpos, kpos, o_mine, l_mine, parts, lses,
    ctx, terms, halves, fulls, mirrored,
    in_sem, o_send, o_recv, l_send, l_recv, h_send, h_recv, f_send, f_recv, z_send, z_recv,
):
    y, zl, c, x, zh = place()
    right = device(y, zl, c, (x + 1) % 4, zh)
    left = device(y, zl, c, (x + 3) % 4, zh)
    mirror = device(y, 3 - zl, c, x, 1 - zh)
    peers = [((zl + d) % 4, other_core(c, e)) for d, e in OTHERS]
    ids = [device(y, pz, pc, x, zh) for pz, pc in peers]
    mine = zl * 2 + c
    barrier = greet([right, left, mirror] + ids)
    loads = [
        pltpu.make_async_copy(src, dst, in_sem.at[i])
        for i, (src, dst) in enumerate(((q_hbm, q_ref), (kv_hbm, kv_ref), (w_hbm, w_ref)))
    ]
    for load in loads:
        load.start()

    lane = lax.broadcasted_iota(jnp.int32, (1, HD), 1)
    row = lax.broadcasted_iota(jnp.int32, (HB, HD), 0)
    for src in range(SRC):
        starts = [start_of(order, slot, src // 2, zl, src % 2, x, zh) for slot in range(SLOTS)]
        for u in range(SLOTS // 2):
            kpos[src * (SLOTS // 2) + u] = jnp.where(
                lane < HB, starts[2 * u] + lane, starts[2 * u + 1] + lane - HB
            )
        for slot in range(SLOTS):
            qpos[slot, src * HB : (src + 1) * HB, :] = row + start_of(
                order, slot, y, src // 2, src % 2, x, zh
            )
    diagonal = lax.broadcasted_iota(jnp.int32, (HD, HD), 0) == lax.broadcasted_iota(
        jnp.int32, (HD, HD), 1
    )
    per = TK // HD
    values[:, HD:] = jnp.ones((ALL, HD), BF16)
    for load in loads:
        load.wait()
    values[:, :HD] = kv_ref[:, HD:]
    pl.semaphore_wait(barrier, len(ids) + 3)

    def score_tile(t, j, scores, top):
        at = pl.ds(pl.multiple_of(t * HB, HB), HB)
        q = q_ref[:, at, :].reshape(TQ, HD)
        keys = kv_ref[pl.ds(pl.multiple_of(j * TK, TK), TK), 0:HD]
        s = lax.dot_general(q, keys, (((1,), (1,)), ((), ())), preferred_element_type=F32)
        best = top[...]
        for u in range(per):
            keep = kpos[j * per + u] <= qpos[t]
            kept = jnp.where(keep, s[:, u * HD : (u + 1) * HD], -1e30)
            scores[j * per + u] = kept
            best = jnp.maximum(best, kept)
        top[...] = best

    def weigh_tile(j, scores, top):
        best = top[...]
        weight = [jnp.exp2(scores[j * per + u] - best).astype(BF16) for u in range(per)]
        at = pl.ds(pl.multiple_of(j * TK, TK), TK)
        summed[...] += jnp.dot(
            jnp.concatenate(weight, axis=1), values[at, :], preferred_element_type=F32
        )

    def clear(top):
        top[...] = jnp.full((TQ, HD), -1e29, F32)

    def attend_chunk(t, scores, top, next_scores=None, next_top=None):
        top[...] = jnp.broadcast_to(jnp.max(top[...], axis=1, keepdims=True), (TQ, HD))
        summed[...] = jnp.zeros((TQ, 2 * HD), F32)
        if next_top is not None:
            clear(next_top)

        @pl.loop(0, ALL // TK)
        def _(j):
            if next_top is not None:
                score_tile(t + 1, j, next_scores, next_top)
            weigh_tile(j, scores, top)

        total = summed[:, HD:]
        some = total > 0
        total = jnp.where(some, total, 1.0)
        o_mine[t] = (summed[:, :HD] / total).astype(BF16).reshape(SRC, HB, HD)
        lse = jnp.where(some, top[...] + jnp.log2(total), -1e30)
        for u in range(SRC // 2):
            block = lse[u * HD : (u + 1) * HD, :]
            line = jnp.sum(jnp.where(diagonal, block, 0.0), axis=0, keepdims=True)
            l_mine[t, 2 * u, 0:1, :] = line
            l_mine[t, 2 * u + 1, 0:1, :] = pltpu.roll(line, HB, 1)
        parts[t, mine] = o_mine[t, mine]
        lses[t, mine] = l_mine[t, mine]
        for i, (pz, pc) in enumerate(peers):
            to = pz * 2 + pc
            remote(
                l_mine.at[t, to], lses.at[t, mine], l_send.at[i], l_recv.at[t, mine], ids[i]
            ).start()
            remote(
                o_mine.at[t, to], parts.at[t, mine], o_send.at[i], o_recv.at[t, mine], ids[i]
            ).start()

    def term(t):
        for i, (pz, pc) in enumerate(peers):
            src = pz * 2 + pc
            remote(
                l_mine.at[t, src], lses.at[t, src], l_send.at[i], l_recv.at[t, src], ids[i]
            ).wait_recv()
            remote(
                o_mine.at[t, src], parts.at[t, src], o_send.at[i], o_recv.at[t, src], ids[i]
            ).wait_recv()
        stats = jnp.concatenate([lses[t, src, 0:1, :] for src in range(SRC)], axis=0)
        stats = jnp.concatenate([stats] * (HD // SRC), axis=0).T
        for h in range(2):
            cols = [stats[0:HB, z * 2 + h : z * 2 + h + 1] for z in range(4)]
            best = jnp.maximum(jnp.maximum(cols[0], cols[1]), jnp.maximum(cols[2], cols[3]))
            shares = [jnp.exp2(col - best) for col in cols]
            total = shares[0] + shares[1] + shares[2] + shares[3]
            mixed = jnp.zeros((HB, HD), F32)
            for z in range(4):
                mixed += (shares[z] / total) * parts[t, z * 2 + h].astype(F32)
            ctx[:, h * HD : (h + 1) * HD] = mixed.astype(BF16)
        at = pl.ds(pl.multiple_of(t * HB, HB), HB)
        terms[at, :] = jnp.dot(ctx[...], w_ref[...], preferred_element_type=F32).astype(BF16)

    def cols(v):
        return pl.ds(v * (D // 2), D // 2)

    def at(slot, lo, v):
        return terms.at[pl.ds(slot * HB + lo, HALF), cols(v)]

    def far(p, slot, side, v):
        return remote(
            at(slot, side * HALF, v), halves.at[p, side, :, cols(v)],
            h_send.at[p, side, v], h_recv.at[p, side, v], left if side else right,
        )

    def near(p, slot, side, upper, v):
        return remote(
            at(slot, upper * HALF, v), fulls.at[p, side, pl.ds(upper * HALF, HALF), cols(v)],
            f_send.at[p, side, upper, v], f_recv.at[p, side, upper, v], left if side else right,
        )

    def over(upper, v):
        return remote(
            at(MIR, upper * HALF, v), mirrored.at[pl.ds(upper * HALF, HALF), cols(v)],
            z_send.at[upper, v], z_recv.at[upper, v], mirror,
        )

    fars, nears = (O0, O1), ((R0, L0), (R1, L1))

    def add(lo, v, *more):
        rows, columns = slice(lo, lo + HALF), slice(v * (D // 2), (v + 1) * (D // 2))
        total = terms[rows, columns].astype(F32)
        for ref in more:
            total = total + ref[:, columns].astype(F32)
        return total

    def store(lo, v, total):
        terms[lo : lo + HALF, v * (D // 2) : (v + 1) * (D // 2)] = total.astype(BF16)

    def send_far(p):
        for v in range(2):
            for side in range(2):
                far(p, fars[p], side, v).start()

    def send_near(p, side):
        slot = nears[p][side]
        lo = slot * HB + side * HALF
        for v in range(2):
            near(p, slot, side, 1 - side, v).start()
            far(p, fars[p], side, v).wait_recv()
            store(lo, v, add(lo, v, halves.at[p, side]))
            near(p, slot, side, side, v).start()

    def send_over(v):
        for upper in range(2):
            for side in range(2):
                near(1, nears[1][side], side, upper, v).wait_recv()
            lo = MIR * HB + upper * HALF
            rows = pl.ds(upper * HALF, HALF)
            store(lo, v, add(lo, v, fulls.at[1, 0, rows], fulls.at[1, 1, rows]))
            over(upper, v).start()

    def ring(t):
        pl.when(t > 0)(lambda: term(t - 1))

        @pl.when(t == O1 + 1)
        def _():
            send_far(1)

        @pl.when(t == L1 + 1)
        def _():
            send_near(1, 1)

        @pl.when(t == R1 + 1)
        def _():
            send_near(1, 0)

        @pl.when(t == O0 + 1)
        def _():
            send_far(0)
            send_over(0)

        @pl.when(t == L0 + 1)
        def _():
            send_over(1)
            send_near(0, 1)

    clear(top_a)
    pl.loop(0, ALL // TK)(lambda j: score_tile(0, j, scores_a, top_a))

    @pl.loop(0, SLOTS // 2 - 1)
    def _(i):
        attend_chunk(2 * i, scores_a, top_a, scores_b, top_b)
        ring(2 * i)
        attend_chunk(2 * i + 1, scores_b, top_b, scores_a, top_a)
        ring(2 * i + 1)

    attend_chunk(SLOTS - 2, scores_a, top_a, scores_b, top_b)
    ring(SLOTS - 2)
    attend_chunk(SLOTS - 1, scores_b, top_b)
    term(R0)
    send_near(0, 0)
    term(OWN)
    for v in range(2):
        for upper in range(2):
            for side in range(2):
                near(0, nears[0][side], side, upper, v).wait_recv()
            over(upper, v).wait_recv()
            rows = pl.ds(upper * HALF, HALF)
            total = add(
                OWN * HB + upper * HALF, v, fulls.at[0, 0, rows], fulls.at[0, 1, rows], mirrored.at[rows]
            )
            out_ref[rows, v * (D // 2) : (v + 1) * (D // 2)] = total.astype(BF16)
    for v in range(2):
        for p in range(2):
            for side in range(2):
                far(p, fars[p], side, v).wait_send()
                for upper in range(2):
                    near(p, nears[p][side], side, upper, v).wait_send()
        for upper in range(2):
            over(upper, v).wait_send()
    for i, (pz, pc) in enumerate(peers):
        src = pz * 2 + pc
        remote(l_mine.at[:, src], lses.at[:, src], l_send.at[i], l_recv.at[0, src], ids[i]).wait_send()
        remote(o_mine.at[:, src], parts.at[:, src], o_send.at[i], o_recv.at[0, src], ids[i]).wait_send()


def attend(block_order, q, kv, out_weight):
    vmem = pl.BlockSpec(memory_space=pltpu.VMEM)
    hbm = pl.BlockSpec(memory_space=pl.ANY)
    dma = pltpu.SemaphoreType.DMA
    return pl.pallas_call(
        attend_kernel,
        out_shape=jax.ShapeDtypeStruct((HB, D), BF16),
        in_specs=[pl.BlockSpec(memory_space=pltpu.SMEM), hbm, hbm, hbm],
        out_specs=vmem,
        scratch_shapes=[
            pltpu.VMEM((SRC, ROWS, HD), BF16),
            pltpu.VMEM((ALL, 2 * HD), BF16),
            pltpu.VMEM((2 * HD, D), BF16),
            pltpu.VMEM((ALL, 2 * HD), BF16),
            pltpu.VMEM((ALL // HD, TQ, HD), F32),
            pltpu.VMEM((ALL // HD, TQ, HD), F32),
            pltpu.VMEM((TQ, HD), F32),
            pltpu.VMEM((TQ, HD), F32),
            pltpu.VMEM((TQ, 2 * HD), F32),
            pltpu.VMEM((SLOTS, TQ, HD), jnp.int32),
            pltpu.VMEM((ALL // HD, 1, HD), jnp.int32),
            pltpu.VMEM((SLOTS, SRC, HB, HD), BF16),
            pltpu.VMEM((SLOTS, SRC, 8, HD), F32),
            pltpu.VMEM((SLOTS, SRC, HB, HD), BF16),
            pltpu.VMEM((SLOTS, SRC, 8, HD), F32),
            pltpu.VMEM((HB, 2 * HD), BF16),
            pltpu.VMEM((ROWS, D), BF16),
            pltpu.VMEM((2, 2, HALF, D), BF16),
            pltpu.VMEM((2, 2, HB, D), BF16),
            pltpu.VMEM((HB, D), BF16),
            dma((3,)),
            dma((SRC,)), dma((SLOTS, SRC)), dma((SRC,)), dma((SLOTS, SRC)),
            dma((2, 2, 2)), dma((2, 2, 2)), dma((2, 2, 2, 2)), dma((2, 2, 2, 2)),
            dma((2, 2)), dma((2, 2)),
        ],
        compiler_params=pltpu.CompilerParams(
            collective_id=1, has_side_effects=True, vmem_limit_bytes=56 << 20
        ),
        name="attend",
    )(block_order, q, kv.reshape(ALL, 2 * HD), out_weight)


def local(hidden_in, norm_gain, qkv_weight, out_weight, block_order):
    weight = jnp.transpose(qkv_weight, (1, 0, 2))
    q, kv = project(block_order, hidden_in, norm_gain[None, :], weight)
    return attend(block_order, q, kv, out_weight)


def solution(mesh):
    in_specs = (P(("seq", "tp"), None), P(), P(None, None, "tp"), P("tp", None), P())
    out_specs = P(("seq", "tp"), None)
    return jax.shard_map(local, mesh=mesh, in_specs=in_specs, out_specs=out_specs, check_vma=False)
```

```python
import math

import jax
import jax.numpy as jnp
import numpy as np
from jax import lax
from jax.experimental import pallas as pl
from jax.experimental.pallas import tpu as pltpu
from jax.sharding import PartitionSpec as P

HD = 128
BLK = 128
D = 4096
SEQ = 16384
HB = 64
SLOTS = 8
ROWS = HB * SLOTS
SRC = 8
ALL = SRC * ROWS
HALF = HB // 2
TQ = SRC * HB
MESH = pl.DeviceIdType.MESH
F32 = jnp.float32
BF16 = jnp.bfloat16

O1, L1, R1, MIR, O0, L0, R0, OWN = range(8)
CHUNKS = ((1, 2), (1, -1), (1, 1), (1, 0), (0, 2), (0, -1), (0, 1), (0, 0))
SCALE = math.log2(math.e) / HD**0.5
OTHERS = [(d, e) for d in range(4) for e in range(2)][1:]


def place():
    s = lax.axis_index("seq")
    t = lax.axis_index("tp")
    return s // 8, (s // 2) % 4, s % 2, t // 2, t % 2


def device(y, zl, c, x, zh):
    return ((y * 4 + zl) * 2 + c, x * 2 + zh)


def other_core(c, e):
    return 1 - c if e else c


def start_of(order, slot, y, zl, c, x, zh):
    mirrored, shift = CHUNKS[slot]
    if mirrored:
        zl, zh = 3 - zl, 1 - zh
    block = ((y * 4 + zl) * 2 + c) * (ROWS // BLK) + (x + shift + 4) % 4
    return order[block] * BLK + zh * HB


def tables():
    frequency = 10000.0 ** (-(np.arange(HD) % (HD // 2)) * 2.0 / HD)
    starts = np.arange(SEQ // HB)[:, None] * float(HB) * frequency[None, :]
    rows = np.arange(HB)[:, None] * frequency[None, :]
    made = [np.cos(starts), np.sin(starts), np.cos(rows), np.sin(rows)]
    return [jnp.asarray(t.astype(np.float32)) for t in made]


def greet(peers):
    barrier = pltpu.get_barrier_semaphore()
    for peer in peers:
        pl.semaphore_signal(barrier, inc=1, device_id=peer, device_id_type=MESH)
    return barrier


def remote(src, dst, send, recv, peer):
    return pltpu.make_async_remote_copy(
        src_ref=src, dst_ref=dst, send_sem=send, recv_sem=recv, device_id=peer, device_id_type=MESH
    )


def sublayer_kernel(
    order, hid, gain, w_hbm, wo_hbm, cos_start, sin_start, cos_row, sin_row, out_ref,
    rows, cos, sin, wv, qs, kvs, q_ref, kv_ref, w_ref, values, scores_a, scores_b,
    top_a, top_b, summed, qpos, kpos, o_mine, l_mine, parts, lses, ctx, halves, fulls, mirrored,
    w_sem, wo_sem, x_send, x_recv, m_send, m_recv, kv_send, kv_recv, q_send, q_recv,
    o_send, o_recv, l_send, l_recv, h_send, h_recv, f_send, f_recv, z_send, z_recv,
):
    y, zl, c, x, zh = place()
    right = device(y, zl, c, (x + 1) % 4, zh)
    left = device(y, zl, c, (x + 3) % 4, zh)
    mirror = device(y, 3 - zl, c, x, 1 - zh)
    kv_peers = [((y + d) % 4, other_core(c, e)) for d, e in OTHERS]
    q_peers = [((zl + d) % 4, other_core(c, e)) for d, e in OTHERS]
    kv_ids = [device(py, zl, pc, x, zh) for py, pc in kv_peers]
    q_ids = [device(y, pz, pc, x, zh) for pz, pc in q_peers]
    peers = [right, left, mirror] + kv_ids + q_ids[1:]
    barrier = greet(peers)
    w_copy = pltpu.make_async_copy(w_hbm, wv, w_sem)
    w_copy.start()
    wo_copy = pltpu.make_async_copy(wo_hbm, w_ref, wo_sem)
    wo_copy.start()

    floats = hid[...].astype(F32)
    scale = lax.rsqrt(jnp.mean(floats * floats, axis=-1, keepdims=True) + 1e-05)
    rows[OWN * HB : (OWN + 1) * HB, :] = (floats * scale * gain[...]).astype(BF16)
    first_half = lax.broadcasted_iota(jnp.int32, (1, HD), 1) < HD // 2
    for slot in range(SLOTS):
        start = start_of(order, slot, y, zl, c, x, zh) // HB
        cs, sn = cos_start[pl.ds(start, 1), :], sin_start[pl.ds(start, 1), :]
        lo, hi = slot * HB, (slot + 1) * HB
        cos[lo:hi, :] = cs * cos_row[...] - sn * sin_row[...]
        sine = sn * cos_row[...] + cs * sin_row[...]
        sin[lo:hi, :] = jnp.where(first_half, -sine, sine)
    pl.semaphore_wait(barrier, len(peers))

    def at(slot, lo=0, hi=HB):
        return rows.at[pl.ds(slot * HB + lo, hi - lo), :]

    def step(p, kind, src, dst, lo, hi, peer):
        return remote(at(src, lo, hi), at(dst, lo, hi), x_send.at[p, kind], x_recv.at[p, kind], peer)

    def spread(p, src, from_left, from_right, far):
        return (
            step(p, 0, src, from_left, 0, HALF, right),
            step(p, 1, src, from_right, HALF, HB, left),
            step(p, 2, src, from_left, HALF, HB, right),
            step(p, 3, src, from_right, 0, HALF, left),
            step(p, 4, from_left, far, 0, HALF, right),
            step(p, 5, from_right, far, HALF, HB, left),
        )

    mirror_lo = remote(at(OWN, 0, HALF), at(MIR, 0, HALF), m_send.at[0], m_recv.at[0], mirror)
    mirror_hi = remote(at(OWN, HALF, HB), at(MIR, HALF, HB), m_send.at[1], m_recv.at[1], mirror)
    own = spread(0, OWN, L0, R0, O0)
    mir = spread(1, MIR, L1, R1, O1)

    mirror_lo.start()
    mirror_hi.start()
    for copy in own[:4]:
        copy.start()
    mine = y * 2 + c
    mine_q = zl * 2 + c

    def part(ref, lo, hi, *index):
        return ref.at[(*index, pl.ds(lo, hi - lo), slice(None))]

    def work(first, last):
        lo, hi = first * HB, last * HB
        chunk = rows[lo:hi, :]
        cs, sn = cos[lo:hi, :], sin[lo:hi, :]
        q = jnp.dot(chunk, wv[0], preferred_element_type=F32)
        k = jnp.dot(chunk, wv[1], preferred_element_type=F32)
        v = jnp.dot(chunk, wv[2], preferred_element_type=F32)
        for h in range(2):
            lane = slice(h * HD, (h + 1) * HD)
            for out, by, t in ((qs, SCALE, q[:, lane]), (kvs, 1.0, k[:, lane])):
                turned = t * cs + pltpu.roll(t, HD // 2, 1) * sn
                out[h, lo:hi, 0:HD] = (turned * by).astype(BF16)
            kvs[h, lo:hi, HD : 2 * HD] = v[:, lane].astype(BF16)
        for i, (py, pc) in enumerate(kv_peers):
            remote(
                part(kvs, lo, hi, pc), part(kv_ref, lo, hi, mine),
                kv_send.at[i], kv_recv.at[mine], kv_ids[i],
            ).start()
        kv_ref[mine, lo:hi, :] = kvs[c, lo:hi, :]
        q_ref[mine_q, lo:hi, :] = qs[c, lo:hi, :]
        for i, (pz, pc) in enumerate(q_peers):
            remote(
                part(qs, lo, hi, pc), part(q_ref, lo, hi, mine_q),
                q_send.at[i], q_recv.at[mine_q], q_ids[i],
            ).start()

    w_copy.wait()
    work(OWN, OWN + 1)
    own[0].wait_recv()
    own[4].start()
    own[1].wait_recv()
    own[5].start()
    own[2].wait_recv()
    own[3].wait_recv()
    work(L0, R0 + 1)
    mirror_lo.wait_recv()
    mir[0].start()
    mir[3].start()
    own[4].wait_recv()
    own[5].wait_recv()
    work(O0, O0 + 1)
    mirror_hi.wait_recv()
    mir[1].start()
    mir[2].start()
    work(MIR, MIR + 1)
    mir[0].wait_recv()
    mir[4].start()
    mir[1].wait_recv()
    mir[5].start()
    mir[2].wait_recv()
    mir[3].wait_recv()
    work(L1, R1 + 1)
    mir[4].wait_recv()
    mir[5].wait_recv()
    work(O1, O1 + 1)
    lane = lax.broadcasted_iota(jnp.int32, (1, HD), 1)
    row = lax.broadcasted_iota(jnp.int32, (HB, HD), 0)
    for src in range(SRC):
        starts = [start_of(order, slot, src // 2, zl, src % 2, x, zh) for slot in range(SLOTS)]
        for u in range(SLOTS // 2):
            kpos[src * (SLOTS // 2) + u] = jnp.where(
                lane < HB, starts[2 * u] + lane, starts[2 * u + 1] + lane - HB
            )
        for slot in range(SLOTS):
            qpos[slot, src * HB : (src + 1) * HB, :] = row + start_of(
                order, slot, y, src // 2, src % 2, x, zh
            )
    diagonal = lax.broadcasted_iota(jnp.int32, (HD, HD), 0) == lax.broadcasted_iota(
        jnp.int32, (HD, HD), 1
    )
    per = ALL // HD
    values[:, HD:] = jnp.ones((ALL, HD), BF16)
    for copy in (mirror_lo, mirror_hi, *own, *mir):
        copy.wait_send()
    wo_copy.wait()
    for i, (py, pc) in enumerate(kv_peers):
        src = py * 2 + pc
        remote(kvs.at[pc], kv_ref.at[src], kv_send.at[i], kv_recv.at[src], kv_ids[i]).wait()
    for i, (pz, pc) in enumerate(q_peers):
        src = pz * 2 + pc
        remote(qs.at[pc], q_ref.at[src], q_send.at[i], q_recv.at[src], q_ids[i]).wait()
    values[:, :HD] = kv_ref[:, :, HD:].reshape(ALL, HD)
    peers, ids, mine = q_peers, q_ids, mine_q
    terms = rows

    def score_chunk(t, scores, top):
        at = pl.ds(pl.multiple_of(t * HB, HB), HB)
        q = q_ref[:, at, :].reshape(TQ, HD)
        keys = kv_ref[:, :, 0:HD].reshape(ALL, HD)
        s = lax.dot_general(q, keys, (((1,), (1,)), ((), ())), preferred_element_type=F32)
        best = top[...]
        for u in range(per):
            keep = kpos[u] <= qpos[t]
            kept = jnp.where(keep, s[:, u * HD : (u + 1) * HD], -1e30)
            scores[u] = kept
            best = jnp.maximum(best, kept)
        top[...] = best

    def weigh_chunk(scores, top):
        best = top[...]
        weight = [jnp.exp2(scores[u] - best).astype(BF16) for u in range(per)]
        summed[...] = jnp.dot(
            jnp.concatenate(weight, axis=1), values[...], preferred_element_type=F32
        )

    def clear(top):
        top[...] = jnp.full((TQ, HD), -1e29, F32)

    def attend_chunk(t, scores, top, next_scores=None, next_top=None):
        top[...] = jnp.broadcast_to(jnp.max(top[...], axis=1, keepdims=True), (TQ, HD))
        if next_top is not None:
            clear(next_top)
            score_chunk(t + 1, next_scores, next_top)
        weigh_chunk(scores, top)

        total = summed[:, HD:]
        some = total > 0
        total = jnp.where(some, total, 1.0)
        o_mine[t] = (summed[:, :HD] / total).astype(BF16).reshape(SRC, HB, HD)
        lse = jnp.where(some, top[...] + jnp.log2(total), -1e30)
        for u in range(SRC // 2):
            block = lse[u * HD : (u + 1) * HD, :]
            line = jnp.sum(jnp.where(diagonal, block, 0.0), axis=0, keepdims=True)
            l_mine[t, 2 * u] = line
            l_mine[t, 2 * u + 1] = pltpu.roll(line, HB, 1)
        parts[t, mine] = o_mine[t, mine]
        lses[t, mine] = l_mine[t, mine]
        for i, (pz, pc) in enumerate(peers):
            to = pz * 2 + pc
            remote(
                l_mine.at[t, to], lses.at[t, mine], l_send.at[i], l_recv.at[t, mine], ids[i]
            ).start()
            remote(
                o_mine.at[t, to], parts.at[t, mine], o_send.at[i], o_recv.at[t, mine], ids[i]
            ).start()

    def term(t):
        for i, (pz, pc) in enumerate(peers):
            src = pz * 2 + pc
            remote(
                l_mine.at[t, src], lses.at[t, src], l_send.at[i], l_recv.at[t, src], ids[i]
            ).wait_recv()
            remote(
                o_mine.at[t, src], parts.at[t, src], o_send.at[i], o_recv.at[t, src], ids[i]
            ).wait_recv()
        shares = []
        for h in range(2):
            lse = [lses[t, z * 2 + h] for z in range(4)]
            best = jnp.maximum(jnp.maximum(lse[0], lse[1]), jnp.maximum(lse[2], lse[3]))
            share = [jnp.exp2(line - best) for line in lse]
            total = share[0] + share[1] + share[2] + share[3]
            shares += [line / total for line in share]
        turned = jnp.concatenate(shares * (HD // SRC), axis=0).T
        for h in range(2):
            mixed = jnp.zeros((HB, HD), F32)
            for z in range(4):
                share = turned[0:HB, h * 4 + z : h * 4 + z + 1]
                mixed += share * parts[t, z * 2 + h].astype(F32)
            ctx[:, h * HD : (h + 1) * HD] = mixed.astype(BF16)
        at = pl.ds(pl.multiple_of(t * HB, HB), HB)
        terms[at, :] = jnp.dot(ctx[...], w_ref[...], preferred_element_type=F32).astype(BF16)

    def cols(v):
        return pl.ds(v * (D // 2), D // 2)

    def cut(slot, lo, v):
        return terms.at[pl.ds(slot * HB + lo, HALF), cols(v)]

    def far(p, slot, side, v):
        return remote(
            cut(slot, side * HALF, v), halves.at[p, side, :, cols(v)],
            h_send.at[p, side, v], h_recv.at[p, side, v], left if side else right,
        )

    def near(p, slot, side, upper, v):
        return remote(
            cut(slot, upper * HALF, v), fulls.at[p, side, pl.ds(upper * HALF, HALF), cols(v)],
            f_send.at[p, side, upper, v], f_recv.at[p, side, upper, v], left if side else right,
        )

    def over(upper, v):
        return remote(
            cut(MIR, upper * HALF, v), mirrored.at[pl.ds(upper * HALF, HALF), cols(v)],
            z_send.at[upper, v], z_recv.at[upper, v], mirror,
        )

    fars, nears = (O0, O1), ((R0, L0), (R1, L1))

    def add(lo, v, *more):
        rows, columns = slice(lo, lo + HALF), slice(v * (D // 2), (v + 1) * (D // 2))
        total = terms[rows, columns].astype(F32)
        for ref in more:
            total = total + ref[:, columns].astype(F32)
        return total

    def store(lo, v, total):
        terms[lo : lo + HALF, v * (D // 2) : (v + 1) * (D // 2)] = total.astype(BF16)

    def send_far(p):
        for v in range(2):
            for side in range(2):
                far(p, fars[p], side, v).start()

    def send_near(p, side):
        slot = nears[p][side]
        lo = slot * HB + side * HALF
        for v in range(2):
            near(p, slot, side, 1 - side, v).start()
            far(p, fars[p], side, v).wait_recv()
            store(lo, v, add(lo, v, halves.at[p, side]))
            near(p, slot, side, side, v).start()

    def send_over(v):
        for upper in range(2):
            for side in range(2):
                near(1, nears[1][side], side, upper, v).wait_recv()
            lo = MIR * HB + upper * HALF
            rows = pl.ds(upper * HALF, HALF)
            store(lo, v, add(lo, v, fulls.at[1, 0, rows], fulls.at[1, 1, rows]))
            over(upper, v).start()

    def ring(t):
        pl.when(t > 0)(lambda: term(t - 1))

        @pl.when(t == O1 + 1)
        def _():
            send_far(1)

        @pl.when(t == L1 + 1)
        def _():
            send_near(1, 1)

        @pl.when(t == R1 + 1)
        def _():
            send_near(1, 0)

        @pl.when(t == MIR + 1)
        def _():
            send_over(0)

        @pl.when(t == O0 + 1)
        def _():
            send_far(0)
            send_over(1)

        @pl.when(t == L0 + 1)
        def _():
            send_near(0, 1)

    clear(top_a)
    score_chunk(0, scores_a, top_a)

    @pl.loop(0, SLOTS // 2 - 1)
    def _(i):
        attend_chunk(2 * i, scores_a, top_a, scores_b, top_b)
        ring(2 * i)
        attend_chunk(2 * i + 1, scores_b, top_b, scores_a, top_a)
        ring(2 * i + 1)

    attend_chunk(SLOTS - 2, scores_a, top_a, scores_b, top_b)
    ring(SLOTS - 2)
    attend_chunk(SLOTS - 1, scores_b, top_b)
    term(R0)
    send_near(0, 0)
    term(OWN)
    for v in range(2):
        for upper in range(2):
            for side in range(2):
                near(0, nears[0][side], side, upper, v).wait_recv()
            over(upper, v).wait_recv()
            rows = pl.ds(upper * HALF, HALF)
            total = add(
                OWN * HB + upper * HALF, v, fulls.at[0, 0, rows], fulls.at[0, 1, rows], mirrored.at[rows]
            )
            out_ref[rows, v * (D // 2) : (v + 1) * (D // 2)] = total.astype(BF16)
    for v in range(2):
        for p in range(2):
            for side in range(2):
                far(p, fars[p], side, v).wait_send()
                for upper in range(2):
                    near(p, nears[p][side], side, upper, v).wait_send()
        for upper in range(2):
            over(upper, v).wait_send()
    for i, (pz, pc) in enumerate(peers):
        src = pz * 2 + pc
        remote(l_mine.at[:, src], lses.at[:, src], l_send.at[i], l_recv.at[0, src], ids[i]).wait_send()
        remote(o_mine.at[:, src], parts.at[:, src], o_send.at[i], o_recv.at[0, src], ids[i]).wait_send()


def sublayer(block_order, hidden_in, norm_gain, weight, out_weight):
    smem = pl.BlockSpec(memory_space=pltpu.SMEM)
    vmem = pl.BlockSpec(memory_space=pltpu.VMEM)
    hbm = pl.BlockSpec(memory_space=pl.ANY)
    dma = pltpu.SemaphoreType.DMA
    return pl.pallas_call(
        sublayer_kernel,
        out_shape=jax.ShapeDtypeStruct((HB, D), BF16),
        in_specs=[smem, vmem, vmem, hbm, hbm, vmem, vmem, vmem, vmem],
        out_specs=vmem,
        scratch_shapes=[
            pltpu.VMEM((ROWS, D), BF16),
            pltpu.VMEM((ROWS, HD), F32),
            pltpu.VMEM((ROWS, HD), F32),
            pltpu.VMEM((3, D, 2 * HD), BF16),
            pltpu.VMEM((2, ROWS, HD), BF16),
            pltpu.VMEM((2, ROWS, 2 * HD), BF16),
            pltpu.VMEM((SRC, ROWS, HD), BF16),
            pltpu.VMEM((SRC, ROWS, 2 * HD), BF16),
            pltpu.VMEM((2 * HD, D), BF16),
            pltpu.VMEM((ALL, 2 * HD), BF16),
            pltpu.VMEM((ALL // HD, TQ, HD), F32),
            pltpu.VMEM((ALL // HD, TQ, HD), F32),
            pltpu.VMEM((TQ, HD), F32),
            pltpu.VMEM((TQ, HD), F32),
            pltpu.VMEM((TQ, 2 * HD), F32),
            pltpu.VMEM((SLOTS, TQ, HD), jnp.int32),
            pltpu.VMEM((ALL // HD, 1, HD), jnp.int32),
            pltpu.VMEM((SLOTS, SRC, HB, HD), BF16),
            pltpu.VMEM((SLOTS, SRC, 1, HD), F32),
            pltpu.VMEM((SLOTS, SRC, HB, HD), BF16),
            pltpu.VMEM((SLOTS, SRC, 1, HD), F32),
            pltpu.VMEM((HB, 2 * HD), BF16),
            pltpu.VMEM((2, 2, HALF, D), BF16),
            pltpu.VMEM((2, 2, HB, D), BF16),
            pltpu.VMEM((HB, D), BF16),
            dma, dma, dma((2, 6)), dma((2, 6)), dma((2,)), dma((2,)),
            dma((SRC,)), dma((SRC,)), dma((SRC,)), dma((SRC,)),
            dma((SRC,)), dma((SLOTS, SRC)), dma((SRC,)), dma((SLOTS, SRC)),
            dma((2, 2, 2)), dma((2, 2, 2)), dma((2, 2, 2, 2)), dma((2, 2, 2, 2)),
            dma((2, 2)), dma((2, 2)),
        ],
        compiler_params=pltpu.CompilerParams(
            collective_id=0, has_side_effects=True, vmem_limit_bytes=60 << 20
        ),
        name="sublayer",
    )(block_order, hidden_in, norm_gain, weight, out_weight, *tables())


def local(hidden_in, norm_gain, qkv_weight, out_weight, block_order):
    weight = jnp.transpose(qkv_weight, (1, 0, 2))
    return sublayer(block_order, hidden_in, norm_gain[None, :], weight, out_weight)


def solution(mesh):
    in_specs = (P(("seq", "tp"), None), P(), P(None, None, "tp"), P("tp", None), P())
    out_specs = P(("seq", "tp"), None)
    return jax.shard_map(local, mesh=mesh, in_specs=in_specs, out_specs=out_specs, check_vma=False)
```

```python
import math

import jax
import jax.numpy as jnp
import numpy as np
from jax import lax
from jax.experimental import pallas as pl
from jax.experimental.pallas import tpu as pltpu
from jax.sharding import PartitionSpec as P

HD = 128
BLK = 128
D = 4096
SEQ = 16384
HB = 64
SLOTS = 8
ROWS = HB * SLOTS
SRC = 8
ALL = SRC * ROWS
HALF = HB // 2
CUTS = 4
WIDTH = D // CUTS
TQ = SRC * HB
MESH = pl.DeviceIdType.MESH
F32 = jnp.float32
BF16 = jnp.bfloat16

O1, L1, R1, MIR, O0, L0, R0, OWN = range(8)
CHUNKS = ((1, 2), (1, -1), (1, 1), (1, 0), (0, 2), (0, -1), (0, 1), (0, 0))
SCALE = math.log2(math.e) / HD**0.5
OTHERS = [(d, e) for d in range(4) for e in range(2)][1:]


def place():
    s = lax.axis_index("seq")
    t = lax.axis_index("tp")
    return s // 8, (s // 2) % 4, s % 2, t // 2, t % 2


def device(y, zl, c, x, zh):
    return ((y * 4 + zl) * 2 + c, x * 2 + zh)


def other_core(c, e):
    return 1 - c if e else c


def start_of(order, slot, y, zl, c, x, zh):
    mirrored, shift = CHUNKS[slot]
    if mirrored:
        zl, zh = 3 - zl, 1 - zh
    block = ((y * 4 + zl) * 2 + c) * (ROWS // BLK) + (x + shift + 4) % 4
    return order[block] * BLK + zh * HB


def tables():
    frequency = 10000.0 ** (-(np.arange(HD) % (HD // 2)) * 2.0 / HD)
    starts = np.arange(SEQ // HB)[:, None] * float(HB) * frequency[None, :]
    rows = np.arange(HB)[:, None] * frequency[None, :]
    made = [np.cos(starts), np.sin(starts), np.cos(rows), np.sin(rows)]
    return [jnp.asarray(t.astype(np.float32)) for t in made]


def greet(peers):
    barrier = pltpu.get_barrier_semaphore()
    for peer in peers:
        pl.semaphore_signal(barrier, inc=1, device_id=peer, device_id_type=MESH)
    return barrier


def remote(src, dst, send, recv, peer):
    return pltpu.make_async_remote_copy(
        src_ref=src, dst_ref=dst, send_sem=send, recv_sem=recv, device_id=peer, device_id_type=MESH
    )


def sublayer_kernel(
    order, hid, gain, w_hbm, wo_hbm, cos_start, sin_start, cos_row, sin_row, out_ref,
    rows, cos, sin, wv, qs, kvs, q_ref, kv_ref, w_ref, values, scores_a, scores_b,
    top_a, top_b, summed, qpos, kpos, o_mine, l_mine, parts, lses, ctx, halves, fulls, mirrored,
    w_sem, wo_sem, x_send, x_recv, m_send, m_recv, kv_send, kv_recv, q_send, q_recv,
    o_send, o_recv, l_send, l_recv, h_send, h_recv, f_send, f_recv, z_send, z_recv,
):
    y, zl, c, x, zh = place()
    right = device(y, zl, c, (x + 1) % 4, zh)
    left = device(y, zl, c, (x + 3) % 4, zh)
    mirror = device(y, 3 - zl, c, x, 1 - zh)
    kv_peers = [((y + d) % 4, other_core(c, e)) for d, e in OTHERS]
    q_peers = [((zl + d) % 4, other_core(c, e)) for d, e in OTHERS]
    kv_ids = [device(py, zl, pc, x, zh) for py, pc in kv_peers]
    q_ids = [device(y, pz, pc, x, zh) for pz, pc in q_peers]
    peers = [right, left, mirror] + kv_ids + q_ids[1:]
    barrier = greet(peers)
    w_copy = pltpu.make_async_copy(w_hbm, wv, w_sem)
    w_copy.start()
    wo_copy = pltpu.make_async_copy(wo_hbm, w_ref, wo_sem)
    wo_copy.start()

    floats = hid[...].astype(F32)
    scale = lax.rsqrt(jnp.mean(floats * floats, axis=-1, keepdims=True) + 1e-05)
    rows[OWN * HB : (OWN + 1) * HB, :] = (floats * scale * gain[...]).astype(BF16)
    first_half = lax.broadcasted_iota(jnp.int32, (1, HD), 1) < HD // 2
    for slot in range(SLOTS):
        start = start_of(order, slot, y, zl, c, x, zh) // HB
        cs, sn = cos_start[pl.ds(start, 1), :], sin_start[pl.ds(start, 1), :]
        lo, hi = slot * HB, (slot + 1) * HB
        cos[lo:hi, :] = cs * cos_row[...] - sn * sin_row[...]
        sine = sn * cos_row[...] + cs * sin_row[...]
        sin[lo:hi, :] = jnp.where(first_half, -sine, sine)
    pl.semaphore_wait(barrier, len(peers))

    def at(slot, lo=0, hi=HB):
        return rows.at[pl.ds(slot * HB + lo, hi - lo), :]

    def step(p, kind, src, dst, lo, hi, peer):
        return remote(at(src, lo, hi), at(dst, lo, hi), x_send.at[p, kind], x_recv.at[p, kind], peer)

    def spread(p, src, from_left, from_right, far):
        return (
            step(p, 0, src, from_left, 0, HALF, right),
            step(p, 1, src, from_right, HALF, HB, left),
            step(p, 2, src, from_left, HALF, HB, right),
            step(p, 3, src, from_right, 0, HALF, left),
            step(p, 4, from_left, far, 0, HALF, right),
            step(p, 5, from_right, far, HALF, HB, left),
        )

    mirror_lo = remote(at(OWN, 0, HALF), at(MIR, 0, HALF), m_send.at[0], m_recv.at[0], mirror)
    mirror_hi = remote(at(OWN, HALF, HB), at(MIR, HALF, HB), m_send.at[1], m_recv.at[1], mirror)
    own = spread(0, OWN, L0, R0, O0)
    mir = spread(1, MIR, L1, R1, O1)

    mirror_lo.start()
    mirror_hi.start()
    for copy in own[:4]:
        copy.start()
    mine = y * 2 + c
    mine_q = zl * 2 + c

    def part(ref, lo, hi, *index):
        return ref.at[(*index, pl.ds(lo, hi - lo), slice(None))]

    def work(first, last):
        lo, hi = first * HB, last * HB
        chunk = rows[lo:hi, :]
        cs, sn = cos[lo:hi, :], sin[lo:hi, :]
        q = jnp.dot(chunk, wv[0], preferred_element_type=F32)
        k = jnp.dot(chunk, wv[1], preferred_element_type=F32)
        v = jnp.dot(chunk, wv[2], preferred_element_type=F32)
        for h in range(2):
            lane = slice(h * HD, (h + 1) * HD)
            for out, by, t in ((qs, SCALE, q[:, lane]), (kvs, 1.0, k[:, lane])):
                turned = t * cs + pltpu.roll(t, HD // 2, 1) * sn
                out[h, lo:hi, 0:HD] = (turned * by).astype(BF16)
            kvs[h, lo:hi, HD : 2 * HD] = v[:, lane].astype(BF16)
        for i, (py, pc) in enumerate(kv_peers):
            remote(
                part(kvs, lo, hi, pc), part(kv_ref, lo, hi, mine),
                kv_send.at[i], kv_recv.at[mine], kv_ids[i],
            ).start()
        kv_ref[mine, lo:hi, :] = kvs[c, lo:hi, :]
        q_ref[mine_q, lo:hi, :] = qs[c, lo:hi, :]
        for i, (pz, pc) in enumerate(q_peers):
            remote(
                part(qs, lo, hi, pc), part(q_ref, lo, hi, mine_q),
                q_send.at[i], q_recv.at[mine_q], q_ids[i],
            ).start()

    w_copy.wait()
    work(OWN, OWN + 1)
    own[0].wait_recv()
    own[4].start()
    own[1].wait_recv()
    own[5].start()
    own[2].wait_recv()
    own[3].wait_recv()
    work(L0, R0 + 1)
    mirror_lo.wait_recv()
    mir[0].start()
    mir[3].start()
    own[4].wait_recv()
    own[5].wait_recv()
    work(O0, O0 + 1)
    mirror_hi.wait_recv()
    mir[1].start()
    mir[2].start()
    work(MIR, MIR + 1)
    mir[0].wait_recv()
    mir[4].start()
    mir[1].wait_recv()
    mir[5].start()
    mir[2].wait_recv()
    mir[3].wait_recv()
    work(L1, R1 + 1)
    mir[4].wait_recv()
    mir[5].wait_recv()
    work(O1, O1 + 1)
    lane = lax.broadcasted_iota(jnp.int32, (1, HD), 1)
    row = lax.broadcasted_iota(jnp.int32, (HB, HD), 0)
    for src in range(SRC):
        starts = [start_of(order, slot, src // 2, zl, src % 2, x, zh) for slot in range(SLOTS)]
        for u in range(SLOTS // 2):
            kpos[src * (SLOTS // 2) + u] = jnp.where(
                lane < HB, starts[2 * u] + lane, starts[2 * u + 1] + lane - HB
            )
        for slot in range(SLOTS):
            qpos[slot, src * HB : (src + 1) * HB, :] = row + start_of(
                order, slot, y, src // 2, src % 2, x, zh
            )
    diagonal = lax.broadcasted_iota(jnp.int32, (HD, HD), 0) == lax.broadcasted_iota(
        jnp.int32, (HD, HD), 1
    )
    per = ALL // HD
    values[:, HD:] = jnp.ones((ALL, HD), BF16)
    for copy in (mirror_lo, mirror_hi, *own, *mir):
        copy.wait_send()
    wo_copy.wait()
    for i, (py, pc) in enumerate(kv_peers):
        src = py * 2 + pc
        remote(kvs.at[pc], kv_ref.at[src], kv_send.at[i], kv_recv.at[src], kv_ids[i]).wait()
    for i, (pz, pc) in enumerate(q_peers):
        src = pz * 2 + pc
        remote(qs.at[pc], q_ref.at[src], q_send.at[i], q_recv.at[src], q_ids[i]).wait()
    values[:, :HD] = kv_ref[:, :, HD:].reshape(ALL, HD)
    peers, ids, mine = q_peers, q_ids, mine_q
    terms = rows

    def score_chunk(t, scores, top):
        at = pl.ds(pl.multiple_of(t * HB, HB), HB)
        q = q_ref[:, at, :].reshape(TQ, HD)
        keys = kv_ref[:, :, 0:HD].reshape(ALL, HD)
        s = lax.dot_general(q, keys, (((1,), (1,)), ((), ())), preferred_element_type=F32)
        best = top[...]
        for u in range(per):
            keep = kpos[u] <= qpos[t]
            kept = jnp.where(keep, s[:, u * HD : (u + 1) * HD], -1e30)
            scores[u] = kept
            best = jnp.maximum(best, kept)
        top[...] = best

    def weigh_chunk(scores, top):
        best = top[...]
        weight = [jnp.exp2(scores[u] - best).astype(BF16) for u in range(per)]
        summed[...] = jnp.dot(
            jnp.concatenate(weight, axis=1), values[...], preferred_element_type=F32
        )

    def clear(top):
        top[...] = jnp.full((TQ, HD), -1e29, F32)

    def attend_chunk(t, scores, top, next_scores=None, next_top=None):
        top[...] = jnp.broadcast_to(jnp.max(top[...], axis=1, keepdims=True), (TQ, HD))
        if next_top is not None:
            clear(next_top)
            score_chunk(t + 1, next_scores, next_top)
        weigh_chunk(scores, top)

        total = summed[:, HD:]
        some = total > 0
        total = jnp.where(some, total, 1.0)
        o_mine[t] = (summed[:, :HD] / total).astype(BF16).reshape(SRC, HB, HD)
        lse = jnp.where(some, top[...] + jnp.log2(total), -1e30)
        for u in range(SRC // 2):
            block = lse[u * HD : (u + 1) * HD, :]
            line = jnp.sum(jnp.where(diagonal, block, 0.0), axis=0, keepdims=True)
            l_mine[t, 2 * u] = line
            l_mine[t, 2 * u + 1] = pltpu.roll(line, HB, 1)
        parts[t, mine] = o_mine[t, mine]
        lses[t, mine] = l_mine[t, mine]
        for i, (pz, pc) in enumerate(peers):
            to = pz * 2 + pc
            remote(
                l_mine.at[t, to], lses.at[t, mine], l_send.at[i], l_recv.at[t, mine], ids[i]
            ).start()
            remote(
                o_mine.at[t, to], parts.at[t, mine], o_send.at[i], o_recv.at[t, mine], ids[i]
            ).start()

    def term(t):
        for i, (pz, pc) in enumerate(peers):
            src = pz * 2 + pc
            remote(
                l_mine.at[t, src], lses.at[t, src], l_send.at[i], l_recv.at[t, src], ids[i]
            ).wait_recv()
            remote(
                o_mine.at[t, src], parts.at[t, src], o_send.at[i], o_recv.at[t, src], ids[i]
            ).wait_recv()
        shares = []
        for h in range(2):
            lse = [lses[t, z * 2 + h] for z in range(4)]
            best = jnp.maximum(jnp.maximum(lse[0], lse[1]), jnp.maximum(lse[2], lse[3]))
            share = [jnp.exp2(line - best) for line in lse]
            total = share[0] + share[1] + share[2] + share[3]
            shares += [line / total for line in share]
        turned = jnp.concatenate(shares * (HD // SRC), axis=0).T
        for h in range(2):
            mixed = jnp.zeros((HB, HD), F32)
            for z in range(4):
                share = turned[0:HB, h * 4 + z : h * 4 + z + 1]
                mixed += share * parts[t, z * 2 + h].astype(F32)
            ctx[:, h * HD : (h + 1) * HD] = mixed.astype(BF16)
        at = pl.ds(pl.multiple_of(t * HB, HB), HB)
        terms[at, :] = jnp.dot(ctx[...], w_ref[...], preferred_element_type=F32).astype(BF16)

    def cols(v):
        return pl.ds(v * WIDTH, WIDTH)

    def cut(slot, lo, v):
        return terms.at[pl.ds(slot * HB + lo, HALF), cols(v)]

    def far(p, slot, side, v):
        return remote(
            cut(slot, side * HALF, v), halves.at[p, side, :, cols(v)],
            h_send.at[p, side, v], h_recv.at[p, side, v], left if side else right,
        )

    def near(p, slot, side, upper, v):
        return remote(
            cut(slot, upper * HALF, v), fulls.at[p, side, pl.ds(upper * HALF, HALF), cols(v)],
            f_send.at[p, side, upper, v], f_recv.at[p, side, upper, v], left if side else right,
        )

    def over(upper, v):
        return remote(
            cut(MIR, upper * HALF, v), mirrored.at[pl.ds(upper * HALF, HALF), cols(v)],
            z_send.at[upper, v], z_recv.at[upper, v], mirror,
        )

    fars, nears = (O0, O1), ((R0, L0), (R1, L1))

    def add(lo, v, *more):
        rows, columns = slice(lo, lo + HALF), slice(v * WIDTH, (v + 1) * WIDTH)
        total = terms[rows, columns].astype(F32)
        for ref in more:
            total = total + ref[:, columns].astype(F32)
        return total

    def store(lo, v, total):
        terms[lo : lo + HALF, v * WIDTH : (v + 1) * WIDTH] = total.astype(BF16)

    def send_far(p):
        for v in range(CUTS):
            for side in range(2):
                far(p, fars[p], side, v).start()

    def send_near(p, side):
        slot = nears[p][side]
        lo = slot * HB + side * HALF
        for v in range(CUTS):
            near(p, slot, side, 1 - side, v).start()
            far(p, fars[p], side, v).wait_recv()
            store(lo, v, add(lo, v, halves.at[p, side]))
            near(p, slot, side, side, v).start()

    def send_over(v):
        for upper in range(2):
            for side in range(2):
                near(1, nears[1][side], side, upper, v).wait_recv()
            lo = MIR * HB + upper * HALF
            rows = pl.ds(upper * HALF, HALF)
            store(lo, v, add(lo, v, fulls.at[1, 0, rows], fulls.at[1, 1, rows]))
            over(upper, v).start()

    def step_far():
        term(O1)
        send_far(1)

    def step_near():
        term(L1)
        send_near(1, 1)
        term(R1)
        send_near(1, 0)

    def step_mirror():
        term(MIR)
        send_over(0)

    clear(top_a)
    score_chunk(0, scores_a, top_a)

    @pl.loop(0, SLOTS // 2 - 1)
    def _(i):
        attend_chunk(2 * i, scores_a, top_a, scores_b, top_b)
        pl.when(i == 1)(step_far)
        pl.when(i == 2)(step_mirror)
        attend_chunk(2 * i + 1, scores_b, top_b, scores_a, top_a)
        pl.when(i == 1)(step_near)
        pl.when(i == 2)(lambda: send_over(1))

    attend_chunk(SLOTS - 2, scores_a, top_a, scores_b, top_b)
    term(O0)
    send_far(0)
    send_over(2)
    send_over(3)
    attend_chunk(SLOTS - 1, scores_b, top_b)
    term(L0)
    send_near(0, 1)
    term(R0)
    send_near(0, 0)
    term(OWN)
    for v in range(CUTS):
        for upper in range(2):
            for side in range(2):
                near(0, nears[0][side], side, upper, v).wait_recv()
            over(upper, v).wait_recv()
            rows = pl.ds(upper * HALF, HALF)
            total = add(
                OWN * HB + upper * HALF, v, fulls.at[0, 0, rows], fulls.at[0, 1, rows], mirrored.at[rows]
            )
            out_ref[rows, v * WIDTH : (v + 1) * WIDTH] = total.astype(BF16)
    for v in range(CUTS):
        for p in range(2):
            for side in range(2):
                far(p, fars[p], side, v).wait_send()
                for upper in range(2):
                    near(p, nears[p][side], side, upper, v).wait_send()
        for upper in range(2):
            over(upper, v).wait_send()
    for i, (pz, pc) in enumerate(peers):
        src = pz * 2 + pc
        remote(l_mine.at[:, src], lses.at[:, src], l_send.at[i], l_recv.at[0, src], ids[i]).wait_send()
        remote(o_mine.at[:, src], parts.at[:, src], o_send.at[i], o_recv.at[0, src], ids[i]).wait_send()


def sublayer(block_order, hidden_in, norm_gain, weight, out_weight):
    smem = pl.BlockSpec(memory_space=pltpu.SMEM)
    vmem = pl.BlockSpec(memory_space=pltpu.VMEM)
    hbm = pl.BlockSpec(memory_space=pl.ANY)
    dma = pltpu.SemaphoreType.DMA
    return pl.pallas_call(
        sublayer_kernel,
        out_shape=jax.ShapeDtypeStruct((HB, D), BF16),
        in_specs=[smem, vmem, vmem, hbm, hbm, vmem, vmem, vmem, vmem],
        out_specs=vmem,
        scratch_shapes=[
            pltpu.VMEM((ROWS, D), BF16),
            pltpu.VMEM((ROWS, HD), F32),
            pltpu.VMEM((ROWS, HD), F32),
            pltpu.VMEM((3, D, 2 * HD), BF16),
            pltpu.VMEM((2, ROWS, HD), BF16),
            pltpu.VMEM((2, ROWS, 2 * HD), BF16),
            pltpu.VMEM((SRC, ROWS, HD), BF16),
            pltpu.VMEM((SRC, ROWS, 2 * HD), BF16),
            pltpu.VMEM((2 * HD, D), BF16),
            pltpu.VMEM((ALL, 2 * HD), BF16),
            pltpu.VMEM((ALL // HD, TQ, HD), F32),
            pltpu.VMEM((ALL // HD, TQ, HD), F32),
            pltpu.VMEM((TQ, HD), F32),
            pltpu.VMEM((TQ, HD), F32),
            pltpu.VMEM((TQ, 2 * HD), F32),
            pltpu.VMEM((SLOTS, TQ, HD), jnp.int32),
            pltpu.VMEM((ALL // HD, 1, HD), jnp.int32),
            pltpu.VMEM((SLOTS, SRC, HB, HD), BF16),
            pltpu.VMEM((SLOTS, SRC, 1, HD), F32),
            pltpu.VMEM((SLOTS, SRC, HB, HD), BF16),
            pltpu.VMEM((SLOTS, SRC, 1, HD), F32),
            pltpu.VMEM((HB, 2 * HD), BF16),
            pltpu.VMEM((2, 2, HALF, D), BF16),
            pltpu.VMEM((2, 2, HB, D), BF16),
            pltpu.VMEM((HB, D), BF16),
            dma, dma, dma((2, 6)), dma((2, 6)), dma((2,)), dma((2,)),
            dma((SRC,)), dma((SRC,)), dma((SRC,)), dma((SRC,)),
            dma((SRC,)), dma((SLOTS, SRC)), dma((SRC,)), dma((SLOTS, SRC)),
            dma((2, 2, CUTS)), dma((2, 2, CUTS)), dma((2, 2, 2, CUTS)), dma((2, 2, 2, CUTS)),
            dma((2, CUTS)), dma((2, CUTS)),
        ],
        compiler_params=pltpu.CompilerParams(
            collective_id=0, has_side_effects=True, vmem_limit_bytes=60 << 20
        ),
        name="sublayer",
    )(block_order, hidden_in, norm_gain, weight, out_weight, *tables())


def local(hidden_in, norm_gain, qkv_weight, out_weight, block_order):
    weight = jnp.transpose(qkv_weight, (1, 0, 2))
    return sublayer(block_order, hidden_in, norm_gain[None, :], weight, out_weight)


def solution(mesh):
    in_specs = (P(("seq", "tp"), None), P(), P(None, None, "tp"), P("tp", None), P())
    out_specs = P(("seq", "tp"), None)
    return jax.shard_map(local, mesh=mesh, in_specs=in_specs, out_specs=out_specs, check_vma=False)
```

```python
import math

import jax
import jax.numpy as jnp
import numpy as np
from jax import lax
from jax.experimental import pallas as pl
from jax.experimental.pallas import tpu as pltpu
from jax.sharding import PartitionSpec as P

HD = 128
BLK = 128
D = 4096
SEQ = 16384
HB = 64
SLOTS = 8
ROWS = HB * SLOTS
SRC = 8
ALL = SRC * ROWS
HALF = HB // 2
CUTS = 4
WIDTH = D // CUTS
TQ = SRC * HB
MESH = pl.DeviceIdType.MESH
F32 = jnp.float32
BF16 = jnp.bfloat16

O1, L1, R1, MIR, O0, L0, R0, OWN = range(8)
CHUNKS = ((1, 2), (1, -1), (1, 1), (1, 0), (0, 2), (0, -1), (0, 1), (0, 0))
SCALE = math.log2(math.e) / HD**0.5
OTHERS = [(d, e) for d in range(4) for e in range(2)][1:]


def place():
    s = lax.axis_index("seq")
    t = lax.axis_index("tp")
    return s // 8, (s // 2) % 4, s % 2, t // 2, t % 2


def device(y, zl, c, x, zh):
    return ((y * 4 + zl) * 2 + c, x * 2 + zh)


def other_core(c, e):
    return 1 - c if e else c


def start_of(order, slot, y, zl, c, x, zh):
    mirrored, shift = CHUNKS[slot]
    if mirrored:
        zl, zh = 3 - zl, 1 - zh
    block = ((y * 4 + zl) * 2 + c) * (ROWS // BLK) + (x + shift + 4) % 4
    return order[block] * BLK + zh * HB


def tables():
    frequency = 10000.0 ** (-(np.arange(HD) % (HD // 2)) * 2.0 / HD)
    starts = np.arange(SEQ // HB)[:, None] * float(HB) * frequency[None, :]
    rows = np.arange(HB)[:, None] * frequency[None, :]
    made = [np.cos(starts), np.sin(starts), np.cos(rows), np.sin(rows)]
    return [jnp.asarray(t.astype(np.float32)) for t in made]


def greet(peers):
    barrier = pltpu.get_barrier_semaphore()
    for peer in peers:
        pl.semaphore_signal(barrier, inc=1, device_id=peer, device_id_type=MESH)
    return barrier


def remote(src, dst, send, recv, peer):
    return pltpu.make_async_remote_copy(
        src_ref=src, dst_ref=dst, send_sem=send, recv_sem=recv, device_id=peer, device_id_type=MESH
    )


def sublayer_kernel(
    order, hid, gain, w_hbm, wo_hbm, cos_start, sin_start, cos_row, sin_row, out_ref,
    rows, cos, sin, wv, qs, kvs, q_ref, kv_ref, w_ref, values, scores_a, scores_b,
    top_a, top_b, summed, qpos, kpos, o_mine, l_mine, parts, lses, ctx, halves, fulls, mirrored,
    w_sem, wo_sem, x_send, x_recv, m_send, m_recv, kv_send, kv_recv, q_send, q_recv,
    o_send, o_recv, l_send, l_recv, h_send, h_recv, f_send, f_recv, z_send, z_recv,
):
    y, zl, c, x, zh = place()
    right = device(y, zl, c, (x + 1) % 4, zh)
    left = device(y, zl, c, (x + 3) % 4, zh)
    mirror = device(y, 3 - zl, c, x, 1 - zh)
    kv_peers = [((y + d) % 4, other_core(c, e)) for d, e in OTHERS]
    q_peers = [((zl + d) % 4, other_core(c, e)) for d, e in OTHERS]
    kv_ids = [device(py, zl, pc, x, zh) for py, pc in kv_peers]
    q_ids = [device(y, pz, pc, x, zh) for pz, pc in q_peers]
    peers = [right, left, mirror] + kv_ids + q_ids[1:]
    barrier = greet(peers)
    w_copy = pltpu.make_async_copy(w_hbm, wv, w_sem)
    w_copy.start()
    wo_copy = pltpu.make_async_copy(wo_hbm, w_ref, wo_sem)
    wo_copy.start()

    floats = hid[...].astype(F32)
    scale = lax.rsqrt(jnp.mean(floats * floats, axis=-1, keepdims=True) + 1e-05)
    rows[OWN * HB : (OWN + 1) * HB, :] = (floats * scale * gain[...]).astype(BF16)
    pl.semaphore_wait(barrier, len(peers))

    def piece(slot, upper, v):
        return rows.at[pl.ds(slot * HB + upper * HALF, HALF), pl.ds(v * (D // 2), D // 2)]

    def spread(p, src, from_left, from_right, far):
        plan = (
            (src, from_left, 0, right),
            (src, from_right, 1, left),
            (src, from_left, 1, right),
            (src, from_right, 0, left),
            (from_left, far, 0, right),
            (from_right, far, 1, left),
        )
        return [
            [
                remote(
                    piece(a, upper, v), piece(b, upper, v),
                    x_send.at[p, kind, v], x_recv.at[p, kind, v], peer,
                )
                for v in range(2)
            ]
            for kind, (a, b, upper, peer) in enumerate(plan)
        ]

    over = [
        [
            remote(
                piece(OWN, upper, v), piece(MIR, upper, v),
                m_send.at[upper, v], m_recv.at[upper, v], mirror,
            )
            for v in range(2)
        ]
        for upper in range(2)
    ]
    own = spread(0, OWN, L0, R0, O0)
    mir = spread(1, MIR, L1, R1, O1)

    def arrived(*copies):
        for pair in copies:
            for copy in pair:
                copy.wait_recv()

    for upper in range(2):
        for copy in over[upper]:
            copy.start()
    for kinds in ((0, 1), (2, 3)):
        for v in range(2):
            for kind in kinds:
                own[kind][v].start()
    first_half = lax.broadcasted_iota(jnp.int32, (1, HD), 1) < HD // 2
    for slot in range(SLOTS):
        start = start_of(order, slot, y, zl, c, x, zh) // HB
        cs, sn = cos_start[pl.ds(start, 1), :], sin_start[pl.ds(start, 1), :]
        lo, hi = slot * HB, (slot + 1) * HB
        cos[lo:hi, :] = cs * cos_row[...] - sn * sin_row[...]
        sine = sn * cos_row[...] + cs * sin_row[...]
        sin[lo:hi, :] = jnp.where(first_half, -sine, sine)
    mine = y * 2 + c
    mine_q = zl * 2 + c

    def part(ref, lo, hi, *index):
        return ref.at[(*index, pl.ds(lo, hi - lo), slice(None))]

    def work(first, last):
        lo, hi = first * HB, last * HB
        chunk = rows[lo:hi, :]
        cs, sn = cos[lo:hi, :], sin[lo:hi, :]
        q = jnp.dot(chunk, wv[0], preferred_element_type=F32)
        k = jnp.dot(chunk, wv[1], preferred_element_type=F32)
        v = jnp.dot(chunk, wv[2], preferred_element_type=F32)
        for h in range(2):
            lane = slice(h * HD, (h + 1) * HD)
            for out, by, t in ((qs, SCALE, q[:, lane]), (kvs, 1.0, k[:, lane])):
                turned = t * cs + pltpu.roll(t, HD // 2, 1) * sn
                out[h, lo:hi, 0:HD] = (turned * by).astype(BF16)
            kvs[h, lo:hi, HD : 2 * HD] = v[:, lane].astype(BF16)
        for i, (py, pc) in enumerate(kv_peers):
            remote(
                part(kvs, lo, hi, pc), part(kv_ref, lo, hi, mine),
                kv_send.at[i], kv_recv.at[mine], kv_ids[i],
            ).start()
        kv_ref[mine, lo:hi, :] = kvs[c, lo:hi, :]
        values[pl.ds(pl.multiple_of(mine * ROWS, ROWS) + lo, hi - lo), :HD] = kvs[c, lo:hi, HD:]
        q_ref[mine_q, lo:hi, :] = qs[c, lo:hi, :]
        for i, (pz, pc) in enumerate(q_peers):
            remote(
                part(qs, lo, hi, pc), part(q_ref, lo, hi, mine_q),
                q_send.at[i], q_recv.at[mine_q], q_ids[i],
            ).start()

    w_copy.wait()
    work(OWN, OWN + 1)
    for v in range(2):
        for kind in range(2):
            own[kind][v].wait_recv()
            own[4 + kind][v].start()
    lane = lax.broadcasted_iota(jnp.int32, (1, HD), 1)
    row = lax.broadcasted_iota(jnp.int32, (HB, HD), 0)
    for src in range(SRC):
        starts = [start_of(order, slot, src // 2, zl, src % 2, x, zh) for slot in range(SLOTS)]
        for u in range(SLOTS // 2):
            kpos[src * (SLOTS // 2) + u] = jnp.where(
                lane < HB, starts[2 * u] + lane, starts[2 * u + 1] + lane - HB
            )
        for slot in range(SLOTS):
            qpos[slot, src * HB : (src + 1) * HB, :] = row + start_of(
                order, slot, y, src // 2, src % 2, x, zh
            )
    diagonal = lax.broadcasted_iota(jnp.int32, (HD, HD), 0) == lax.broadcasted_iota(
        jnp.int32, (HD, HD), 1
    )
    per = ALL // HD
    values[:, HD:] = jnp.ones((ALL, HD), BF16)
    arrived(own[2], own[3])
    work(L0, R0 + 1)
    for v in range(2):
        over[0][v].wait_recv()
        mir[0][v].start()
        mir[3][v].start()
    arrived(own[4], own[5])
    work(O0, O0 + 1)
    for v in range(2):
        over[1][v].wait_recv()
        mir[1][v].start()
        mir[2][v].start()
        mir[0][v].wait_recv()
        mir[4][v].start()
    work(MIR, MIR + 1)
    for v in range(2):
        mir[1][v].wait_recv()
        mir[5][v].start()
    arrived(mir[2], mir[3])
    work(L1, R1 + 1)
    arrived(mir[4], mir[5])
    work(O1, O1 + 1)
    for pair in (*over, *own, *mir):
        for copy in pair:
            copy.wait_send()
    wo_copy.wait()
    for i, (py, pc) in enumerate(kv_peers):
        src = py * 2 + pc
        remote(kvs.at[pc], kv_ref.at[src], kv_send.at[i], kv_recv.at[src], kv_ids[i]).wait()
        values[pl.ds(pl.multiple_of(src * ROWS, ROWS), ROWS), :HD] = kv_ref[src, :, HD:]
    for i, (pz, pc) in enumerate(q_peers):
        src = pz * 2 + pc
        remote(qs.at[pc], q_ref.at[src], q_send.at[i], q_recv.at[src], q_ids[i]).wait()
    peers, ids, mine = q_peers, q_ids, mine_q
    terms = rows

    def score_chunk(t, scores, top):
        at = pl.ds(pl.multiple_of(t * HB, HB), HB)
        q = q_ref[:, at, :].reshape(TQ, HD)
        keys = kv_ref[:, :, 0:HD].reshape(ALL, HD)
        s = lax.dot_general(q, keys, (((1,), (1,)), ((), ())), preferred_element_type=F32)
        best = top[...]
        for u in range(per):
            keep = kpos[u] <= qpos[t]
            kept = jnp.where(keep, s[:, u * HD : (u + 1) * HD], -1e30)
            scores[u] = kept
            best = jnp.maximum(best, kept)
        top[...] = best

    def weigh_chunk(scores, top):
        best = top[...]
        weight = [jnp.exp2(scores[u] - best).astype(BF16) for u in range(per)]
        summed[...] = jnp.dot(
            jnp.concatenate(weight, axis=1), values[...], preferred_element_type=F32
        )

    def clear(top):
        top[...] = jnp.full((TQ, HD), -1e29, F32)

    def attend_chunk(t, scores, top, next_scores=None, next_top=None):
        top[...] = jnp.broadcast_to(jnp.max(top[...], axis=1, keepdims=True), (TQ, HD))
        if next_top is not None:
            clear(next_top)
            score_chunk(t + 1, next_scores, next_top)
        weigh_chunk(scores, top)

        total = summed[:, HD:]
        some = total > 0
        total = jnp.where(some, total, 1.0)
        o_mine[t] = (summed[:, :HD] / total).astype(BF16).reshape(SRC, HB, HD)
        lse = jnp.where(some, top[...] + jnp.log2(total), -1e30)
        for u in range(SRC // 2):
            block = lse[u * HD : (u + 1) * HD, :]
            line = jnp.sum(jnp.where(diagonal, block, 0.0), axis=0, keepdims=True)
            l_mine[t, 2 * u] = line
            l_mine[t, 2 * u + 1] = pltpu.roll(line, HB, 1)
        parts[t, mine] = o_mine[t, mine]
        lses[t, mine] = l_mine[t, mine]
        for i, (pz, pc) in enumerate(peers):
            to = pz * 2 + pc
            remote(
                l_mine.at[t, to], lses.at[t, mine], l_send.at[i], l_recv.at[t, mine], ids[i]
            ).start()
            remote(
                o_mine.at[t, to], parts.at[t, mine], o_send.at[i], o_recv.at[t, mine], ids[i]
            ).start()

    def term(t):
        for i, (pz, pc) in enumerate(peers):
            src = pz * 2 + pc
            remote(
                l_mine.at[t, src], lses.at[t, src], l_send.at[i], l_recv.at[t, src], ids[i]
            ).wait_recv()
            remote(
                o_mine.at[t, src], parts.at[t, src], o_send.at[i], o_recv.at[t, src], ids[i]
            ).wait_recv()
        shares = []
        for h in range(2):
            lse = [lses[t, z * 2 + h] for z in range(4)]
            best = jnp.maximum(jnp.maximum(lse[0], lse[1]), jnp.maximum(lse[2], lse[3]))
            share = [jnp.exp2(line - best) for line in lse]
            total = share[0] + share[1] + share[2] + share[3]
            shares += [line / total for line in share]
        turned = jnp.concatenate(shares * (HD // SRC), axis=0).T
        for h in range(2):
            mixed = jnp.zeros((HB, HD), F32)
            for z in range(4):
                share = turned[0:HB, h * 4 + z : h * 4 + z + 1]
                mixed += share * parts[t, z * 2 + h].astype(F32)
            ctx[:, h * HD : (h + 1) * HD] = mixed.astype(BF16)
        at = pl.ds(pl.multiple_of(t * HB, HB), HB)
        terms[at, :] = jnp.dot(ctx[...], w_ref[...], preferred_element_type=F32).astype(BF16)

    def cols(v):
        return pl.ds(v * WIDTH, WIDTH)

    def cut(slot, lo, v):
        return terms.at[pl.ds(slot * HB + lo, HALF), cols(v)]

    def far(p, slot, side, v):
        return remote(
            cut(slot, side * HALF, v), halves.at[p, side, :, cols(v)],
            h_send.at[p, side, v], h_recv.at[p, side, v], left if side else right,
        )

    def near(p, slot, side, upper, v):
        return remote(
            cut(slot, upper * HALF, v), fulls.at[p, side, pl.ds(upper * HALF, HALF), cols(v)],
            f_send.at[p, side, upper, v], f_recv.at[p, side, upper, v], left if side else right,
        )

    def across(upper, v):
        return remote(
            cut(MIR, upper * HALF, v), mirrored.at[pl.ds(upper * HALF, HALF), cols(v)],
            z_send.at[upper, v], z_recv.at[upper, v], mirror,
        )

    fars, nears = (O0, O1), ((R0, L0), (R1, L1))

    def add(lo, v, *more):
        rows, columns = slice(lo, lo + HALF), slice(v * WIDTH, (v + 1) * WIDTH)
        total = terms[rows, columns].astype(F32)
        for ref in more:
            total = total + ref[:, columns].astype(F32)
        return total

    def store(lo, v, total):
        terms[lo : lo + HALF, v * WIDTH : (v + 1) * WIDTH] = total.astype(BF16)

    def send_far(p):
        for v in range(CUTS):
            for side in range(2):
                far(p, fars[p], side, v).start()

    def send_near(p, side):
        slot = nears[p][side]
        lo = slot * HB + side * HALF
        for v in range(CUTS):
            near(p, slot, side, 1 - side, v).start()
            far(p, fars[p], side, v).wait_recv()
            store(lo, v, add(lo, v, halves.at[p, side]))
            near(p, slot, side, side, v).start()

    def send_over(v):
        for upper in range(2):
            for side in range(2):
                near(1, nears[1][side], side, upper, v).wait_recv()
            lo = MIR * HB + upper * HALF
            rows = pl.ds(upper * HALF, HALF)
            store(lo, v, add(lo, v, fulls.at[1, 0, rows], fulls.at[1, 1, rows]))
            across(upper, v).start()

    def step_far():
        term(O1)
        send_far(1)

    def step_near():
        term(L1)
        send_near(1, 1)
        term(R1)
        send_near(1, 0)

    def step_mirror():
        term(MIR)
        send_over(0)

    clear(top_a)
    score_chunk(0, scores_a, top_a)

    @pl.loop(0, SLOTS // 2 - 1)
    def _(i):
        attend_chunk(2 * i, scores_a, top_a, scores_b, top_b)
        pl.when(i == 1)(step_far)
        pl.when(i == 2)(step_mirror)
        attend_chunk(2 * i + 1, scores_b, top_b, scores_a, top_a)
        pl.when(i == 1)(step_near)
        pl.when(i == 2)(lambda: send_over(1))

    attend_chunk(SLOTS - 2, scores_a, top_a, scores_b, top_b)
    term(O0)
    send_far(0)
    send_over(2)
    send_over(3)
    attend_chunk(SLOTS - 1, scores_b, top_b)
    term(L0)
    send_near(0, 1)
    term(R0)
    send_near(0, 0)
    term(OWN)
    for v in range(CUTS):
        for upper in range(2):
            for side in range(2):
                near(0, nears[0][side], side, upper, v).wait_recv()
            across(upper, v).wait_recv()
            rows = pl.ds(upper * HALF, HALF)
            total = add(
                OWN * HB + upper * HALF, v, fulls.at[0, 0, rows], fulls.at[0, 1, rows], mirrored.at[rows]
            )
            out_ref[rows, v * WIDTH : (v + 1) * WIDTH] = total.astype(BF16)
    for v in range(CUTS):
        for p in range(2):
            for side in range(2):
                far(p, fars[p], side, v).wait_send()
                for upper in range(2):
                    near(p, nears[p][side], side, upper, v).wait_send()
        for upper in range(2):
            across(upper, v).wait_send()
    for i, (pz, pc) in enumerate(peers):
        src = pz * 2 + pc
        remote(l_mine.at[:, src], lses.at[:, src], l_send.at[i], l_recv.at[0, src], ids[i]).wait_send()
        remote(o_mine.at[:, src], parts.at[:, src], o_send.at[i], o_recv.at[0, src], ids[i]).wait_send()


def sublayer(block_order, hidden_in, norm_gain, weight, out_weight):
    smem = pl.BlockSpec(memory_space=pltpu.SMEM)
    vmem = pl.BlockSpec(memory_space=pltpu.VMEM)
    hbm = pl.BlockSpec(memory_space=pl.ANY)
    dma = pltpu.SemaphoreType.DMA
    return pl.pallas_call(
        sublayer_kernel,
        out_shape=jax.ShapeDtypeStruct((HB, D), BF16),
        in_specs=[smem, vmem, vmem, hbm, hbm, vmem, vmem, vmem, vmem],
        out_specs=vmem,
        scratch_shapes=[
            pltpu.VMEM((ROWS, D), BF16),
            pltpu.VMEM((ROWS, HD), F32),
            pltpu.VMEM((ROWS, HD), F32),
            pltpu.VMEM((3, D, 2 * HD), BF16),
            pltpu.VMEM((2, ROWS, HD), BF16),
            pltpu.VMEM((2, ROWS, 2 * HD), BF16),
            pltpu.VMEM((SRC, ROWS, HD), BF16),
            pltpu.VMEM((SRC, ROWS, 2 * HD), BF16),
            pltpu.VMEM((2 * HD, D), BF16),
            pltpu.VMEM((ALL, 2 * HD), BF16),
            pltpu.VMEM((ALL // HD, TQ, HD), F32),
            pltpu.VMEM((ALL // HD, TQ, HD), F32),
            pltpu.VMEM((TQ, HD), F32),
            pltpu.VMEM((TQ, HD), F32),
            pltpu.VMEM((TQ, 2 * HD), F32),
            pltpu.VMEM((SLOTS, TQ, HD), jnp.int32),
            pltpu.VMEM((ALL // HD, 1, HD), jnp.int32),
            pltpu.VMEM((SLOTS, SRC, HB, HD), BF16),
            pltpu.VMEM((SLOTS, SRC, 1, HD), F32),
            pltpu.VMEM((SLOTS, SRC, HB, HD), BF16),
            pltpu.VMEM((SLOTS, SRC, 1, HD), F32),
            pltpu.VMEM((HB, 2 * HD), BF16),
            pltpu.VMEM((2, 2, HALF, D), BF16),
            pltpu.VMEM((2, 2, HB, D), BF16),
            pltpu.VMEM((HB, D), BF16),
            dma, dma, dma((2, 6, 2)), dma((2, 6, 2)), dma((2, 2)), dma((2, 2)),
            dma((SRC,)), dma((SRC,)), dma((SRC,)), dma((SRC,)),
            dma((SRC,)), dma((SLOTS, SRC)), dma((SRC,)), dma((SLOTS, SRC)),
            dma((2, 2, CUTS)), dma((2, 2, CUTS)), dma((2, 2, 2, CUTS)), dma((2, 2, 2, CUTS)),
            dma((2, CUTS)), dma((2, CUTS)),
        ],
        compiler_params=pltpu.CompilerParams(
            collective_id=0, has_side_effects=True, vmem_limit_bytes=60 << 20
        ),
        name="sublayer",
    )(block_order, hidden_in, norm_gain, weight, out_weight, *tables())


def local(hidden_in, norm_gain, qkv_weight, out_weight, block_order):
    weight = jnp.transpose(qkv_weight, (1, 0, 2))
    return sublayer(block_order, hidden_in, norm_gain[None, :], weight, out_weight)


def solution(mesh):
    in_specs = (P(("seq", "tp"), None), P(), P(None, None, "tp"), P("tp", None), P())
    out_specs = P(("seq", "tp"), None)
    return jax.shard_map(local, mesh=mesh, in_specs=in_specs, out_specs=out_specs, check_vma=False)
```

```python
import math

import jax
import jax.numpy as jnp
import numpy as np
from jax import lax
from jax.experimental import pallas as pl
from jax.experimental.pallas import tpu as pltpu
from jax.sharding import PartitionSpec as P

HD = 128
BLK = 128
D = 4096
SEQ = 16384
HB = 64
SLOTS = 8
ROWS = HB * SLOTS
SRC = 8
ALL = SRC * ROWS
HALF = HB // 2
CUTS = 4
WIDTH = D // CUTS
TQ = SRC * HB
MESH = pl.DeviceIdType.MESH
F32 = jnp.float32
BF16 = jnp.bfloat16

O1, L1, R1, MIR, O0, L0, R0, OWN = range(8)
CHUNKS = ((1, 2), (1, -1), (1, 1), (1, 0), (0, 2), (0, -1), (0, 1), (0, 0))
SCALE = math.log2(math.e) / HD**0.5
OTHERS = [(d, e) for d in range(4) for e in range(2)][1:]


def place():
    s = lax.axis_index("seq")
    t = lax.axis_index("tp")
    return s // 8, (s // 2) % 4, s % 2, t // 2, t % 2


def device(y, zl, c, x, zh):
    return ((y * 4 + zl) * 2 + c, x * 2 + zh)


def other_core(c, e):
    return 1 - c if e else c


def start_of(order, slot, y, zl, c, x, zh):
    mirrored, shift = CHUNKS[slot]
    if mirrored:
        zl, zh = 3 - zl, 1 - zh
    block = ((y * 4 + zl) * 2 + c) * (ROWS // BLK) + (x + shift + 4) % 4
    return order[block] * BLK + zh * HB


def tables():
    frequency = 10000.0 ** (-(np.arange(HD) % (HD // 2)) * 2.0 / HD)
    starts = np.arange(SEQ // HB)[:, None] * float(HB) * frequency[None, :]
    rows = np.arange(HB)[:, None] * frequency[None, :]
    made = [np.cos(starts), np.sin(starts), np.cos(rows), np.sin(rows)]
    return [jnp.asarray(t.astype(np.float32)) for t in made]


def greet(peers):
    barrier = pltpu.get_barrier_semaphore()
    for peer in peers:
        pl.semaphore_signal(barrier, inc=1, device_id=peer, device_id_type=MESH)
    return barrier


def remote(src, dst, send, recv, peer):
    return pltpu.make_async_remote_copy(
        src_ref=src, dst_ref=dst, send_sem=send, recv_sem=recv, device_id=peer, device_id_type=MESH
    )


def sublayer_kernel(
    order, hid_hbm, gain_hbm, w_hbm, wo_hbm, cos_start_hbm, sin_start_hbm, cos_row_hbm, sin_row_hbm,
    out_ref, hid, gain, cos_start, sin_start, cos_row, sin_row,
    rows, cos, sin, wv, qs, kvs, q_ref, kv_ref, w_ref, values, scores_a, scores_b,
    top_a, top_b, summed, qpos, kpos, o_mine, l_mine, parts, lses, ctx, halves, fulls, mirrored,
    in_sem, w_sem, wo_sem, x_send, x_recv, m_send, m_recv, kv_send, kv_recv, q_send, q_recv,
    o_send, o_recv, l_send, l_recv, h_send, h_recv, f_send, f_recv, z_send, z_recv,
):
    y, zl, c, x, zh = place()
    right = device(y, zl, c, (x + 1) % 4, zh)
    left = device(y, zl, c, (x + 3) % 4, zh)
    mirror = device(y, 3 - zl, c, x, 1 - zh)
    kv_peers = [((y + d) % 4, other_core(c, e)) for d, e in OTHERS]
    q_peers = [((zl + d) % 4, other_core(c, e)) for d, e in OTHERS]
    kv_ids = [device(py, zl, pc, x, zh) for py, pc in kv_peers]
    q_ids = [device(y, pz, pc, x, zh) for pz, pc in q_peers]
    peers = [right, left, mirror] + kv_ids + q_ids[1:]
    barrier = greet(peers)
    inputs = [
        pltpu.make_async_copy(src, dst, in_sem.at[i])
        for i, (src, dst) in enumerate((
            (hid_hbm, hid), (gain_hbm, gain), (cos_start_hbm, cos_start),
            (sin_start_hbm, sin_start), (cos_row_hbm, cos_row), (sin_row_hbm, sin_row),
        ))
    ]
    for copy in inputs:
        copy.start()
    w_copy = pltpu.make_async_copy(w_hbm, wv, w_sem)
    w_copy.start()
    wo_copy = pltpu.make_async_copy(wo_hbm, w_ref, wo_sem)
    wo_copy.start()

    inputs[0].wait()
    inputs[1].wait()
    floats = hid[...].astype(F32)
    scale = lax.rsqrt(jnp.mean(floats * floats, axis=-1, keepdims=True) + 1e-05)
    rows[OWN * HB : (OWN + 1) * HB, :] = (floats * scale * gain[...]).astype(BF16)
    pl.semaphore_wait(barrier, len(peers))

    def piece(slot, upper, v):
        return rows.at[pl.ds(slot * HB + upper * HALF, HALF), pl.ds(v * (D // 2), D // 2)]

    def spread(p, src, from_left, from_right, far):
        plan = (
            (src, from_left, 0, right),
            (src, from_right, 1, left),
            (src, from_left, 1, right),
            (src, from_right, 0, left),
            (from_left, far, 0, right),
            (from_right, far, 1, left),
        )
        return [
            [
                remote(
                    piece(a, upper, v), piece(b, upper, v),
                    x_send.at[p, kind, v], x_recv.at[p, kind, v], peer,
                )
                for v in range(2)
            ]
            for kind, (a, b, upper, peer) in enumerate(plan)
        ]

    over = [
        [
            remote(
                piece(OWN, upper, v), piece(MIR, upper, v),
                m_send.at[upper, v], m_recv.at[upper, v], mirror,
            )
            for v in range(2)
        ]
        for upper in range(2)
    ]
    own = spread(0, OWN, L0, R0, O0)
    mir = spread(1, MIR, L1, R1, O1)

    def arrived(*copies):
        for pair in copies:
            for copy in pair:
                copy.wait_recv()

    for upper in range(2):
        for copy in over[upper]:
            copy.start()
    for kinds in ((0, 1), (2, 3)):
        for v in range(2):
            for kind in kinds:
                own[kind][v].start()
    for copy in inputs[2:]:
        copy.wait()
    first_half = lax.broadcasted_iota(jnp.int32, (1, HD), 1) < HD // 2
    for slot in range(SLOTS):
        start = start_of(order, slot, y, zl, c, x, zh) // HB
        cs, sn = cos_start[pl.ds(start, 1), :], sin_start[pl.ds(start, 1), :]
        lo, hi = slot * HB, (slot + 1) * HB
        cos[lo:hi, :] = cs * cos_row[...] - sn * sin_row[...]
        sine = sn * cos_row[...] + cs * sin_row[...]
        sin[lo:hi, :] = jnp.where(first_half, -sine, sine)
    mine = y * 2 + c
    mine_q = zl * 2 + c

    def part(ref, lo, hi, *index):
        return ref.at[(*index, pl.ds(lo, hi - lo), slice(None))]

    def work(first, last):
        lo, hi = first * HB, last * HB
        chunk = rows[lo:hi, :]
        cs, sn = cos[lo:hi, :], sin[lo:hi, :]

        def turn(t):
            return t * cs + pltpu.roll(t, HD // 2, 1) * sn

        k = jnp.dot(chunk, wv[1], preferred_element_type=F32)
        v = jnp.dot(chunk, wv[2], preferred_element_type=F32)
        for h in range(2):
            lane = slice(h * HD, (h + 1) * HD)
            kvs[h, lo:hi, 0:HD] = turn(k[:, lane]).astype(BF16)
            kvs[h, lo:hi, HD : 2 * HD] = v[:, lane].astype(BF16)
        for i, (py, pc) in enumerate(kv_peers):
            remote(
                part(kvs, lo, hi, pc), part(kv_ref, lo, hi, mine),
                kv_send.at[i], kv_recv.at[mine], kv_ids[i],
            ).start()
        q = jnp.dot(chunk, wv[0], preferred_element_type=F32)
        for h in range(2):
            qs[h, lo:hi, :] = (turn(q[:, h * HD : (h + 1) * HD]) * SCALE).astype(BF16)
        kv_ref[mine, lo:hi, :] = kvs[c, lo:hi, :]
        values[pl.ds(pl.multiple_of(mine * ROWS, ROWS) + lo, hi - lo), :HD] = kvs[c, lo:hi, HD:]
        q_ref[mine_q, lo:hi, :] = qs[c, lo:hi, :]
        for i, (pz, pc) in enumerate(q_peers):
            remote(
                part(qs, lo, hi, pc), part(q_ref, lo, hi, mine_q),
                q_send.at[i], q_recv.at[mine_q], q_ids[i],
            ).start()

    w_copy.wait()
    work(OWN, OWN + 1)
    for v in range(2):
        for kind in range(2):
            own[kind][v].wait_recv()
            own[4 + kind][v].start()
    lane = lax.broadcasted_iota(jnp.int32, (1, HD), 1)
    row = lax.broadcasted_iota(jnp.int32, (HB, HD), 0)
    for src in range(SRC):
        starts = [start_of(order, slot, src // 2, zl, src % 2, x, zh) for slot in range(SLOTS)]
        for u in range(SLOTS // 2):
            kpos[src * (SLOTS // 2) + u] = jnp.where(
                lane < HB, starts[2 * u] + lane, starts[2 * u + 1] + lane - HB
            )
        for slot in range(SLOTS):
            qpos[slot, src * HB : (src + 1) * HB, :] = row + start_of(
                order, slot, y, src // 2, src % 2, x, zh
            )
    diagonal = lax.broadcasted_iota(jnp.int32, (HD, HD), 0) == lax.broadcasted_iota(
        jnp.int32, (HD, HD), 1
    )
    per = ALL // HD
    values[:, HD:] = jnp.ones((ALL, HD), BF16)
    arrived(own[2], own[3])
    work(L0, R0 + 1)
    for v in range(2):
        over[0][v].wait_recv()
        mir[0][v].start()
        mir[3][v].start()
    arrived(own[4], own[5])
    work(O0, O0 + 1)
    for v in range(2):
        over[1][v].wait_recv()
        mir[1][v].start()
        mir[2][v].start()
        mir[0][v].wait_recv()
        mir[4][v].start()
    work(MIR, MIR + 1)
    for v in range(2):
        mir[1][v].wait_recv()
        mir[5][v].start()
    arrived(mir[2], mir[3])
    work(L1, R1 + 1)
    arrived(mir[4], mir[5])
    work(O1, O1 + 1)
    for pair in (*over, *own, *mir):
        for copy in pair:
            copy.wait_send()
    wo_copy.wait()
    for i, (py, pc) in enumerate(kv_peers):
        src = py * 2 + pc
        remote(kvs.at[pc], kv_ref.at[src], kv_send.at[i], kv_recv.at[src], kv_ids[i]).wait()
        values[pl.ds(pl.multiple_of(src * ROWS, ROWS), ROWS), :HD] = kv_ref[src, :, HD:]
    for i, (pz, pc) in enumerate(q_peers):
        src = pz * 2 + pc
        remote(qs.at[pc], q_ref.at[src], q_send.at[i], q_recv.at[src], q_ids[i]).wait()
    peers, ids, mine = q_peers, q_ids, mine_q
    terms = rows

    def score_chunk(t, scores, top):
        at = pl.ds(pl.multiple_of(t * HB, HB), HB)
        q = q_ref[:, at, :].reshape(TQ, HD)
        keys = kv_ref[:, :, 0:HD].reshape(ALL, HD)
        s = lax.dot_general(q, keys, (((1,), (1,)), ((), ())), preferred_element_type=F32)
        best = top[...]
        for u in range(per):
            keep = kpos[u] <= qpos[t]
            kept = jnp.where(keep, s[:, u * HD : (u + 1) * HD], -1e30)
            scores[u] = kept
            best = jnp.maximum(best, kept)
        top[...] = best

    def weigh_chunk(scores, top):
        best = top[...]
        weight = [jnp.exp2(scores[u] - best).astype(BF16) for u in range(per)]
        summed[...] = jnp.dot(
            jnp.concatenate(weight, axis=1), values[...], preferred_element_type=F32
        )

    def clear(top):
        top[...] = jnp.full((TQ, HD), -1e29, F32)

    def attend_chunk(t, scores, top, next_scores=None, next_top=None):
        top[...] = jnp.broadcast_to(jnp.max(top[...], axis=1, keepdims=True), (TQ, HD))
        if next_top is not None:
            clear(next_top)
            score_chunk(t + 1, next_scores, next_top)
        weigh_chunk(scores, top)

        total = summed[:, HD:]
        some = total > 0
        total = jnp.where(some, total, 1.0)
        o_mine[t] = (summed[:, :HD] / total).astype(BF16).reshape(SRC, HB, HD)
        lse = jnp.where(some, top[...] + jnp.log2(total), -1e30)
        for u in range(SRC // 2):
            block = lse[u * HD : (u + 1) * HD, :]
            line = jnp.sum(jnp.where(diagonal, block, 0.0), axis=0, keepdims=True)
            l_mine[t, 2 * u] = line
            l_mine[t, 2 * u + 1] = pltpu.roll(line, HB, 1)
        parts[t, mine] = o_mine[t, mine]
        lses[t, mine] = l_mine[t, mine]
        for i, (pz, pc) in enumerate(peers):
            to = pz * 2 + pc
            remote(
                l_mine.at[t, to], lses.at[t, mine], l_send.at[i], l_recv.at[t, mine], ids[i]
            ).start()
            remote(
                o_mine.at[t, to], parts.at[t, mine], o_send.at[i], o_recv.at[t, mine], ids[i]
            ).start()

    def term(t):
        for i, (pz, pc) in enumerate(peers):
            src = pz * 2 + pc
            remote(
                l_mine.at[t, src], lses.at[t, src], l_send.at[i], l_recv.at[t, src], ids[i]
            ).wait_recv()
            remote(
                o_mine.at[t, src], parts.at[t, src], o_send.at[i], o_recv.at[t, src], ids[i]
            ).wait_recv()
        shares = []
        for h in range(2):
            lse = [lses[t, z * 2 + h] for z in range(4)]
            best = jnp.maximum(jnp.maximum(lse[0], lse[1]), jnp.maximum(lse[2], lse[3]))
            share = [jnp.exp2(line - best) for line in lse]
            total = share[0] + share[1] + share[2] + share[3]
            shares += [line / total for line in share]
        turned = jnp.concatenate(shares * (HD // SRC), axis=0).T
        for h in range(2):
            mixed = jnp.zeros((HB, HD), F32)
            for z in range(4):
                share = turned[0:HB, h * 4 + z : h * 4 + z + 1]
                mixed += share * parts[t, z * 2 + h].astype(F32)
            ctx[:, h * HD : (h + 1) * HD] = mixed.astype(BF16)
        at = pl.ds(pl.multiple_of(t * HB, HB), HB)
        terms[at, :] = jnp.dot(ctx[...], w_ref[...], preferred_element_type=F32).astype(BF16)

    def cols(v):
        return pl.ds(v * WIDTH, WIDTH)

    def cut(slot, lo, v):
        return terms.at[pl.ds(slot * HB + lo, HALF), cols(v)]

    def far(p, slot, side, v):
        return remote(
            cut(slot, side * HALF, v), halves.at[p, side, :, cols(v)],
            h_send.at[p, side, v], h_recv.at[p, side, v], left if side else right,
        )

    def near(p, slot, side, upper, v):
        return remote(
            cut(slot, upper * HALF, v), fulls.at[p, side, pl.ds(upper * HALF, HALF), cols(v)],
            f_send.at[p, side, upper, v], f_recv.at[p, side, upper, v], left if side else right,
        )

    def across(upper, v):
        return remote(
            cut(MIR, upper * HALF, v), mirrored.at[pl.ds(upper * HALF, HALF), cols(v)],
            z_send.at[upper, v], z_recv.at[upper, v], mirror,
        )

    fars, nears = (O0, O1), ((R0, L0), (R1, L1))

    def add(lo, v, *more):
        rows, columns = slice(lo, lo + HALF), slice(v * WIDTH, (v + 1) * WIDTH)
        total = terms[rows, columns].astype(F32)
        for ref in more:
            total = total + ref[:, columns].astype(F32)
        return total

    def store(lo, v, total):
        terms[lo : lo + HALF, v * WIDTH : (v + 1) * WIDTH] = total.astype(BF16)

    def send_far(p):
        for v in range(CUTS):
            for side in range(2):
                far(p, fars[p], side, v).start()

    def send_near(p, side):
        slot = nears[p][side]
        lo = slot * HB + side * HALF
        for v in range(CUTS):
            near(p, slot, side, 1 - side, v).start()
            far(p, fars[p], side, v).wait_recv()
            store(lo, v, add(lo, v, halves.at[p, side]))
            near(p, slot, side, side, v).start()

    def send_over(v):
        for upper in range(2):
            for side in range(2):
                near(1, nears[1][side], side, upper, v).wait_recv()
            lo = MIR * HB + upper * HALF
            rows = pl.ds(upper * HALF, HALF)
            store(lo, v, add(lo, v, fulls.at[1, 0, rows], fulls.at[1, 1, rows]))
            across(upper, v).start()

    def step_far():
        term(O1)
        send_far(1)

    def step_near():
        term(L1)
        send_near(1, 1)
        term(R1)
        send_near(1, 0)

    def step_mirror():
        term(MIR)
        send_over(0)

    clear(top_a)
    score_chunk(0, scores_a, top_a)

    @pl.loop(0, SLOTS // 2 - 1)
    def _(i):
        attend_chunk(2 * i, scores_a, top_a, scores_b, top_b)
        pl.when(i == 1)(step_far)
        pl.when(i == 2)(step_mirror)
        attend_chunk(2 * i + 1, scores_b, top_b, scores_a, top_a)
        pl.when(i == 1)(step_near)
        pl.when(i == 2)(lambda: send_over(1))

    attend_chunk(SLOTS - 2, scores_a, top_a, scores_b, top_b)
    term(O0)
    send_far(0)
    send_over(2)
    send_over(3)
    attend_chunk(SLOTS - 1, scores_b, top_b)
    term(L0)
    send_near(0, 1)
    term(R0)
    send_near(0, 0)
    term(OWN)
    for v in range(CUTS):
        for upper in range(2):
            for side in range(2):
                near(0, nears[0][side], side, upper, v).wait_recv()
            across(upper, v).wait_recv()
            rows = pl.ds(upper * HALF, HALF)
            total = add(
                OWN * HB + upper * HALF, v, fulls.at[0, 0, rows], fulls.at[0, 1, rows], mirrored.at[rows]
            )
            out_ref[rows, v * WIDTH : (v + 1) * WIDTH] = total.astype(BF16)
    for v in range(CUTS):
        for p in range(2):
            for side in range(2):
                far(p, fars[p], side, v).wait_send()
                for upper in range(2):
                    near(p, nears[p][side], side, upper, v).wait_send()
        for upper in range(2):
            across(upper, v).wait_send()
    for i, (pz, pc) in enumerate(peers):
        src = pz * 2 + pc
        remote(l_mine.at[:, src], lses.at[:, src], l_send.at[i], l_recv.at[0, src], ids[i]).wait_send()
        remote(o_mine.at[:, src], parts.at[:, src], o_send.at[i], o_recv.at[0, src], ids[i]).wait_send()


def sublayer(block_order, hidden_in, norm_gain, weight, out_weight):
    smem = pl.BlockSpec(memory_space=pltpu.SMEM)
    vmem = pl.BlockSpec(memory_space=pltpu.VMEM)
    hbm = pl.BlockSpec(memory_space=pl.ANY)
    dma = pltpu.SemaphoreType.DMA
    return pl.pallas_call(
        sublayer_kernel,
        out_shape=jax.ShapeDtypeStruct((HB, D), BF16),
        in_specs=[smem] + [hbm] * 8,
        out_specs=vmem,
        scratch_shapes=[
            pltpu.VMEM((HB, D), BF16),
            pltpu.VMEM((1, D), F32),
            pltpu.VMEM((SEQ // HB, HD), F32),
            pltpu.VMEM((SEQ // HB, HD), F32),
            pltpu.VMEM((HB, HD), F32),
            pltpu.VMEM((HB, HD), F32),
            pltpu.VMEM((ROWS, D), BF16),
            pltpu.VMEM((ROWS, HD), F32),
            pltpu.VMEM((ROWS, HD), F32),
            pltpu.VMEM((3, D, 2 * HD), BF16),
            pltpu.VMEM((2, ROWS, HD), BF16),
            pltpu.VMEM((2, ROWS, 2 * HD), BF16),
            pltpu.VMEM((SRC, ROWS, HD), BF16),
            pltpu.VMEM((SRC, ROWS, 2 * HD), BF16),
            pltpu.VMEM((2 * HD, D), BF16),
            pltpu.VMEM((ALL, 2 * HD), BF16),
            pltpu.VMEM((ALL // HD, TQ, HD), F32),
            pltpu.VMEM((ALL // HD, TQ, HD), F32),
            pltpu.VMEM((TQ, HD), F32),
            pltpu.VMEM((TQ, HD), F32),
            pltpu.VMEM((TQ, 2 * HD), F32),
            pltpu.VMEM((SLOTS, TQ, HD), jnp.int32),
            pltpu.VMEM((ALL // HD, 1, HD), jnp.int32),
            pltpu.VMEM((SLOTS, SRC, HB, HD), BF16),
            pltpu.VMEM((SLOTS, SRC, 1, HD), F32),
            pltpu.VMEM((SLOTS, SRC, HB, HD), BF16),
            pltpu.VMEM((SLOTS, SRC, 1, HD), F32),
            pltpu.VMEM((HB, 2 * HD), BF16),
            pltpu.VMEM((2, 2, HALF, D), BF16),
            pltpu.VMEM((2, 2, HB, D), BF16),
            pltpu.VMEM((HB, D), BF16),
            dma((6,)), dma, dma, dma((2, 6, 2)), dma((2, 6, 2)), dma((2, 2)), dma((2, 2)),
            dma((SRC,)), dma((SRC,)), dma((SRC,)), dma((SRC,)),
            dma((SRC,)), dma((SLOTS, SRC)), dma((SRC,)), dma((SLOTS, SRC)),
            dma((2, 2, CUTS)), dma((2, 2, CUTS)), dma((2, 2, 2, CUTS)), dma((2, 2, 2, CUTS)),
            dma((2, CUTS)), dma((2, CUTS)),
        ],
        compiler_params=pltpu.CompilerParams(
            collective_id=0, has_side_effects=True, vmem_limit_bytes=60 << 20
        ),
        name="sublayer",
    )(block_order, hidden_in, norm_gain, weight, out_weight, *tables())


def local(hidden_in, norm_gain, qkv_weight, out_weight, block_order):
    weight = jnp.transpose(qkv_weight, (1, 0, 2))
    return sublayer(block_order, hidden_in, norm_gain[None, :], weight, out_weight)


def solution(mesh):
    in_specs = (P(("seq", "tp"), None), P(), P(None, None, "tp"), P("tp", None), P())
    out_specs = P(("seq", "tp"), None)
    return jax.shard_map(local, mesh=mesh, in_specs=in_specs, out_specs=out_specs, check_vma=False)
```

```python
import math

import jax
import jax.numpy as jnp
import numpy as np
from jax import lax
from jax.experimental import pallas as pl
from jax.experimental.pallas import tpu as pltpu
from jax.sharding import PartitionSpec as P

HD = 128
BLK = 128
D = 4096
SEQ = 16384
HB = 64
SLOTS = 8
ROWS = HB * SLOTS
SRC = 8
ALL = SRC * ROWS
HALF = HB // 2
CUTS = 4
WIDTH = D // CUTS
TQ = SRC * HB
MESH = pl.DeviceIdType.MESH
F32 = jnp.float32
BF16 = jnp.bfloat16

O1, L1, R1, MIR, O0, L0, R0, OWN = range(8)
CHUNKS = ((1, 2), (1, -1), (1, 1), (1, 0), (0, 2), (0, -1), (0, 1), (0, 0))
SCALE = math.log2(math.e) / HD**0.5
OTHERS = [(0, 1)] + [(d, e) for d in (2, 1, 3) for e in range(2)]


def place():
    s = lax.axis_index("seq")
    t = lax.axis_index("tp")
    return s // 8, (s // 2) % 4, s % 2, t // 2, t % 2


def device(y, zl, c, x, zh):
    return ((y * 4 + zl) * 2 + c, x * 2 + zh)


def far_first(zl):
    upper = zl // 2
    turned = zl + upper * (3 - 2 * zl)
    return [place + upper * (3 - 2 * place) for place in (3, 2, 1 - turned)]


def other_core(c, e):
    return 1 - c if e else c


def start_of(order, slot, y, zl, c, x, zh):
    mirrored, shift = CHUNKS[slot]
    if mirrored:
        zl, zh = 3 - zl, 1 - zh
    block = ((y * 4 + zl) * 2 + c) * (ROWS // BLK) + (x + shift + 4) % 4
    return order[block] * BLK + zh * HB


def tables():
    frequency = 10000.0 ** (-(np.arange(HD) % (HD // 2)) * 2.0 / HD)
    starts = np.arange(SEQ // HB)[:, None] * float(HB) * frequency[None, :]
    rows = np.arange(HB)[:, None] * frequency[None, :]
    made = [np.cos(starts), np.sin(starts), np.cos(rows), np.sin(rows)]
    return [jnp.asarray(t.astype(np.float32)) for t in made]


def greet(peers):
    barrier = pltpu.get_barrier_semaphore()
    for peer in peers:
        pl.semaphore_signal(barrier, inc=1, device_id=peer, device_id_type=MESH)
    return barrier


def remote(src, dst, send, recv, peer):
    return pltpu.make_async_remote_copy(
        src_ref=src, dst_ref=dst, send_sem=send, recv_sem=recv, device_id=peer, device_id_type=MESH
    )


def sublayer_kernel(
    order, hid_hbm, gain_hbm, w_hbm, wo_hbm, cos_start_hbm, sin_start_hbm, cos_row_hbm, sin_row_hbm,
    out_ref, hid, gain, cos_start, sin_start, cos_row, sin_row,
    rows, cos, sin, wv, qs, kvs, q_ref, kv_ref, w_ref, values, scores_a, scores_b,
    top_a, top_b, summed, qpos, kpos, o_mine, l_mine, parts, lses, ctx, halves, fulls, mirrored,
    in_sem, w_sem, wo_sem, x_send, x_recv, m_send, m_recv, kv_send, kv_recv, q_send, q_recv,
    o_send, o_recv, l_send, l_recv, h_send, h_recv, f_send, f_recv, z_send, z_recv,
):
    y, zl, c, x, zh = place()
    right = device(y, zl, c, (x + 1) % 4, zh)
    left = device(y, zl, c, (x + 3) % 4, zh)
    mirror = device(y, 3 - zl, c, x, 1 - zh)
    kv_peers = [((y + d) % 4, other_core(c, e)) for d, e in OTHERS]
    q_peers = [(zl, 1 - c)] + [(pz, other_core(c, e)) for pz in far_first(zl) for e in range(2)]
    kv_ids = [device(py, zl, pc, x, zh) for py, pc in kv_peers]
    q_ids = [device(y, pz, pc, x, zh) for pz, pc in q_peers]
    peers = [right, left, mirror] + kv_ids + q_ids[1:]
    barrier = greet(peers)
    inputs = [
        pltpu.make_async_copy(src, dst, in_sem.at[i])
        for i, (src, dst) in enumerate((
            (hid_hbm, hid), (gain_hbm, gain), (cos_start_hbm, cos_start),
            (sin_start_hbm, sin_start), (cos_row_hbm, cos_row), (sin_row_hbm, sin_row),
        ))
    ]
    for copy in inputs:
        copy.start()
    w_copy = pltpu.make_async_copy(w_hbm, wv, w_sem)
    w_copy.start()
    wo_copy = pltpu.make_async_copy(wo_hbm, w_ref, wo_sem)
    wo_copy.start()

    inputs[0].wait()
    inputs[1].wait()
    floats = hid[...].astype(F32)
    scale = lax.rsqrt(jnp.mean(floats * floats, axis=-1, keepdims=True) + 1e-05)
    rows[OWN * HB : (OWN + 1) * HB, :] = (floats * scale * gain[...]).astype(BF16)
    pl.semaphore_wait(barrier, len(peers))

    def piece(slot, upper, v):
        return rows.at[pl.ds(slot * HB + upper * HALF, HALF), pl.ds(v * (D // 2), D // 2)]

    def spread(p, src, from_left, from_right, far):
        plan = (
            (src, from_left, 0, right),
            (src, from_right, 1, left),
            (src, from_left, 1, right),
            (src, from_right, 0, left),
            (from_left, far, 0, right),
            (from_right, far, 1, left),
        )
        return [
            [
                remote(
                    piece(a, upper, v), piece(b, upper, v),
                    x_send.at[p, kind, v], x_recv.at[p, kind, v], peer,
                )
                for v in range(2)
            ]
            for kind, (a, b, upper, peer) in enumerate(plan)
        ]

    over = [
        [
            remote(
                piece(OWN, upper, v), piece(MIR, upper, v),
                m_send.at[upper, v], m_recv.at[upper, v], mirror,
            )
            for v in range(2)
        ]
        for upper in range(2)
    ]
    own = spread(0, OWN, L0, R0, O0)
    mir = spread(1, MIR, L1, R1, O1)

    def arrived(*copies):
        for pair in copies:
            for copy in pair:
                copy.wait_recv()

    for upper in range(2):
        for copy in over[upper]:
            copy.start()
    for kinds in ((0, 1), (2, 3)):
        for v in range(2):
            for kind in kinds:
                own[kind][v].start()
    for copy in inputs[2:]:
        copy.wait()
    first_half = lax.broadcasted_iota(jnp.int32, (1, HD), 1) < HD // 2
    for slot in range(SLOTS):
        start = start_of(order, slot, y, zl, c, x, zh) // HB
        cs, sn = cos_start[pl.ds(start, 1), :], sin_start[pl.ds(start, 1), :]
        lo, hi = slot * HB, (slot + 1) * HB
        cos[lo:hi, :] = cs * cos_row[...] - sn * sin_row[...]
        sine = sn * cos_row[...] + cs * sin_row[...]
        sin[lo:hi, :] = jnp.where(first_half, -sine, sine)
    mine = y * 2 + c
    mine_q = zl * 2 + c

    def part(ref, lo, hi, *index):
        return ref.at[(*index, pl.ds(lo, hi - lo), slice(None))]

    def work(first, last):
        lo, hi = first * HB, last * HB
        chunk = rows[lo:hi, :]
        cs, sn = cos[lo:hi, :], sin[lo:hi, :]

        def turn(t):
            return t * cs + pltpu.roll(t, HD // 2, 1) * sn

        k = jnp.dot(chunk, wv[1], preferred_element_type=F32)
        v = jnp.dot(chunk, wv[2], preferred_element_type=F32)
        for h in range(2):
            lane = slice(h * HD, (h + 1) * HD)
            kvs[h, lo:hi, 0:HD] = turn(k[:, lane]).astype(BF16)
            kvs[h, lo:hi, HD : 2 * HD] = v[:, lane].astype(BF16)
        for i, (py, pc) in enumerate(kv_peers):
            remote(
                part(kvs, lo, hi, pc), part(kv_ref, lo, hi, mine),
                kv_send.at[i], kv_recv.at[mine], kv_ids[i],
            ).start()
        q = jnp.dot(chunk, wv[0], preferred_element_type=F32)
        for h in range(2):
            qs[h, lo:hi, :] = (turn(q[:, h * HD : (h + 1) * HD]) * SCALE).astype(BF16)
        kv_ref[mine, lo:hi, :] = kvs[c, lo:hi, :]
        values[pl.ds(pl.multiple_of(mine * ROWS, ROWS) + lo, hi - lo), :HD] = kvs[c, lo:hi, HD:]
        q_ref[mine_q, lo:hi, :] = qs[c, lo:hi, :]
        for i, (pz, pc) in enumerate(q_peers):
            remote(
                part(qs, lo, hi, pc), part(q_ref, lo, hi, mine_q),
                q_send.at[i], q_recv.at[mine_q], q_ids[i],
            ).start()

    w_copy.wait()
    work(OWN, OWN + 1)
    for v in range(2):
        for kind in range(2):
            own[kind][v].wait_recv()
            own[4 + kind][v].start()
    lane = lax.broadcasted_iota(jnp.int32, (1, HD), 1)
    row = lax.broadcasted_iota(jnp.int32, (HB, HD), 0)
    for src in range(SRC):
        starts = [start_of(order, slot, src // 2, zl, src % 2, x, zh) for slot in range(SLOTS)]
        for u in range(SLOTS // 2):
            kpos[src * (SLOTS // 2) + u] = jnp.where(
                lane < HB, starts[2 * u] + lane, starts[2 * u + 1] + lane - HB
            )
        for slot in range(SLOTS):
            qpos[slot, src * HB : (src + 1) * HB, :] = row + start_of(
                order, slot, y, src // 2, src % 2, x, zh
            )
    diagonal = lax.broadcasted_iota(jnp.int32, (HD, HD), 0) == lax.broadcasted_iota(
        jnp.int32, (HD, HD), 1
    )
    per = ALL // HD
    values[:, HD:] = jnp.ones((ALL, HD), BF16)
    arrived(own[2], own[3])
    work(L0, R0 + 1)
    for v in range(2):
        over[0][v].wait_recv()
        mir[0][v].start()
        mir[3][v].start()
    arrived(own[4], own[5])
    work(O0, O0 + 1)
    for v in range(2):
        over[1][v].wait_recv()
        mir[1][v].start()
        mir[2][v].start()
        mir[0][v].wait_recv()
        mir[4][v].start()
    work(MIR, MIR + 1)
    for v in range(2):
        mir[1][v].wait_recv()
        mir[5][v].start()
    arrived(mir[2], mir[3])
    work(L1, R1 + 1)
    arrived(mir[4], mir[5])
    work(O1, O1 + 1)
    for pair in (*over, *own, *mir):
        for copy in pair:
            copy.wait_send()
    wo_copy.wait()
    for i, (py, pc) in enumerate(kv_peers):
        src = py * 2 + pc
        remote(kvs.at[pc], kv_ref.at[src], kv_send.at[i], kv_recv.at[src], kv_ids[i]).wait()
        values[pl.ds(pl.multiple_of(src * ROWS, ROWS), ROWS), :HD] = kv_ref[src, :, HD:]
    for i, (pz, pc) in enumerate(q_peers):
        src = pz * 2 + pc
        remote(qs.at[pc], q_ref.at[src], q_send.at[i], q_recv.at[src], q_ids[i]).wait()
    peers, ids, mine = q_peers, q_ids, mine_q
    terms = rows

    def score_chunk(t, scores, top):
        at = pl.ds(pl.multiple_of(t * HB, HB), HB)
        q = q_ref[:, at, :].reshape(TQ, HD)
        keys = kv_ref[:, :, 0:HD].reshape(ALL, HD)
        s = lax.dot_general(q, keys, (((1,), (1,)), ((), ())), preferred_element_type=F32)
        best = top[...]
        for u in range(per):
            keep = kpos[u] <= qpos[t]
            kept = jnp.where(keep, s[:, u * HD : (u + 1) * HD], -1e30)
            scores[u] = kept
            best = jnp.maximum(best, kept)
        top[...] = best

    def weigh_chunk(scores, top):
        best = top[...]
        weight = [jnp.exp2(scores[u] - best).astype(BF16) for u in range(per)]
        summed[...] = jnp.dot(
            jnp.concatenate(weight, axis=1), values[...], preferred_element_type=F32
        )

    def clear(top):
        top[...] = jnp.full((TQ, HD), -1e29, F32)

    def attend_chunk(t, scores, top, next_scores=None, next_top=None):
        top[...] = jnp.broadcast_to(jnp.max(top[...], axis=1, keepdims=True), (TQ, HD))
        if next_top is not None:
            clear(next_top)
            score_chunk(t + 1, next_scores, next_top)
        weigh_chunk(scores, top)

        total = summed[:, HD:]
        some = total > 0
        total = jnp.where(some, total, 1.0)
        o_mine[t] = (summed[:, :HD] / total).astype(BF16).reshape(SRC, HB, HD)
        lse = jnp.where(some, top[...] + jnp.log2(total), -1e30)
        for u in range(SRC // 2):
            block = lse[u * HD : (u + 1) * HD, :]
            line = jnp.sum(jnp.where(diagonal, block, 0.0), axis=0, keepdims=True)
            l_mine[t, 2 * u] = line
            l_mine[t, 2 * u + 1] = pltpu.roll(line, HB, 1)
        parts[t, mine] = o_mine[t, mine]
        lses[t, mine] = l_mine[t, mine]
        for i, (pz, pc) in enumerate(peers):
            to = pz * 2 + pc
            remote(
                l_mine.at[t, to], lses.at[t, mine], l_send.at[i], l_recv.at[t, mine], ids[i]
            ).start()
            remote(
                o_mine.at[t, to], parts.at[t, mine], o_send.at[i], o_recv.at[t, mine], ids[i]
            ).start()

    def term(t):
        for i, (pz, pc) in enumerate(peers):
            src = pz * 2 + pc
            remote(
                l_mine.at[t, src], lses.at[t, src], l_send.at[i], l_recv.at[t, src], ids[i]
            ).wait_recv()
            remote(
                o_mine.at[t, src], parts.at[t, src], o_send.at[i], o_recv.at[t, src], ids[i]
            ).wait_recv()
        shares = []
        for h in range(2):
            lse = [lses[t, z * 2 + h] for z in range(4)]
            best = jnp.maximum(jnp.maximum(lse[0], lse[1]), jnp.maximum(lse[2], lse[3]))
            share = [jnp.exp2(line - best) for line in lse]
            total = share[0] + share[1] + share[2] + share[3]
            shares += [line / total for line in share]
        turned = jnp.concatenate(shares * (HD // SRC), axis=0).T
        for h in range(2):
            mixed = jnp.zeros((HB, HD), F32)
            for z in range(4):
                share = turned[0:HB, h * 4 + z : h * 4 + z + 1]
                mixed += share * parts[t, z * 2 + h].astype(F32)
            ctx[:, h * HD : (h + 1) * HD] = mixed.astype(BF16)
        at = pl.ds(pl.multiple_of(t * HB, HB), HB)
        terms[at, :] = jnp.dot(ctx[...], w_ref[...], preferred_element_type=F32).astype(BF16)

    def cols(v):
        return pl.ds(v * WIDTH, WIDTH)

    def cut(slot, lo, v):
        return terms.at[pl.ds(slot * HB + lo, HALF), cols(v)]

    def far(p, slot, side, v):
        return remote(
            cut(slot, side * HALF, v), halves.at[p, side, :, cols(v)],
            h_send.at[p, side, v], h_recv.at[p, side, v], left if side else right,
        )

    def near(p, slot, side, upper, v):
        return remote(
            cut(slot, upper * HALF, v), fulls.at[p, side, pl.ds(upper * HALF, HALF), cols(v)],
            f_send.at[p, side, upper, v], f_recv.at[p, side, upper, v], left if side else right,
        )

    def across(upper, v):
        return remote(
            cut(MIR, upper * HALF, v), mirrored.at[pl.ds(upper * HALF, HALF), cols(v)],
            z_send.at[upper, v], z_recv.at[upper, v], mirror,
        )

    fars, nears = (O0, O1), ((R0, L0), (R1, L1))

    def add(lo, v, *more):
        rows, columns = slice(lo, lo + HALF), slice(v * WIDTH, (v + 1) * WIDTH)
        total = terms[rows, columns].astype(F32)
        for ref in more:
            total = total + ref[:, columns].astype(F32)
        return total

    def store(lo, v, total):
        terms[lo : lo + HALF, v * WIDTH : (v + 1) * WIDTH] = total.astype(BF16)

    def send_far(p):
        for v in range(CUTS):
            for side in range(2):
                far(p, fars[p], side, v).start()

    def send_near(p, side):
        slot = nears[p][side]
        lo = slot * HB + side * HALF
        for v in range(CUTS):
            near(p, slot, side, 1 - side, v).start()
            far(p, fars[p], side, v).wait_recv()
            store(lo, v, add(lo, v, halves.at[p, side]))
            near(p, slot, side, side, v).start()

    def send_over(v):
        for upper in range(2):
            for side in range(2):
                near(1, nears[1][side], side, upper, v).wait_recv()
            lo = MIR * HB + upper * HALF
            rows = pl.ds(upper * HALF, HALF)
            store(lo, v, add(lo, v, fulls.at[1, 0, rows], fulls.at[1, 1, rows]))
            across(upper, v).start()

    def step_far():
        term(O1)
        send_far(1)

    def step_near():
        term(L1)
        send_near(1, 1)
        term(R1)
        send_near(1, 0)

    def step_mirror():
        term(MIR)
        send_over(0)

    clear(top_a)
    score_chunk(0, scores_a, top_a)

    @pl.loop(0, SLOTS // 2 - 1)
    def _(i):
        attend_chunk(2 * i, scores_a, top_a, scores_b, top_b)
        pl.when(i == 1)(step_far)
        pl.when(i == 2)(step_mirror)
        attend_chunk(2 * i + 1, scores_b, top_b, scores_a, top_a)
        pl.when(i == 1)(step_near)
        pl.when(i == 2)(lambda: send_over(1))

    attend_chunk(SLOTS - 2, scores_a, top_a, scores_b, top_b)
    term(O0)
    send_far(0)
    send_over(2)
    send_over(3)
    attend_chunk(SLOTS - 1, scores_b, top_b)
    term(L0)
    send_near(0, 1)
    term(R0)
    send_near(0, 0)
    term(OWN)
    for v in range(CUTS):
        for upper in range(2):
            for side in range(2):
                near(0, nears[0][side], side, upper, v).wait_recv()
            across(upper, v).wait_recv()
            rows = pl.ds(upper * HALF, HALF)
            total = add(
                OWN * HB + upper * HALF, v, fulls.at[0, 0, rows], fulls.at[0, 1, rows], mirrored.at[rows]
            )
            out_ref[rows, v * WIDTH : (v + 1) * WIDTH] = total.astype(BF16)
    for v in range(CUTS):
        for p in range(2):
            for side in range(2):
                far(p, fars[p], side, v).wait_send()
                for upper in range(2):
                    near(p, nears[p][side], side, upper, v).wait_send()
        for upper in range(2):
            across(upper, v).wait_send()
    for i, (pz, pc) in enumerate(peers):
        src = pz * 2 + pc
        remote(l_mine.at[:, src], lses.at[:, src], l_send.at[i], l_recv.at[0, src], ids[i]).wait_send()
        remote(o_mine.at[:, src], parts.at[:, src], o_send.at[i], o_recv.at[0, src], ids[i]).wait_send()


def sublayer(block_order, hidden_in, norm_gain, weight, out_weight):
    smem = pl.BlockSpec(memory_space=pltpu.SMEM)
    vmem = pl.BlockSpec(memory_space=pltpu.VMEM)
    hbm = pl.BlockSpec(memory_space=pl.ANY)
    dma = pltpu.SemaphoreType.DMA
    return pl.pallas_call(
        sublayer_kernel,
        out_shape=jax.ShapeDtypeStruct((HB, D), BF16),
        in_specs=[smem] + [hbm] * 8,
        out_specs=vmem,
        scratch_shapes=[
            pltpu.VMEM((HB, D), BF16),
            pltpu.VMEM((1, D), F32),
            pltpu.VMEM((SEQ // HB, HD), F32),
            pltpu.VMEM((SEQ // HB, HD), F32),
            pltpu.VMEM((HB, HD), F32),
            pltpu.VMEM((HB, HD), F32),
            pltpu.VMEM((ROWS, D), BF16),
            pltpu.VMEM((ROWS, HD), F32),
            pltpu.VMEM((ROWS, HD), F32),
            pltpu.VMEM((3, D, 2 * HD), BF16),
            pltpu.VMEM((2, ROWS, HD), BF16),
            pltpu.VMEM((2, ROWS, 2 * HD), BF16),
            pltpu.VMEM((SRC, ROWS, HD), BF16),
            pltpu.VMEM((SRC, ROWS, 2 * HD), BF16),
            pltpu.VMEM((2 * HD, D), BF16),
            pltpu.VMEM((ALL, 2 * HD), BF16),
            pltpu.VMEM((ALL // HD, TQ, HD), F32),
            pltpu.VMEM((ALL // HD, TQ, HD), F32),
            pltpu.VMEM((TQ, HD), F32),
            pltpu.VMEM((TQ, HD), F32),
            pltpu.VMEM((TQ, 2 * HD), F32),
            pltpu.VMEM((SLOTS, TQ, HD), jnp.int32),
            pltpu.VMEM((ALL // HD, 1, HD), jnp.int32),
            pltpu.VMEM((SLOTS, SRC, HB, HD), BF16),
            pltpu.VMEM((SLOTS, SRC, 1, HD), F32),
            pltpu.VMEM((SLOTS, SRC, HB, HD), BF16),
            pltpu.VMEM((SLOTS, SRC, 1, HD), F32),
            pltpu.VMEM((HB, 2 * HD), BF16),
            pltpu.VMEM((2, 2, HALF, D), BF16),
            pltpu.VMEM((2, 2, HB, D), BF16),
            pltpu.VMEM((HB, D), BF16),
            dma((6,)), dma, dma, dma((2, 6, 2)), dma((2, 6, 2)), dma((2, 2)), dma((2, 2)),
            dma((SRC,)), dma((SRC,)), dma((SRC,)), dma((SRC,)),
            dma((SRC,)), dma((SLOTS, SRC)), dma((SRC,)), dma((SLOTS, SRC)),
            dma((2, 2, CUTS)), dma((2, 2, CUTS)), dma((2, 2, 2, CUTS)), dma((2, 2, 2, CUTS)),
            dma((2, CUTS)), dma((2, CUTS)),
        ],
        compiler_params=pltpu.CompilerParams(
            collective_id=0, has_side_effects=True, vmem_limit_bytes=60 << 20
        ),
        name="sublayer",
    )(block_order, hidden_in, norm_gain, weight, out_weight, *tables())


def local(hidden_in, norm_gain, qkv_weight, out_weight, block_order):
    weight = jnp.transpose(qkv_weight, (1, 0, 2))
    return sublayer(block_order, hidden_in, norm_gain[None, :], weight, out_weight)


def solution(mesh):
    in_specs = (P(("seq", "tp"), None), P(), P(None, None, "tp"), P("tp", None), P())
    out_specs = P(("seq", "tp"), None)
    return jax.shard_map(local, mesh=mesh, in_specs=in_specs, out_specs=out_specs, check_vma=False)
```
